256 devices in a mesh: context: 32 (over y, x, core), tensor: 8 (over z).
Axes of the slice: x: 4, y: 4, z: 8, core: 2. Of those that a mesh axis runs over, the one named last changes fastest.
Arguments:
- queries: bfloat16 [8192, 8192], P('context', 'tensor'), may hold values from -40 to 40
- keys: bfloat16 [8192, 1024], P('context', 'tensor'), may hold values from -6 to 6
- values: bfloat16 [8192, 1024], P('context', 'tensor'), may hold values from -6 to 6
- output_gradient: bfloat16 [8192, 8192], P('context', 'tensor'), may hold values from -6 to 6
- q_gain: float32 [128], replicated, may hold values from 0.5 to 5.5
- k_gain: float32 [128], replicated, may hold values from 0.5 to 5.5
- doc_ids: int32 [8192], P('context'), may hold values from 0 to 63, as said below
Outputs:
- attended: bfloat16 [8192, 8192], P('context', 'tensor')
- grad_queries: bfloat16 [8192, 8192], P('context', 'tensor')
- grad_keys: bfloat16 [8192, 1024], P('context', 'tensor')
- value_gradients: bfloat16 [8192, 1024], P('context', 'tensor')
- grad_q_gain: float32 [128], replicated
- grad_k_gain: float32 [128], replicated
The draws below stay inside these ranges and needn't reach their ends.
Inputs may be any that keep to these rules, and one draw needn't show every extreme that they name: `doc_ids`: Non-decreasing along the pack; every one of the 64 documents holds 1 to 1024 consecutive tokens; document 0 holds at most 128 tokens, document 64 - 2 exactly 1024 and document 64 - 1 exactly 128.
All inputs are finite; a program needn't handle non-finite values.
Results may differ from the reference program's by a relative error of at most 0.024.
The reference program's roundings to bfloat16 on the way (of `weights` and `d_scores`) count: a program that leaves them out, or rounds other values in their place, can miss the bound.
Values may be sent and summed in bfloat16 or wider, within the bound.
No kernel may reach another device: no remote copies, remote signals or barrier semaphores. Data moves between devices by JAX's collectives and lax.ppermute only.
A program may use at most 64 MiB of HBM per device.

```python
import jax
import jax.numpy as jnp
from jax import lax

QUERY_HEADS = 64
KEY_VALUE_HEADS = 8
HEAD_WIDTH = 128
TOK_DEV = 256
REACH = 4
MAXDOC = 1024
PACK_TOKENS = 8192
DOCS = 64


def shared_normals(key):
    return jax.random.truncated_normal(jax.random.fold_in(key, 101), -6.0, 6.0, (PACK_TOKENS, KEY_VALUE_HEADS * HEAD_WIDTH), jnp.float32)


def draw_keys(key, part):
    rotary_base = shared_normals(key)
    return rotary_base.astype(jnp.bfloat16)


def draw_queries(key, part):
    key = jax.random.fold_in(key, 7)
    fresh = jax.random.truncated_normal(key, -6.0, 6.0, (PACK_TOKENS, QUERY_HEADS * HEAD_WIDTH), jnp.float32)
    return fresh.astype(jnp.bfloat16)


def draw_q_gain(key, part):
    key = jax.random.fold_in(key, 5)
    spread = jax.random.uniform(key, (HEAD_WIDTH,), jnp.float32)
    return 0.5 * jnp.exp(1.4 * spread)


def draw_k_gain(key, part):
    key = jax.random.fold_in(key, 9)
    spread = jax.random.uniform(key, (HEAD_WIDTH,), jnp.float32)
    return 0.5 * jnp.exp(1.4 * spread)


def draw_doc_ids(key, part):
    key = jax.random.fold_in(key, 13)
    first_key, jitter_key, slot_key, length_key = jax.random.split(key, 4)
    first_length = jax.random.randint(first_key, (), 1, TOK_DEV // 2 + 1, jnp.int32)
    tail_length = TOK_DEV // 2
    long_end = PACK_TOKENS - tail_length
    long_start = long_end - MAXDOC
    remaining = long_start - first_length
    middle_docs = DOCS - 3
    long_count = max(1, DOCS // 16)
    least_remaining = PACK_TOKENS - tail_length - MAXDOC - TOK_DEV // 2
    long_most = min(MAXDOC, (least_remaining - (middle_docs - long_count)) // long_count)
    long_least = max(1, 3 * long_most // 4)
    long_lengths = jax.random.randint(length_key, (long_count,), long_least, long_most + 1, jnp.int32)
    short_count = middle_docs - long_count
    short_total = remaining - jnp.sum(long_lengths).astype(jnp.int32)
    spacing = short_total // short_count
    reach_jitter = spacing // 3
    steps_index = jnp.arange(1, short_count, dtype=jnp.int32)
    jitter = jax.random.randint(jitter_key, (short_count - 1,), -reach_jitter, reach_jitter + 1, jnp.int32)
    cuts = steps_index * short_total // short_count + jitter
    short_bounds = jnp.concatenate([jnp.zeros((1,), jnp.int32), cuts.astype(jnp.int32), jnp.stack([short_total]).astype(jnp.int32)])
    short_lengths = short_bounds[1:] - short_bounds[:-1]
    stride = middle_docs // long_count
    slot_offsets = jax.random.randint(slot_key, (long_count,), 0, stride, jnp.int32)
    slots = jnp.arange(long_count, dtype=jnp.int32) * stride + slot_offsets
    middle_index = jnp.arange(middle_docs, dtype=jnp.int32)
    is_long = jnp.any(middle_index[:, None] == slots[None, :], axis=1)
    long_order = jnp.clip(jnp.cumsum(is_long.astype(jnp.int32)) - 1, 0, long_count - 1).astype(jnp.int32)
    short_order = jnp.clip(jnp.cumsum((~is_long).astype(jnp.int32)) - 1, 0, short_count - 1).astype(jnp.int32)
    lengths = jnp.where(is_long, long_lengths[long_order], short_lengths[short_order]).astype(jnp.int32)
    ends = first_length + jnp.cumsum(lengths).astype(jnp.int32)
    bounds = jnp.concatenate([jnp.stack([first_length]).astype(jnp.int32), ends, jnp.stack([jnp.int32(long_end)]).astype(jnp.int32)])
    token_index = jnp.arange(PACK_TOKENS, dtype=jnp.int32)
    return jnp.sum((token_index[:, None] >= bounds[None, :]).astype(jnp.int32), axis=1).astype(jnp.int32)


def levels(key, shape, cuts, least, high):
    factor_of = 1.0
    for axis_at, parts in cuts:
        draws = jax.random.uniform(jax.random.fold_in(jax.random.fold_in(key, 6), axis_at), (parts,), jnp.float32, least / len(cuts), high / len(cuts))
        factor_of = factor_of * jnp.repeat(jnp.exp(draws), shape[axis_at] // parts).reshape((-1,) + (1,) * (len(shape) - 1 - axis_at))
    return factor_of


def bell_draw(rng, extent, scale, reach, shards=(), kind=jnp.bfloat16):
    loudness = levels(rng, extent, shards, -0.22, 0.18) if shards else 1.0
    entries = jax.random.normal(rng, extent, jnp.float32) * scale * loudness
    return jnp.minimum(jnp.maximum(entries, -reach), reach).astype(kind)


def setup_inputs(seed: int = 0) -> dict:
    arg_keys = jax.random.split(jax.random.key(seed), 8)
    return {
        "queries": draw_queries(jax.random.fold_in(arg_keys[7], 71), 0),
        "keys": draw_keys(jax.random.fold_in(arg_keys[7], 71), 0),
        "values": bell_draw(arg_keys[2], (PACK_TOKENS, KEY_VALUE_HEADS * HEAD_WIDTH), 1.0, 6.0, ((0, 32), (1, 8))),
        "output_gradient": bell_draw(arg_keys[3], (PACK_TOKENS, QUERY_HEADS * HEAD_WIDTH), 1.0, 6.0, ((0, 32), (1, 8))),
        "q_gain": draw_q_gain(jax.random.fold_in(arg_keys[7], 71), 0),
        "k_gain": draw_k_gain(jax.random.fold_in(arg_keys[7], 71), 0),
        "doc_ids": draw_doc_ids(jax.random.fold_in(arg_keys[7], 71), 0),
    }


THETA = 500000.0
EPSILON = 1e-06

def rotate(field, factor, position):
    head_size = field.shape[-1]
    halfway = head_size // 2
    normalized = field * lax.rsqrt(lax.optimization_barrier(jnp.mean(field * field, axis=-1, keepdims=True)) + EPSILON) * factor
    frequency = THETA ** (-(jnp.arange(halfway, dtype=jnp.float32) * 2.0 / head_size))
    angles = position.astype(jnp.float32)[:, None] * frequency[None, :]
    cosine = jnp.cos(angles)[:, None, :]
    sine_part = jnp.sin(angles)[:, None, :]
    leading = normalized[..., :halfway]
    second = normalized[..., halfway:]
    return jnp.concatenate([leading * cosine - second * sine_part, second * cosine + leading * sine_part], axis=-1)

def reference(queries, keys, values, output_gradient, q_gain, k_gain, doc_ids):
    query_group_count = QUERY_HEADS // KEY_VALUE_HEADS
    window = (REACH + 1) * TOK_DEV
    padding_margin = REACH * TOK_DEV
    first_index = jnp.searchsorted(doc_ids, doc_ids, side='left').astype(jnp.int32)
    position = jnp.arange(PACK_TOKENS, dtype=jnp.int32) - first_index
    q_raw = queries.reshape(PACK_TOKENS, QUERY_HEADS, HEAD_WIDTH).astype(jnp.float32)
    unnormed_keys = keys.reshape(PACK_TOKENS, KEY_VALUE_HEADS, HEAD_WIDTH).astype(jnp.float32)
    normed_query = lax.optimization_barrier(rotate(q_raw, q_gain, position).astype(jnp.bfloat16))
    normed_query = normed_query.reshape(PACK_TOKENS, KEY_VALUE_HEADS, query_group_count, HEAD_WIDTH)
    normed_key = lax.optimization_barrier(rotate(unnormed_keys, k_gain, position).astype(jnp.bfloat16))
    padded_keys = jnp.concatenate([jnp.zeros((padding_margin, KEY_VALUE_HEADS, HEAD_WIDTH), jnp.bfloat16), normed_key])
    padded_values = jnp.concatenate([jnp.zeros((padding_margin, KEY_VALUE_HEADS, HEAD_WIDTH), jnp.bfloat16), values.reshape(PACK_TOKENS, KEY_VALUE_HEADS, HEAD_WIDTH)])
    id_pad = jnp.concatenate([jnp.full((padding_margin,), -1, jnp.int32), doc_ids])
    gradient_total = output_gradient.reshape(PACK_TOKENS, KEY_VALUE_HEADS, query_group_count, HEAD_WIDTH)
    scaling = HEAD_WIDTH ** (-0.5)
    causal = jnp.arange(window)[None, :] <= padding_margin + jnp.arange(TOK_DEV)[:, None]

    def block(carry, index):
        key_acc, value_running_sum = carry
        start = (index * TOK_DEV).astype(jnp.int32)
        q_blk = lax.dynamic_slice_in_dim(normed_query, start, TOK_DEV, 0).astype(jnp.float32)
        d_blk = lax.dynamic_slice_in_dim(gradient_total, start, TOK_DEV, 0).astype(jnp.float32)
        k_win = lax.dynamic_slice_in_dim(padded_keys, start, window, 0).astype(jnp.float32)
        v_win = lax.dynamic_slice_in_dim(padded_values, start, window, 0).astype(jnp.float32)
        q_ids = lax.dynamic_slice_in_dim(doc_ids, start, TOK_DEV, 0)
        w_ids = lax.dynamic_slice_in_dim(id_pad, start, window, 0)
        allowed = (w_ids[None, :] == q_ids[:, None]) & causal
        scores = jnp.einsum('tkgd,wkd->kgtw', q_blk, k_win) * scaling
        scores = jnp.where(allowed[None, None], scores, -1e+30)
        highest = lax.optimization_barrier(jnp.max(scores, axis=-1, keepdims=True))
        exponent = jnp.exp(scores - highest)
        weights = (exponent / lax.optimization_barrier(jnp.sum(exponent, axis=-1, keepdims=True))).astype(jnp.bfloat16)
        weights_wide = lax.optimization_barrier(weights).astype(jnp.float32)
        attended = jnp.einsum('kgtw,wkd->tkgd', weights_wide, v_win).astype(jnp.bfloat16)
        d_weights = jnp.einsum('tkgd,wkd->kgtw', d_blk, v_win)
        center = lax.optimization_barrier(jnp.sum(weights_wide * d_weights, axis=-1, keepdims=True))
        d_scores = (weights_wide * (d_weights - center)).astype(jnp.bfloat16)
        d_scores = lax.optimization_barrier(d_scores).astype(jnp.float32)
        d_query = jnp.einsum('kgtw,wkd->tkgd', d_scores, k_win) * scaling
        d_key = jnp.einsum('kgtw,tkgd->wkd', d_scores, q_blk) * scaling
        d_value = jnp.einsum('kgtw,tkgd->wkd', weights_wide, d_blk)
        key_part = lax.dynamic_slice_in_dim(key_acc, start, window, 0) + d_key
        value_part = lax.dynamic_slice_in_dim(value_running_sum, start, window, 0) + d_value
        key_acc = lax.dynamic_update_slice_in_dim(key_acc, key_part, start, 0)
        value_running_sum = lax.dynamic_update_slice_in_dim(value_running_sum, value_part, start, 0)
        return ((key_acc, value_running_sum), (attended, d_query))
    blank_block = jnp.zeros((PACK_TOKENS + padding_margin, KEY_VALUE_HEADS, HEAD_WIDTH), jnp.float32)
    blocks = jnp.arange(PACK_TOKENS // TOK_DEV, dtype=jnp.int32)
    (key_acc, value_running_sum), (attended, d_query) = lax.scan(block, (blank_block, blank_block), blocks)
    attended = attended.reshape(PACK_TOKENS, QUERY_HEADS * HEAD_WIDTH)
    d_query = d_query.reshape(PACK_TOKENS, QUERY_HEADS, HEAD_WIDTH)
    _, q_pullback = jax.vjp(lambda field, factor: rotate(field, factor, position), q_raw, q_gain)
    query_gradient, query_gain_gradient = q_pullback(d_query)
    _, k_pullback = jax.vjp(lambda field, factor: rotate(field, factor, position), unnormed_keys, k_gain)
    key_gradient, key_gain_gradient = k_pullback(key_acc[padding_margin:])
    value_gradients = value_running_sum[padding_margin:].reshape(PACK_TOKENS, KEY_VALUE_HEADS * HEAD_WIDTH).astype(jnp.bfloat16)
    return (attended, query_gradient.reshape(PACK_TOKENS, QUERY_HEADS * HEAD_WIDTH).astype(jnp.bfloat16), key_gradient.reshape(PACK_TOKENS, KEY_VALUE_HEADS * HEAD_WIDTH).astype(jnp.bfloat16), value_gradients, query_gain_gradient, key_gain_gradient)
```

```python
import functools

import jax
import jax.numpy as jnp
import numpy as np
from jax import lax
from jax.experimental import pallas as pl
from jax.experimental.pallas import tpu as pltpu
from jax.sharding import PartitionSpec as P

REACH = 4
THETA = 500000.0
EPSILON = 1e-06
TOK = 256
HEAD = 128
HEADS = 8
WINDOW = (REACH + 1) * TOK
SUB = 128
SPAN = 1152
CHUNKS = SPAN // SUB
ID_ROWS = 16
MSG = 2 * TOK + ID_ROWS
SCALING = HEAD ** (-0.5)
EXP2 = float(SCALING * np.log2(np.e))
NT = (((1,), (1,)), ((), ()))

PIO2_A = 1.5703125
PIO2_B = float(np.float32(np.round((np.pi / 2 - PIO2_A) * 2.0**23) / 2.0**23))
PIO2_C = float(np.float32(np.pi / 2 - PIO2_A - PIO2_B))


def passed_along(block, axis, distance):
    devices = range(lax.axis_size(axis))
    route = [(i - distance, i) for i in devices if i - distance in devices]
    return lax.ppermute(block, axis, route)


def dot(a, b):
    return jnp.dot(a, b, preferred_element_type=jnp.float32)


def dot_nt(a, b):
    return lax.dot_general(a, b, NT, preferred_element_type=jnp.float32)


def half_turned(x):
    return pltpu.roll(x, HEAD // 2, 1)


def cos_sin(position, frequency):
    angle = position * frequency
    turns = jnp.floor(angle * np.float32(2.0 / np.pi) + 0.5)
    rest = ((angle - turns * PIO2_A) - turns * PIO2_B) - turns * PIO2_C
    square = rest * rest
    sine = rest + rest * square * (
        np.float32(-1.6666654611e-1)
        + square * (np.float32(8.3321608736e-3) + square * np.float32(-1.9515295891e-4))
    )
    cosine = (1.0 - 0.5 * square) + square * square * (
        np.float32(4.166664568298827e-2)
        + square * (np.float32(-1.388731625493765e-3) + square * np.float32(2.443315711809948e-5))
    )
    lane = lax.broadcasted_iota(jnp.int32, angle.shape, 1)
    quadrant = turns.astype(jnp.int32) + jnp.where(lane < HEAD // 2, 1, 0)
    value = jnp.where((quadrant & 1) == 1, cosine, sine)
    return jnp.where((quadrant & 2) == 2, -value, value)


def kernel(
    b4, b3, b2, b1, b0, q_ref, d_ref, qg_ref, kg_ref, f_ref,
    att_ref, gq_ref, r4, r3, r2, r1, own_ref, gain_ref,
    idc, cosine, sine, khat, vwin, khat_t, v_t, bias, qhat, dcat, dcat_t, s_ref, w_ref, ds_ref,
    dk, dv, qg_acc,
):
    blocks = (b4, b3, b2, b1, b0)
    lane = lax.broadcasted_iota(jnp.int32, (SUB, HEAD), 1)
    row = lax.broadcasted_iota(jnp.int32, (SUB, HEAD), 0)
    lane_f = lane.astype(jnp.float32)
    left = lane < HEAD // 2
    parts = WINDOW // SUB
    q_gain = qg_ref[...]
    k_gain = kg_ref[...]
    frequency = f_ref[...]

    id_rows = []
    for block in blocks:
        both = block[2 * TOK : MSG, :].astype(jnp.float32)
        id_rows += [both[0:1], both[1:2]]
    below = jnp.zeros((SUB, HEAD), jnp.float32)
    for j in range(parts):
        column = jnp.broadcast_to(id_rows[j], (SUB, HEAD)).T
        idc[j * SUB : (j + 1) * SUB, :] = column
        below = below + jnp.where(column < lane_f, 1.0, 0.0)
    first = jnp.sum(below, axis=0, keepdims=True)

    for j in range(parts):
        rows = slice(j * SUB, (j + 1) * SUB)
        here = slice((j % 2) * SUB, (j % 2 + 1) * SUB)
        block = blocks[j // 2]
        start = jnp.sum(jnp.where(idc[rows, :] == lane_f, first, 0.0), axis=1, keepdims=True)
        position = (row + j * SUB).astype(jnp.float32) - start
        both = cos_sin(position, frequency)
        turned = half_turned(both)
        c = jnp.where(left, both, turned)
        s = jnp.where(left, -turned, both)
        cosine[rows, :] = c
        sine[rows, :] = s
        x = block[here, :].astype(jnp.float32)
        normed = x * lax.rsqrt(jnp.mean(x * x, axis=1, keepdims=True) + EPSILON) * k_gain
        hat = normed * c + half_turned(normed) * s
        khat[rows, :] = hat.astype(jnp.bfloat16)
        khat_t[:, rows] = hat.T.astype(jnp.bfloat16)
        values = block[TOK + (j % 2) * SUB : TOK + (j % 2 + 1) * SUB, :]
        vwin[rows, :] = values
        v_t[:, rows] = values.astype(jnp.float32).T.astype(jnp.bfloat16)

    for h in range(HEADS):
        for sub in range(2):
            tokens = slice(sub * SUB, (sub + 1) * SUB)
            at = (h // 2) * 512 + sub * 256 + (h % 2) * SUB
            window_rows = slice(REACH * TOK + sub * SUB, REACH * TOK + (sub + 1) * SUB)
            x = q_ref[tokens, h * HEAD : (h + 1) * HEAD].astype(jnp.float32)
            normed = x * lax.rsqrt(jnp.mean(x * x, axis=1, keepdims=True) + EPSILON) * q_gain
            hat = normed * cosine[window_rows, :] + half_turned(normed) * sine[window_rows, :]
            qhat[at : at + SUB, :] = hat.astype(jnp.bfloat16)
            d = d_ref[tokens, h * HEAD : (h + 1) * HEAD]
            dcat[at : at + SUB, :] = d
            dcat_t[h // 2, :, (at % 512) : (at % 512) + SUB] = d.astype(jnp.float32).T

    for sub in range(2):
        ids_q = id_rows[2 * REACH + sub]
        for c in range(CHUNKS):
            j = sub + c
            kept = idc[j * SUB : (j + 1) * SUB, :] == ids_q
            if c == CHUNKS - 1:
                kept = kept & (row <= lane)
            bias[sub, c * SUB : (c + 1) * SUB, :] = jnp.where(kept, 0.0, -1e30)

    dk[...] = jnp.zeros_like(dk)
    dv[...] = jnp.zeros_like(dv)
    qg_acc[...] = jnp.zeros_like(qg_acc)
    zero = jnp.zeros((SUB, 256), jnp.bfloat16)
    for ref in (w_ref, ds_ref):
        ref[0:SUB, 256:512] = zero
        ref[SPAN:WINDOW, 0:256] = zero

    def pair_step(pair, carry):
        at = pl.multiple_of(pair * 512, 512)
        for sub in range(2):
            base = sub * SUB
            cols = slice(sub * 256, (sub + 1) * 256)
            q_pair = qhat[pl.ds(at + sub * 256, 256), :]
            d_pair = dcat[pl.ds(at + sub * 256, 256), :]
            top = jnp.full((8, 256), -1e30, jnp.float32)
            for c in range(CHUNKS):
                keys = slice(base + c * SUB, base + (c + 1) * SUB)
                block_bias = bias[sub, c * SUB : (c + 1) * SUB, :]
                s = dot_nt(khat[keys, :], q_pair) + jnp.concatenate([block_bias, block_bias], axis=1)
                s_ref[sub, c * SUB : (c + 1) * SUB, :] = s
                top = jnp.maximum(top, jnp.max(s.reshape(SUB // 8, 8, 256), axis=0))
            shift = jnp.max(top, axis=0, keepdims=True) * EXP2
            total = jnp.zeros((8, 256), jnp.float32)
            for c in range(CHUNKS):
                e = jnp.exp2(s_ref[sub, c * SUB : (c + 1) * SUB, :] * EXP2 - shift)
                s_ref[sub, c * SUB : (c + 1) * SUB, :] = e
                total = total + jnp.sum(e.reshape(SUB // 8, 8, 256), axis=0)
            inverse = 1.0 / jnp.sum(total, axis=0, keepdims=True)
            for c in range(CHUNKS):
                keys = slice(base + c * SUB, base + (c + 1) * SUB)
                w = s_ref[sub, c * SUB : (c + 1) * SUB, :] * inverse
                w_ref[keys, cols] = w.astype(jnp.bfloat16)
            span = slice(base, base + SPAN)
            att_t = dot(v_t[:, span], w_ref[span, cols])
            center = jnp.sum(att_t * dcat_t[pair, :, cols], axis=0, keepdims=True)
            for c in range(CHUNKS):
                keys = slice(base + c * SUB, base + (c + 1) * SUB)
                dw = dot_nt(vwin[keys, :], d_pair)
                ds = w_ref[keys, cols].astype(jnp.float32) * (dw - center)
                ds_ref[keys, cols] = ds.astype(jnp.bfloat16)
            dq_t = dot(khat_t[:, span], ds_ref[span, cols]) * SCALING
            tokens = slice(sub * SUB, (sub + 1) * SUB)
            window_rows = slice(REACH * TOK + sub * SUB, REACH * TOK + (sub + 1) * SUB)
            c_q = cosine[window_rows, :]
            s_q = sine[window_rows, :]
            for g in range(2):
                columns = pl.ds(pl.multiple_of(pair * 256 + g * HEAD, HEAD), HEAD)
                att = att_t[:, g * SUB : (g + 1) * SUB].T
                att_ref[tokens, columns] = att.astype(jnp.bfloat16)
                dq = dq_t[:, g * SUB : (g + 1) * SUB].T
                x = q_ref[tokens, columns].astype(jnp.float32)
                r = lax.rsqrt(jnp.mean(x * x, axis=1, keepdims=True) + EPSILON)
                xh = x * r
                dn = dq * c_q - half_turned(dq) * s_q
                qg_acc[...] += jnp.sum((dn * xh).reshape(SUB // 8, 8, HEAD), axis=0)
                dxh = dn * q_gain
                gq = r * (dxh - xh * jnp.mean(dxh * xh, axis=1, keepdims=True))
                gq_ref[tokens, columns] = gq.astype(jnp.bfloat16)
        q_four = qhat[pl.ds(at, 512), :]
        d_four = dcat[pl.ds(at, 512), :]
        for j in range(parts):
            rows = slice(j * SUB, (j + 1) * SUB)
            dk[rows, :] += dot(ds_ref[rows, :], q_four)
            dv[rows, :] += dot(w_ref[rows, :], d_four)
        return carry

    lax.fori_loop(0, HEADS // 2, pair_step, 0)

    kg = jnp.zeros((8, HEAD), jnp.float32)
    outs = (r4, r3, r2, r1, own_ref)
    for j in range(parts):
        rows = slice(j * SUB, (j + 1) * SUB)
        here = slice((j % 2) * SUB, (j % 2 + 1) * SUB)
        x = blocks[j // 2][here, :].astype(jnp.float32)
        r = lax.rsqrt(jnp.mean(x * x, axis=1, keepdims=True) + EPSILON)
        xh = x * r
        d = dk[rows, :] * SCALING
        dn = d * cosine[rows, :] - half_turned(d) * sine[rows, :]
        kg = kg + jnp.sum((dn * xh).reshape(SUB // 8, 8, HEAD), axis=0)
        dxh = dn * k_gain
        gk = r * (dxh - xh * jnp.mean(dxh * xh, axis=1, keepdims=True))
        out = outs[j // 2]
        out[here, :] = gk.astype(out.dtype)
        out[TOK + (j % 2) * SUB : TOK + (j % 2 + 1) * SUB, :] = dv[rows, :].astype(out.dtype)
    gain_ref[0:1, :] = jnp.sum(qg_acc[...], axis=0, keepdims=True)
    gain_ref[1:2, :] = jnp.sum(kg, axis=0, keepdims=True)


RETURN = jnp.float32


def attention(blocks, queries, output_gradient, q_gain, k_gain, frequency):
    vmem = pl.BlockSpec(memory_space=pltpu.VMEM)
    f32, bf16 = jnp.float32, jnp.bfloat16
    shape = jax.ShapeDtypeStruct
    return pl.pallas_call(
        kernel,
        out_shape=[
            shape((TOK, HEADS * HEAD), bf16),
            shape((TOK, HEADS * HEAD), bf16),
            *[shape((2 * TOK, HEAD), RETURN) for _ in range(REACH)],
            shape((2 * TOK, HEAD), f32),
            shape((2, HEAD), f32),
        ],
        in_specs=[vmem] * 10,
        out_specs=[vmem] * 8,
        scratch_shapes=[
            pltpu.VMEM((WINDOW, HEAD), f32),
            pltpu.VMEM((WINDOW, HEAD), f32),
            pltpu.VMEM((WINDOW, HEAD), f32),
            pltpu.VMEM((WINDOW, HEAD), bf16),
            pltpu.VMEM((WINDOW, HEAD), bf16),
            pltpu.VMEM((HEAD, WINDOW), bf16),
            pltpu.VMEM((HEAD, WINDOW), bf16),
            pltpu.VMEM((2, SPAN, SUB), f32),
            pltpu.VMEM((HEADS * TOK, HEAD), bf16),
            pltpu.VMEM((HEADS * TOK, HEAD), bf16),
            pltpu.VMEM((HEADS // 2, HEAD, 512), f32),
            pltpu.VMEM((2, SPAN, 256), f32),
            pltpu.VMEM((WINDOW, 512), bf16),
            pltpu.VMEM((WINDOW, 512), bf16),
            pltpu.VMEM((WINDOW, HEAD), f32),
            pltpu.VMEM((WINDOW, HEAD), f32),
            pltpu.VMEM((8, HEAD), f32),
        ],
        compiler_params=pltpu.CompilerParams(vmem_limit_bytes=40 * 1024 * 1024),
    )(*blocks, queries, output_gradient, q_gain, k_gain, frequency)


def body(queries, keys, values, output_gradient, q_gain, k_gain, doc_ids):
    ids = (doc_ids + 1).astype(jnp.bfloat16).reshape(2, HEAD)
    ids = jnp.concatenate([ids, jnp.zeros((ID_ROWS - 2, HEAD), jnp.bfloat16)])
    message = jnp.concatenate([keys, values, ids])
    blocks = [passed_along(message, "context", distance) for distance in range(REACH, 0, -1)]
    blocks.append(message)
    half = jnp.arange(HEAD // 2, dtype=jnp.float32)
    frequency = THETA ** (-(half * 2.0 / HEAD))
    frequency = jnp.concatenate([frequency, frequency]).reshape(1, HEAD)
    attended, query_gradient, *returns, own, gains = attention(
        blocks,
        queries,
        output_gradient,
        q_gain.reshape(1, HEAD),
        k_gain.reshape(1, HEAD),
        frequency,
    )
    everyone = lax.all_gather(gains, ("context", "tensor"))
    total = own
    for distance, block in zip(range(REACH, 0, -1), returns):
        total = total + passed_along(block, "context", -distance)
    total = total.astype(jnp.bfloat16)
    gain_total = jnp.sum(everyone, axis=0)
    return (
        attended,
        query_gradient,
        total[:TOK],
        total[TOK:],
        gain_total[0],
        gain_total[1],
    )


def solution(mesh):
    placed = (
        P("context", "tensor"),
        P("context", "tensor"),
        P("context", "tensor"),
        P("context", "tensor"),
        P(),
        P(),
        P("context"),
    )
    return jax.shard_map(
        body,
        mesh=mesh,
        in_specs=placed,
        out_specs=(
            P("context", "tensor"),
            P("context", "tensor"),
            P("context", "tensor"),
            P("context", "tensor"),
            P(),
            P(),
        ),
        check_vma=False,
    )
```

```python
import jax
import jax.numpy as jnp
import numpy as np
from jax import lax
from jax.experimental import pallas as pl
from jax.experimental.pallas import tpu as pltpu
from jax.sharding import PartitionSpec as P

REACH = 4
THETA = 500000.0
EPSILON = 1e-06
TOK = 256
HEAD = 128
HEADS = 8
WINDOW = (REACH + 1) * TOK
SUB = 128
SPAN = 1152
CHUNKS = SPAN // SUB
ID_ROWS = 16
MSG = 2 * TOK + ID_ROWS
SCALING = HEAD ** (-0.5)
EXP2 = float(SCALING * np.log2(np.e))

PIO2_A = 1.5703125
PIO2_B = float(np.float32(np.round((np.pi / 2 - PIO2_A) * 2.0**23) / 2.0**23))
PIO2_C = float(np.float32(np.pi / 2 - PIO2_A - PIO2_B))


def passed_along(block, axis, distance):
    devices = range(lax.axis_size(axis))
    route = [(i - distance, i) for i in devices if i - distance in devices]
    return lax.ppermute(block, axis, route)


def dot(a, b):
    return jnp.dot(a, b, preferred_element_type=jnp.float32)


def half_turned(x):
    return pltpu.roll(x, HEAD // 2, 1)


def cos_sin(position, frequency):
    angle = position * frequency
    turns = jnp.floor(angle * np.float32(2.0 / np.pi) + 0.5)
    rest = ((angle - turns * PIO2_A) - turns * PIO2_B) - turns * PIO2_C
    square = rest * rest
    sine = rest + rest * square * (
        np.float32(-1.6666654611e-1)
        + square * (np.float32(8.3321608736e-3) + square * np.float32(-1.9515295891e-4))
    )
    cosine = (1.0 - 0.5 * square) + square * square * (
        np.float32(4.166664568298827e-2)
        + square * (np.float32(-1.388731625493765e-3) + square * np.float32(2.443315711809948e-5))
    )
    lane = lax.broadcasted_iota(jnp.int32, angle.shape, 1)
    quadrant = turns.astype(jnp.int32) + jnp.where(lane < HEAD // 2, 1, 0)
    value = jnp.where((quadrant & 1) == 1, cosine, sine)
    return jnp.where((quadrant & 2) == 2, -value, value)


def kernel(
    b4, b3, b2, b1, b0, q_hbm, d_hbm, qg_ref, kg_ref, f_ref,
    att_hbm, gq_hbm, r4, r3, r2, r1, own_ref, gain_ref,
    q_ref, d_ref, att_ref, gq_ref, cosine, sine, kext, vwin, khat_t, v_t, qhat, qext_t, dcat, dcat_t,
    s_ref, w_ref, ds_ref, dk, dv, qg_acc, in_sem, att_sem, gq_sem,
):
    q_copy = pltpu.make_async_copy(q_hbm, q_ref, in_sem.at[0])
    d_copy = pltpu.make_async_copy(d_hbm, d_ref, in_sem.at[1])
    q_copy.start()
    d_copy.start()
    blocks = (b4, b3, b2, b1, b0)
    lane = lax.broadcasted_iota(jnp.int32, (SUB, HEAD), 1)
    row = lax.broadcasted_iota(jnp.int32, (SUB, HEAD), 0)
    lane_f = lane.astype(jnp.float32)
    row_f = row.astype(jnp.float32)
    left = lane < HEAD // 2
    parts = WINDOW // SUB
    q_gain = qg_ref[...]
    k_gain = kg_ref[...]
    frequency = f_ref[...]

    id_rows = []
    for block in blocks:
        both = block[2 * TOK : MSG, :].astype(jnp.float32)
        id_rows += [both[0:1], both[1:2]]
    below = jnp.zeros((SUB, HEAD), jnp.float32)
    for j in range(parts):
        column = jnp.broadcast_to(id_rows[j], (SUB, HEAD)).T
        kext[j * SUB : (j + 1) * SUB, HEAD:] = jnp.where(column == lane_f, 1.0, 0.0).astype(jnp.bfloat16)
        below = below + jnp.where(column < lane_f, 1.0, 0.0)
    first = jnp.sum(below, axis=0, keepdims=True)

    for j in range(parts):
        rows = slice(j * SUB, (j + 1) * SUB)
        here = slice((j % 2) * SUB, (j % 2 + 1) * SUB)
        block = blocks[j // 2]
        member = kext[rows, HEAD:].astype(jnp.float32)
        start = jnp.sum(member * first, axis=1, keepdims=True)
        position = (row + j * SUB).astype(jnp.float32) - start
        both = cos_sin(position, frequency)
        turned = half_turned(both)
        c = jnp.where(left, both, turned)
        s = jnp.where(left, -turned, both)
        cosine[rows, :] = c
        sine[rows, :] = s
        x = block[here, :].astype(jnp.float32)
        normed = x * lax.rsqrt(jnp.mean(x * x, axis=1, keepdims=True) + EPSILON) * k_gain
        hat = normed * c + half_turned(normed) * s
        kext[rows, 0:HEAD] = hat.astype(jnp.bfloat16)
        khat_t[:, rows] = hat.T.astype(jnp.bfloat16)
        values = block[TOK + (j % 2) * SUB : TOK + (j % 2 + 1) * SUB, :]
        vwin[rows, :] = values
        v_t[:, rows] = values.astype(jnp.float32).T.astype(jnp.bfloat16)

    q_copy.wait()
    d_copy.wait()
    for sub in range(2):
        tokens = slice(sub * SUB, (sub + 1) * SUB)
        window_rows = slice(REACH * TOK + sub * SUB, REACH * TOK + (sub + 1) * SUB)
        c_q = cosine[window_rows, :]
        s_q = sine[window_rows, :]
        other = jnp.where(row_f == id_rows[2 * REACH + sub], 0.0, -1e30).astype(jnp.bfloat16)
        for h in range(HEADS):
            at = (h // 2) * 512 + sub * 256 + (h % 2) * SUB
            lanes = slice(at % 512, at % 512 + SUB)
            x = q_ref[tokens, h * HEAD : (h + 1) * HEAD].astype(jnp.float32)
            normed = x * lax.rsqrt(jnp.mean(x * x, axis=1, keepdims=True) + EPSILON) * q_gain
            hat = normed * c_q + half_turned(normed) * s_q
            qhat[at : at + SUB, :] = hat.astype(jnp.bfloat16)
            qext_t[h // 2, 0:HEAD, lanes] = hat.T.astype(jnp.bfloat16)
            qext_t[h // 2, HEAD:, lanes] = other
            d = d_ref[tokens, h * HEAD : (h + 1) * HEAD]
            dcat[at : at + SUB, :] = d
            dcat_t[h // 2, :, lanes] = d.astype(jnp.float32).T.astype(jnp.bfloat16)

    dk[...] = jnp.zeros_like(dk)
    dv[...] = jnp.zeros_like(dv)
    qg_acc[...] = jnp.zeros_like(qg_acc)
    zero = jnp.zeros((SUB, 256), jnp.bfloat16)
    for ref in (w_ref, ds_ref):
        ref[0:SUB, 256:512] = zero
        ref[SPAN:WINDOW, 0:256] = zero
    later = jnp.where(row <= lane, 0.0, -1e30)
    later = jnp.concatenate([later, later], axis=1)
    last = SPAN - SUB

    def copies(pair):
        columns = pl.ds(pl.multiple_of(pair * 256, 256), 256)
        return (
            pltpu.make_async_copy(att_ref.at[:, columns], att_hbm.at[:, columns], att_sem.at[pair]),
            pltpu.make_async_copy(gq_ref.at[:, columns], gq_hbm.at[:, columns], gq_sem.at[pair]),
        )

    def pair_step(pair, carry):
        at = pl.multiple_of(pair * 512, 512)
        spans = (slice(0, SPAN), slice(SUB, WINDOW))
        columns_of = (slice(0, 256), slice(256, 512))
        shifts = []
        for sub in range(2):
            cols = columns_of[sub]
            s = dot(kext[spans[sub], :], qext_t[pair, :, cols])
            tail = s[last:] + later
            s_ref[sub, 0:last, :] = s[:last]
            s_ref[sub, last:, :] = tail
            top = jnp.maximum(
                jnp.max(s[:last].reshape(last // 8, 8, 256), axis=0),
                jnp.max(tail.reshape(SUB // 8, 8, 256), axis=0),
            )
            shifts.append(jnp.max(top, axis=0, keepdims=True) * EXP2)
        att_ts = []
        for sub in range(2):
            cols = columns_of[sub]
            base = sub * SUB
            total = jnp.zeros((8, 256), jnp.float32)
            for c in range(CHUNKS):
                e = jnp.exp2(s_ref[sub, c * SUB : (c + 1) * SUB, :] * EXP2 - shifts[sub])
                s_ref[sub, c * SUB : (c + 1) * SUB, :] = e
                total = total + jnp.sum(e.reshape(SUB // 8, 8, 256), axis=0)
            inverse = 1.0 / jnp.sum(total, axis=0, keepdims=True)
            for c in range(CHUNKS):
                keys = slice(base + c * SUB, base + (c + 1) * SUB)
                w = s_ref[sub, c * SUB : (c + 1) * SUB, :] * inverse
                w_ref[keys, cols] = w.astype(jnp.bfloat16)
            att_ts.append(dot(v_t[:, spans[sub]], w_ref[spans[sub], cols]))
        for sub in range(2):
            cols = columns_of[sub]
            span = spans[sub]
            att_t = att_ts[sub]
            d_t = dcat_t[pair, :, cols]
            center = jnp.sum(att_t * d_t.astype(jnp.float32), axis=0, keepdims=True)
            dw = dot(vwin[span, :], d_t)
            ds = w_ref[span, cols].astype(jnp.float32) * (dw - center)
            ds_ref[span, cols] = ds.astype(jnp.bfloat16)
            dq_t = dot(khat_t[:, span], ds_ref[span, cols]) * SCALING
            tokens = slice(sub * SUB, (sub + 1) * SUB)
            window_rows = slice(REACH * TOK + sub * SUB, REACH * TOK + (sub + 1) * SUB)
            c_q = cosine[window_rows, :]
            s_q = sine[window_rows, :]
            for g in range(2):
                columns = pl.ds(pl.multiple_of(pair * 256 + g * HEAD, HEAD), HEAD)
                att = att_t[:, g * SUB : (g + 1) * SUB].T
                att_ref[tokens, columns] = att.astype(jnp.bfloat16)
                dq = dq_t[:, g * SUB : (g + 1) * SUB].T
                x = q_ref[tokens, columns].astype(jnp.float32)
                r = lax.rsqrt(jnp.mean(x * x, axis=1, keepdims=True) + EPSILON)
                xh = x * r
                dn = dq * c_q - half_turned(dq) * s_q
                qg_acc[...] += jnp.sum((dn * xh).reshape(SUB // 8, 8, HEAD), axis=0)
                dxh = dn * q_gain
                gq = r * (dxh - xh * jnp.mean(dxh * xh, axis=1, keepdims=True))
                gq_ref[tokens, columns] = gq.astype(jnp.bfloat16)
        dk[...] += dot(ds_ref[...], qhat[pl.ds(at, 512), :])
        dv[...] += dot(w_ref[...], dcat[pl.ds(at, 512), :])
        for copy in copies(pair):
            copy.start()
        return carry

    lax.fori_loop(0, HEADS // 2, pair_step, 0)

    kg = jnp.zeros((8, HEAD), jnp.float32)
    outs = (r4, r3, r2, r1, own_ref)
    for j in range(parts):
        rows = slice(j * SUB, (j + 1) * SUB)
        here = slice((j % 2) * SUB, (j % 2 + 1) * SUB)
        x = blocks[j // 2][here, :].astype(jnp.float32)
        r = lax.rsqrt(jnp.mean(x * x, axis=1, keepdims=True) + EPSILON)
        xh = x * r
        d = dk[rows, :] * SCALING
        dn = d * cosine[rows, :] - half_turned(d) * sine[rows, :]
        kg = kg + jnp.sum((dn * xh).reshape(SUB // 8, 8, HEAD), axis=0)
        dxh = dn * k_gain
        gk = r * (dxh - xh * jnp.mean(dxh * xh, axis=1, keepdims=True))
        out = outs[j // 2]
        out[here, :] = gk.astype(out.dtype)
        out[TOK + (j % 2) * SUB : TOK + (j % 2 + 1) * SUB, :] = dv[rows, :].astype(out.dtype)
    gain_ref[0:1, :] = jnp.sum(qg_acc[...], axis=0, keepdims=True)
    gain_ref[1:2, :] = jnp.sum(kg, axis=0, keepdims=True)
    for pair in range(HEADS // 2):
        for copy in copies(pair):
            copy.wait()


RETURN = jnp.bfloat16


def attention(blocks, queries, output_gradient, q_gain, k_gain, frequency):
    vmem = pl.BlockSpec(memory_space=pltpu.VMEM)
    hbm = pl.BlockSpec(memory_space=pl.ANY)
    f32, bf16 = jnp.float32, jnp.bfloat16
    shape = jax.ShapeDtypeStruct
    return pl.pallas_call(
        kernel,
        out_shape=[
            shape((TOK, HEADS * HEAD), bf16),
            shape((TOK, HEADS * HEAD), bf16),
            *[shape((2 * TOK, HEAD), RETURN) for _ in range(REACH)],
            shape((2 * TOK, HEAD), f32),
            shape((2, HEAD), f32),
        ],
        in_specs=[vmem] * 5 + [hbm] * 2 + [vmem] * 3,
        out_specs=[hbm] * 2 + [vmem] * 6,
        scratch_shapes=[
            pltpu.VMEM((TOK, HEADS * HEAD), bf16),
            pltpu.VMEM((TOK, HEADS * HEAD), bf16),
            pltpu.VMEM((TOK, HEADS * HEAD), bf16),
            pltpu.VMEM((TOK, HEADS * HEAD), bf16),
            pltpu.VMEM((WINDOW, HEAD), f32),
            pltpu.VMEM((WINDOW, HEAD), f32),
            pltpu.VMEM((WINDOW, 2 * HEAD), bf16),
            pltpu.VMEM((WINDOW, HEAD), bf16),
            pltpu.VMEM((HEAD, WINDOW), bf16),
            pltpu.VMEM((HEAD, WINDOW), bf16),
            pltpu.VMEM((HEADS * TOK, HEAD), bf16),
            pltpu.VMEM((HEADS // 2, 2 * HEAD, 512), bf16),
            pltpu.VMEM((HEADS * TOK, HEAD), bf16),
            pltpu.VMEM((HEADS // 2, HEAD, 512), bf16),
            pltpu.VMEM((2, SPAN, 256), f32),
            pltpu.VMEM((WINDOW, 512), bf16),
            pltpu.VMEM((WINDOW, 512), bf16),
            pltpu.VMEM((WINDOW, HEAD), f32),
            pltpu.VMEM((WINDOW, HEAD), f32),
            pltpu.VMEM((8, HEAD), f32),
            pltpu.SemaphoreType.DMA((2,)),
            pltpu.SemaphoreType.DMA((HEADS // 2,)),
            pltpu.SemaphoreType.DMA((HEADS // 2,)),
        ],
        compiler_params=pltpu.CompilerParams(vmem_limit_bytes=40 * 1024 * 1024),
    )(*blocks, queries, output_gradient, q_gain, k_gain, frequency)


def pack_kernel(keys, values, ids, out):
    out[0:TOK, :] = keys[...]
    out[TOK : 2 * TOK, :] = values[...]
    marked = (ids[...] + 1).astype(jnp.float32)
    out[2 * TOK :, :] = jnp.concatenate(
        [marked, jnp.zeros((ID_ROWS - 2, HEAD), jnp.float32)]
    ).astype(jnp.bfloat16)


def pack(keys, values, ids):
    vmem = pl.BlockSpec(memory_space=pltpu.VMEM)
    return pl.pallas_call(
        pack_kernel,
        out_shape=jax.ShapeDtypeStruct((MSG, HEAD), jnp.bfloat16),
        in_specs=[vmem] * 3,
        out_specs=vmem,
    )(keys, values, ids)


def summed_over_all(terms):
    total = jnp.sum(lax.all_gather(terms, "tensor"), axis=0)
    rows = [list(range(8 * y, 8 * y + 8)) for y in range(4)]
    columns = [[8 * y + k for y in range(4)] for k in range(8)]
    for groups in (rows, columns):
        total = jnp.sum(lax.all_gather(total, "context", axis_index_groups=groups), axis=0)
    return total


def body(queries, keys, values, output_gradient, q_gain, k_gain, doc_ids):
    message = pack(keys, values, doc_ids.reshape(2, HEAD))
    blocks = [passed_along(message, "context", distance) for distance in range(REACH, 0, -1)]
    blocks.append(message)
    half = jnp.arange(HEAD // 2, dtype=jnp.float32)
    frequency = THETA ** (-(half * 2.0 / HEAD))
    frequency = jnp.concatenate([frequency, frequency]).reshape(1, HEAD)
    attended, query_gradient, *returns, own, gains = attention(
        blocks,
        queries,
        output_gradient,
        q_gain.reshape(1, HEAD),
        k_gain.reshape(1, HEAD),
        frequency,
    )
    total = own
    for distance, block in zip(range(REACH, 0, -1), returns):
        total = total + passed_along(block, "context", -distance)
    total = total.astype(jnp.bfloat16)
    gain_total = summed_over_all(gains)
    return (
        attended,
        query_gradient,
        total[:TOK],
        total[TOK:],
        gain_total[0],
        gain_total[1],
    )


def solution(mesh):
    placed = (
        P("context", "tensor"),
        P("context", "tensor"),
        P("context", "tensor"),
        P("context", "tensor"),
        P(),
        P(),
        P("context"),
    )
    return jax.shard_map(
        body,
        mesh=mesh,
        in_specs=placed,
        out_specs=(
            P("context", "tensor"),
            P("context", "tensor"),
            P("context", "tensor"),
            P("context", "tensor"),
            P(),
            P(),
        ),
        check_vma=False,
    )
```

```python
import jax
import jax.numpy as jnp
import numpy as np
from jax import lax
from jax.experimental import pallas as pl
from jax.experimental.pallas import tpu as pltpu
from jax.sharding import PartitionSpec as P

REACH = 4
THETA = 500000.0
EPSILON = 1e-06
TOK = 256
HEAD = 128
HEADS = 8
WINDOW = (REACH + 1) * TOK
SUB = 128
SPAN = 1152
CHUNKS = SPAN // SUB
ID_ROWS = 16
MSG = 2 * TOK + ID_ROWS
SCALING = HEAD ** (-0.5)
EXP2 = float(SCALING * np.log2(np.e))

PIO2_A = 1.5703125
PIO2_B = float(np.float32(np.round((np.pi / 2 - PIO2_A) * 2.0**23) / 2.0**23))
PIO2_C = float(np.float32(np.pi / 2 - PIO2_A - PIO2_B))


def passed_along(block, axis, distance):
    devices = range(lax.axis_size(axis))
    route = [(i - distance, i) for i in devices if i - distance in devices]
    return lax.ppermute(block, axis, route)


def dot(a, b):
    return jnp.dot(a, b, preferred_element_type=jnp.float32)


def half_turned(x):
    return pltpu.roll(x, HEAD // 2, 1)


def cos_sin(position, frequency):
    angle = position * frequency
    turns = jnp.floor(angle * np.float32(2.0 / np.pi) + 0.5)
    rest = ((angle - turns * PIO2_A) - turns * PIO2_B) - turns * PIO2_C
    square = rest * rest
    sine = rest + rest * square * (
        np.float32(-1.6666654611e-1)
        + square * (np.float32(8.3321608736e-3) + square * np.float32(-1.9515295891e-4))
    )
    cosine = (1.0 - 0.5 * square) + square * square * (
        np.float32(4.166664568298827e-2)
        + square * (np.float32(-1.388731625493765e-3) + square * np.float32(2.443315711809948e-5))
    )
    lane = lax.broadcasted_iota(jnp.int32, angle.shape, 1)
    quadrant = turns.astype(jnp.int32) + jnp.where(lane < HEAD // 2, 1, 0)
    value = jnp.where((quadrant & 1) == 1, cosine, sine)
    return jnp.where((quadrant & 2) == 2, -value, value)


def kernel(
    b4, b2, b0, first_swap, middle_swap, last_swap, q_hbm, d_hbm, qg_ref, kg_ref, f_ref,
    att_hbm, gq_hbm, r4, r3, r2, r1, own_ref, gain_ref,
    q_ref, d_ref, att_ref, gq_ref, cosine, sine, kext, vwin, khat_t, v_t, qhat, qext_t, dcat, dcat_t,
    s_ref, w_ref, ds_ref, dk, dv, qg_acc, b3, b1, in_sem, att_sem, gq_sem,
):
    q_copy = pltpu.make_async_copy(q_hbm, q_ref, in_sem.at[0])
    d_copy = pltpu.make_async_copy(d_hbm, d_ref, in_sem.at[1])
    q_copy.start()
    d_copy.start()
    even = lax.rem(lax.axis_index("context"), 2) == 0

    @pl.when(even)
    def _():
        b3[...] = last_swap[...]
        b1[...] = middle_swap[...]

    @pl.when(jnp.logical_not(even))
    def _():
        b3[...] = middle_swap[...]
        b1[...] = first_swap[...]

    blocks = (b4, b3, b2, b1, b0)
    lane = lax.broadcasted_iota(jnp.int32, (SUB, HEAD), 1)
    row = lax.broadcasted_iota(jnp.int32, (SUB, HEAD), 0)
    lane_f = lane.astype(jnp.float32)
    row_f = row.astype(jnp.float32)
    left = lane < HEAD // 2
    parts = WINDOW // SUB
    q_gain = qg_ref[...]
    k_gain = kg_ref[...]
    frequency = f_ref[...]

    id_rows = []
    for block in blocks:
        both = block[2 * TOK : MSG, :].astype(jnp.float32)
        id_rows += [both[0:1], both[1:2]]
    below = jnp.zeros((SUB, HEAD), jnp.float32)
    for j in range(parts):
        column = jnp.broadcast_to(id_rows[j], (SUB, HEAD)).T
        kext[j * SUB : (j + 1) * SUB, HEAD:] = jnp.where(column == lane_f, 1.0, 0.0).astype(jnp.bfloat16)
        below = below + jnp.where(column < lane_f, 1.0, 0.0)
    first = jnp.sum(below, axis=0, keepdims=True)

    for j in range(parts):
        rows = slice(j * SUB, (j + 1) * SUB)
        here = slice((j % 2) * SUB, (j % 2 + 1) * SUB)
        block = blocks[j // 2]
        member = kext[rows, HEAD:].astype(jnp.float32)
        start = jnp.sum(member * first, axis=1, keepdims=True)
        position = (row + j * SUB).astype(jnp.float32) - start
        both = cos_sin(position, frequency)
        turned = half_turned(both)
        c = jnp.where(left, both, turned)
        s = jnp.where(left, -turned, both)
        cosine[rows, :] = c
        sine[rows, :] = s
        x = block[here, :].astype(jnp.float32)
        normed = x * lax.rsqrt(jnp.mean(x * x, axis=1, keepdims=True) + EPSILON) * k_gain
        hat = normed * c + half_turned(normed) * s
        kext[rows, 0:HEAD] = hat.astype(jnp.bfloat16)
        khat_t[:, rows] = hat.T.astype(jnp.bfloat16)
        values = block[TOK + (j % 2) * SUB : TOK + (j % 2 + 1) * SUB, :]
        vwin[rows, :] = values
        v_t[:, rows] = values.astype(jnp.float32).T.astype(jnp.bfloat16)

    q_copy.wait()
    d_copy.wait()
    for sub in range(2):
        tokens = slice(sub * SUB, (sub + 1) * SUB)
        window_rows = slice(REACH * TOK + sub * SUB, REACH * TOK + (sub + 1) * SUB)
        c_q = cosine[window_rows, :]
        s_q = sine[window_rows, :]
        other = jnp.where(row_f == id_rows[2 * REACH + sub], 0.0, -1e30).astype(jnp.bfloat16)
        for h in range(HEADS):
            at = (h // 2) * 512 + sub * 256 + (h % 2) * SUB
            lanes = slice(at % 512, at % 512 + SUB)
            x = q_ref[tokens, h * HEAD : (h + 1) * HEAD].astype(jnp.float32)
            normed = x * lax.rsqrt(jnp.mean(x * x, axis=1, keepdims=True) + EPSILON) * q_gain
            hat = normed * c_q + half_turned(normed) * s_q
            qhat[at : at + SUB, :] = hat.astype(jnp.bfloat16)
            qext_t[h // 2, 0:HEAD, lanes] = hat.T.astype(jnp.bfloat16)
            qext_t[h // 2, HEAD:, lanes] = other
            d = d_ref[tokens, h * HEAD : (h + 1) * HEAD]
            dcat[at : at + SUB, :] = d
            dcat_t[h // 2, :, lanes] = d.astype(jnp.float32).T.astype(jnp.bfloat16)

    dk[...] = jnp.zeros_like(dk)
    dv[...] = jnp.zeros_like(dv)
    qg_acc[...] = jnp.zeros_like(qg_acc)
    zero = jnp.zeros((SUB, 256), jnp.bfloat16)
    for ref in (w_ref, ds_ref):
        ref[0:SUB, 256:512] = zero
        ref[SPAN:WINDOW, 0:256] = zero
    later = jnp.where(row <= lane, 0.0, -1e30)
    later = jnp.concatenate([later, later], axis=1)
    last = SPAN - SUB

    def copies(pair):
        columns = pl.ds(pl.multiple_of(pair * 256, 256), 256)
        return (
            pltpu.make_async_copy(att_ref.at[:, columns], att_hbm.at[:, columns], att_sem.at[pair]),
            pltpu.make_async_copy(gq_ref.at[:, columns], gq_hbm.at[:, columns], gq_sem.at[pair]),
        )

    def pair_step(pair, carry):
        at = pl.multiple_of(pair * 512, 512)
        spans = (slice(0, SPAN), slice(SUB, WINDOW))
        columns_of = (slice(0, 256), slice(256, 512))
        shifts = []
        for sub in range(2):
            cols = columns_of[sub]
            s = dot(kext[spans[sub], :], qext_t[pair, :, cols])
            tail = s[last:] + later
            s_ref[sub, 0:last, :] = s[:last]
            s_ref[sub, last:, :] = tail
            top = jnp.maximum(
                jnp.max(s[:last].reshape(last // 8, 8, 256), axis=0),
                jnp.max(tail.reshape(SUB // 8, 8, 256), axis=0),
            )
            shifts.append(jnp.max(top, axis=0, keepdims=True) * EXP2)
        att_ts = []
        for sub in range(2):
            cols = columns_of[sub]
            base = sub * SUB
            total = jnp.zeros((8, 256), jnp.float32)
            for c in range(CHUNKS):
                e = jnp.exp2(s_ref[sub, c * SUB : (c + 1) * SUB, :] * EXP2 - shifts[sub])
                s_ref[sub, c * SUB : (c + 1) * SUB, :] = e
                total = total + jnp.sum(e.reshape(SUB // 8, 8, 256), axis=0)
            inverse = 1.0 / jnp.sum(total, axis=0, keepdims=True)
            for c in range(CHUNKS):
                keys = slice(base + c * SUB, base + (c + 1) * SUB)
                w = s_ref[sub, c * SUB : (c + 1) * SUB, :] * inverse
                w_ref[keys, cols] = w.astype(jnp.bfloat16)
            att_ts.append(dot(v_t[:, spans[sub]], w_ref[spans[sub], cols]))
        for sub in range(2):
            cols = columns_of[sub]
            span = spans[sub]
            att_t = att_ts[sub]
            d_t = dcat_t[pair, :, cols]
            center = jnp.sum(att_t * d_t.astype(jnp.float32), axis=0, keepdims=True)
            dw = dot(vwin[span, :], d_t)
            ds = w_ref[span, cols].astype(jnp.float32) * (dw - center)
            ds_ref[span, cols] = ds.astype(jnp.bfloat16)
            dq_t = dot(khat_t[:, span], ds_ref[span, cols]) * SCALING
            tokens = slice(sub * SUB, (sub + 1) * SUB)
            window_rows = slice(REACH * TOK + sub * SUB, REACH * TOK + (sub + 1) * SUB)
            c_q = cosine[window_rows, :]
            s_q = sine[window_rows, :]
            for g in range(2):
                columns = pl.ds(pl.multiple_of(pair * 256 + g * HEAD, HEAD), HEAD)
                att = att_t[:, g * SUB : (g + 1) * SUB].T
                att_ref[tokens, columns] = att.astype(jnp.bfloat16)
                dq = dq_t[:, g * SUB : (g + 1) * SUB].T
                x = q_ref[tokens, columns].astype(jnp.float32)
                r = lax.rsqrt(jnp.mean(x * x, axis=1, keepdims=True) + EPSILON)
                xh = x * r
                dn = dq * c_q - half_turned(dq) * s_q
                qg_acc[...] += jnp.sum((dn * xh).reshape(SUB // 8, 8, HEAD), axis=0)
                dxh = dn * q_gain
                gq = r * (dxh - xh * jnp.mean(dxh * xh, axis=1, keepdims=True))
                gq_ref[tokens, columns] = gq.astype(jnp.bfloat16)
        dk[...] += dot(ds_ref[...], qhat[pl.ds(at, 512), :])
        dv[...] += dot(w_ref[...], dcat[pl.ds(at, 512), :])
        for copy in copies(pair):
            copy.start()
        return carry

    lax.fori_loop(0, HEADS // 2, pair_step, 0)

    kg = jnp.zeros((8, HEAD), jnp.float32)
    outs = (r4, r3, r2, r1, own_ref)
    for j in range(parts):
        rows = slice(j * SUB, (j + 1) * SUB)
        here = slice((j % 2) * SUB, (j % 2 + 1) * SUB)
        x = blocks[j // 2][here, :].astype(jnp.float32)
        r = lax.rsqrt(jnp.mean(x * x, axis=1, keepdims=True) + EPSILON)
        xh = x * r
        d = dk[rows, :] * SCALING
        dn = d * cosine[rows, :] - half_turned(d) * sine[rows, :]
        kg = kg + jnp.sum((dn * xh).reshape(SUB // 8, 8, HEAD), axis=0)
        dxh = dn * k_gain
        gk = r * (dxh - xh * jnp.mean(dxh * xh, axis=1, keepdims=True))
        out = outs[j // 2]
        out[here, :] = gk.astype(out.dtype)
        out[TOK + (j % 2) * SUB : TOK + (j % 2 + 1) * SUB, :] = dv[rows, :].astype(out.dtype)
    gain_ref[0:1, :] = jnp.sum(qg_acc[...], axis=0, keepdims=True)
    gain_ref[1:2, :] = jnp.sum(kg, axis=0, keepdims=True)
    for pair in range(HEADS // 2):
        for copy in copies(pair):
            copy.wait()


RETURN = jnp.bfloat16


def attention(blocks, queries, output_gradient, q_gain, k_gain, frequency):
    vmem = pl.BlockSpec(memory_space=pltpu.VMEM)
    hbm = pl.BlockSpec(memory_space=pl.ANY)
    f32, bf16 = jnp.float32, jnp.bfloat16
    shape = jax.ShapeDtypeStruct
    return pl.pallas_call(
        kernel,
        out_shape=[
            shape((TOK, HEADS * HEAD), bf16),
            shape((TOK, HEADS * HEAD), bf16),
            *[shape((2 * TOK, HEAD), RETURN) for _ in range(REACH)],
            shape((2 * TOK, HEAD), f32),
            shape((2, HEAD), f32),
        ],
        in_specs=[vmem] * 6 + [hbm] * 2 + [vmem] * 3,
        out_specs=[hbm] * 2 + [vmem] * 6,
        scratch_shapes=[
            pltpu.VMEM((TOK, HEADS * HEAD), bf16),
            pltpu.VMEM((TOK, HEADS * HEAD), bf16),
            pltpu.VMEM((TOK, HEADS * HEAD), bf16),
            pltpu.VMEM((TOK, HEADS * HEAD), bf16),
            pltpu.VMEM((WINDOW, HEAD), f32),
            pltpu.VMEM((WINDOW, HEAD), f32),
            pltpu.VMEM((WINDOW, 2 * HEAD), bf16),
            pltpu.VMEM((WINDOW, HEAD), bf16),
            pltpu.VMEM((HEAD, WINDOW), bf16),
            pltpu.VMEM((HEAD, WINDOW), bf16),
            pltpu.VMEM((HEADS * TOK, HEAD), bf16),
            pltpu.VMEM((HEADS // 2, 2 * HEAD, 512), bf16),
            pltpu.VMEM((HEADS * TOK, HEAD), bf16),
            pltpu.VMEM((HEADS // 2, HEAD, 512), bf16),
            pltpu.VMEM((2, SPAN, 256), f32),
            pltpu.VMEM((WINDOW, 512), bf16),
            pltpu.VMEM((WINDOW, 512), bf16),
            pltpu.VMEM((WINDOW, HEAD), f32),
            pltpu.VMEM((WINDOW, HEAD), f32),
            pltpu.VMEM((8, HEAD), f32),
            pltpu.VMEM((MSG, HEAD), bf16),
            pltpu.VMEM((MSG, HEAD), bf16),
            pltpu.SemaphoreType.DMA((2,)),
            pltpu.SemaphoreType.DMA((HEADS // 2,)),
            pltpu.SemaphoreType.DMA((HEADS // 2,)),
        ],
        compiler_params=pltpu.CompilerParams(vmem_limit_bytes=40 * 1024 * 1024),
    )(*blocks, queries, output_gradient, q_gain, k_gain, frequency)


def pack_kernel(keys, values, ids, out):
    out[0:TOK, :] = keys[...]
    out[TOK : 2 * TOK, :] = values[...]
    marked = (ids[...] + 1).astype(jnp.float32)
    out[2 * TOK :, :] = jnp.concatenate(
        [marked, jnp.zeros((ID_ROWS - 2, HEAD), jnp.float32)]
    ).astype(jnp.bfloat16)


def pack(keys, values, ids):
    vmem = pl.BlockSpec(memory_space=pltpu.VMEM)
    return pl.pallas_call(
        pack_kernel,
        out_shape=jax.ShapeDtypeStruct((MSG, HEAD), jnp.bfloat16),
        in_specs=[vmem] * 3,
        out_specs=vmem,
    )(keys, values, ids)


def swapped(block, ways=(0, 1)):
    route = [(i, i ^ 1) for i in range(lax.axis_size("context")) if i % 2 in ways]
    return lax.ppermute(block, "context", route)


def summed_over(axis, terms):
    copies = jnp.broadcast_to(terms, (lax.axis_size(axis),) + terms.shape)
    return jnp.sum(lax.all_to_all(copies, axis, 0, 0), axis=0)


def body(queries, keys, values, output_gradient, q_gain, k_gain, doc_ids):
    message = pack(keys, values, doc_ids.reshape(2, HEAD))
    two = passed_along(message, "context", 2)
    first_swap = swapped(message, (0,))
    four = passed_along(two, "context", 2)
    middle_swap = swapped(two)
    last_swap = swapped(four, (1,))
    blocks = [four, two, message, first_swap, middle_swap, last_swap]
    half = jnp.arange(HEAD // 2, dtype=jnp.float32)
    frequency = THETA ** (-(half * 2.0 / HEAD))
    frequency = jnp.concatenate([frequency, frequency]).reshape(1, HEAD)
    attended, query_gradient, *returns, own, gains = attention(
        blocks,
        queries,
        output_gradient,
        q_gain.reshape(1, HEAD),
        k_gain.reshape(1, HEAD),
        frequency,
    )
    total = own
    for distance, block in zip(range(REACH, 0, -1), returns):
        total = total + passed_along(block, "context", -distance)
    total = total.astype(jnp.bfloat16)
    gain_total = summed_over("context", summed_over("tensor", gains))
    return (
        attended,
        query_gradient,
        total[:TOK],
        total[TOK:],
        gain_total[0],
        gain_total[1],
    )


def solution(mesh):
    placed = (
        P("context", "tensor"),
        P("context", "tensor"),
        P("context", "tensor"),
        P("context", "tensor"),
        P(),
        P(),
        P("context"),
    )
    return jax.shard_map(
        body,
        mesh=mesh,
        in_specs=placed,
        out_specs=(
            P("context", "tensor"),
            P("context", "tensor"),
            P("context", "tensor"),
            P("context", "tensor"),
            P(),
            P(),
        ),
        check_vma=False,
    )
```

```python
import jax
import jax.numpy as jnp
import numpy as np
from jax import lax
from jax.experimental import pallas as pl
from jax.experimental.pallas import tpu as pltpu
from jax.sharding import PartitionSpec as P

REACH = 4
THETA = 500000.0
EPSILON = 1e-06
TOK = 256
HEAD = 128
HEADS = 8
WINDOW = (REACH + 1) * TOK
SUB = 128
SPAN = 1152
CHUNKS = SPAN // SUB
ID_ROWS = 16
MSG = 2 * TOK + ID_ROWS
SCALING = HEAD ** (-0.5)
EXP2 = float(SCALING * np.log2(np.e))

PIO2_A = 1.5703125
PIO2_B = float(np.float32(np.round((np.pi / 2 - PIO2_A) * 2.0**23) / 2.0**23))
PIO2_C = float(np.float32(np.pi / 2 - PIO2_A - PIO2_B))


def passed_along(block, axis, distance):
    devices = range(lax.axis_size(axis))
    route = [(i - distance, i) for i in devices if i - distance in devices]
    return lax.ppermute(block, axis, route)


def dot(a, b):
    return jnp.dot(a, b, preferred_element_type=jnp.float32)


def half_turned(x):
    return pltpu.roll(x, HEAD // 2, 1)


def cos_sin(position, frequency):
    angle = position * frequency
    turns = jnp.floor(angle * np.float32(2.0 / np.pi) + 0.5)
    rest = ((angle - turns * PIO2_A) - turns * PIO2_B) - turns * PIO2_C
    square = rest * rest
    sine = rest + rest * square * (
        np.float32(-1.6666654611e-1)
        + square * (np.float32(8.3321608736e-3) + square * np.float32(-1.9515295891e-4))
    )
    cosine = (1.0 - 0.5 * square) + square * square * (
        np.float32(4.166664568298827e-2)
        + square * (np.float32(-1.388731625493765e-3) + square * np.float32(2.443315711809948e-5))
    )
    lane = lax.broadcasted_iota(jnp.int32, angle.shape, 1)
    quadrant = turns.astype(jnp.int32) + jnp.where(lane < HEAD // 2, 1, 0)
    value = jnp.where((quadrant & 1) == 1, cosine, sine)
    return jnp.where((quadrant & 2) == 2, -value, value)


def prepare_kernel(q_ref, d_ref, xh_ref, scale_ref, dcat, dcat_t):
    for sub in range(2):
        tokens = slice(sub * SUB, (sub + 1) * SUB)
        for h in range(HEADS):
            at = (h // 2) * 512 + sub * 256 + (h % 2) * SUB
            rows = slice(at, at + SUB)
            x = q_ref[tokens, h * HEAD : (h + 1) * HEAD].astype(jnp.float32)
            r = lax.rsqrt(jnp.mean(x * x, axis=1, keepdims=True) + EPSILON)
            xh_ref[rows, :] = x * r
            scale_ref[rows, :] = jnp.broadcast_to(r, (SUB, HEAD))
            d = d_ref[tokens, h * HEAD : (h + 1) * HEAD]
            dcat[rows, :] = d
            dcat_t[h // 2, :, at % 512 : at % 512 + SUB] = d.astype(jnp.float32).T.astype(jnp.bfloat16)


def prepare(queries, output_gradient):
    vmem = pl.BlockSpec(memory_space=pltpu.VMEM)
    f32, bf16 = jnp.float32, jnp.bfloat16
    shape = jax.ShapeDtypeStruct
    return pl.pallas_call(
        prepare_kernel,
        out_shape=[
            shape((HEADS * TOK, HEAD), f32),
            shape((HEADS * TOK, HEAD), f32),
            shape((HEADS * TOK, HEAD), bf16),
            shape((HEADS // 2, HEAD, 512), bf16),
        ],
        in_specs=[vmem] * 2,
        out_specs=[vmem] * 4,
        cost_estimate=pl.CostEstimate(flops=10**9, bytes_accessed=4 * 2**20, transcendentals=0),
    )(queries, output_gradient)


def kernel(
    b4, b2, b0, first_swap, middle_swap, last_swap, xh_ref, scale_ref, dcat, dcat_t, qg_ref, kg_ref, f_ref,
    att_hbm, gq_hbm, r4, r3, r2, r1, own_ref, gain_ref,
    att_ref, gq_ref, cosine, sine, kext, vwin, khat_t, v_t, qhat, qext_t,
    s_ref, w_ref, ds_ref, dk, dv, qg_acc, b3, b1, att_sem, gq_sem,
):
    even = lax.rem(lax.axis_index("context"), 2) == 0

    @pl.when(even)
    def _():
        b3[...] = last_swap[...]
        b1[...] = middle_swap[...]

    @pl.when(jnp.logical_not(even))
    def _():
        b3[...] = middle_swap[...]
        b1[...] = first_swap[...]

    blocks = (b4, b3, b2, b1, b0)
    lane = lax.broadcasted_iota(jnp.int32, (SUB, HEAD), 1)
    row = lax.broadcasted_iota(jnp.int32, (SUB, HEAD), 0)
    lane_f = lane.astype(jnp.float32)
    row_f = row.astype(jnp.float32)
    left = lane < HEAD // 2
    parts = WINDOW // SUB
    q_gain = qg_ref[...]
    k_gain = kg_ref[...]
    frequency = f_ref[...]

    id_rows = []
    for block in blocks:
        both = block[2 * TOK : MSG, :].astype(jnp.float32)
        id_rows += [both[0:1], both[1:2]]
    below = jnp.zeros((SUB, HEAD), jnp.float32)
    for j in range(parts):
        column = jnp.broadcast_to(id_rows[j], (SUB, HEAD)).T
        kext[j * SUB : (j + 1) * SUB, HEAD:] = jnp.where(column == lane_f, 1.0, 0.0).astype(jnp.bfloat16)
        below = below + jnp.where(column < lane_f, 1.0, 0.0)
    first = jnp.sum(below, axis=0, keepdims=True)

    for j in range(parts):
        rows = slice(j * SUB, (j + 1) * SUB)
        here = slice((j % 2) * SUB, (j % 2 + 1) * SUB)
        block = blocks[j // 2]
        member = kext[rows, HEAD:].astype(jnp.float32)
        start = jnp.sum(member * first, axis=1, keepdims=True)
        position = (row + j * SUB).astype(jnp.float32) - start
        both = cos_sin(position, frequency)
        turned = half_turned(both)
        c = jnp.where(left, both, turned)
        s = jnp.where(left, -turned, both)
        cosine[rows, :] = c
        sine[rows, :] = s
        x = block[here, :].astype(jnp.float32)
        normed = x * lax.rsqrt(jnp.mean(x * x, axis=1, keepdims=True) + EPSILON) * k_gain
        hat = normed * c + half_turned(normed) * s
        kext[rows, 0:HEAD] = hat.astype(jnp.bfloat16)
        khat_t[:, rows] = hat.T.astype(jnp.bfloat16)
        values = block[TOK + (j % 2) * SUB : TOK + (j % 2 + 1) * SUB, :]
        vwin[rows, :] = values
        v_t[:, rows] = values.astype(jnp.float32).T.astype(jnp.bfloat16)

    for sub in range(2):
        window_rows = slice(REACH * TOK + sub * SUB, REACH * TOK + (sub + 1) * SUB)
        c_q = cosine[window_rows, :]
        s_q = sine[window_rows, :]
        other = jnp.where(row_f == id_rows[2 * REACH + sub], 0.0, -1e30).astype(jnp.bfloat16)
        for h in range(HEADS):
            at = (h // 2) * 512 + sub * 256 + (h % 2) * SUB
            lanes = slice(at % 512, at % 512 + SUB)
            normed = xh_ref[at : at + SUB, :] * q_gain
            hat = normed * c_q + half_turned(normed) * s_q
            qhat[at : at + SUB, :] = hat.astype(jnp.bfloat16)
            qext_t[h // 2, 0:HEAD, lanes] = hat.T.astype(jnp.bfloat16)
            qext_t[h // 2, HEAD:, lanes] = other

    dk[...] = jnp.zeros_like(dk)
    dv[...] = jnp.zeros_like(dv)
    qg_acc[...] = jnp.zeros_like(qg_acc)
    zero = jnp.zeros((SUB, 256), jnp.bfloat16)
    for ref in (w_ref, ds_ref):
        ref[0, 0:SUB, 256:512] = zero
        ref[0, SPAN:WINDOW, 0:256] = zero
        ref[1] = jnp.zeros((WINDOW, 512), jnp.bfloat16)
    later = jnp.where(row <= lane, 0.0, -1e30)
    later = jnp.concatenate([later, later], axis=1)
    last = SPAN - SUB
    spans = (slice(0, SPAN), slice(SUB, WINDOW))
    columns_of = (slice(0, 256), slice(256, 512))

    def copies(pair):
        columns = pl.ds(pl.multiple_of(pair * 256, 256), 256)
        return (
            pltpu.make_async_copy(att_ref.at[:, columns], att_hbm.at[:, columns], att_sem.at[pair]),
            pltpu.make_async_copy(gq_ref.at[:, columns], gq_hbm.at[:, columns], gq_sem.at[pair]),
        )

    def key_terms(pair, slot):
        at = pl.multiple_of(pair * 512, 512)
        dk[...] += dot(ds_ref[slot], qhat[pl.ds(at, 512), :])
        dv[...] += dot(w_ref[slot], dcat[pl.ds(at, 512), :])

    def pair_step(pair, carry):
        at = pl.multiple_of(pair * 512, 512)
        slot = lax.rem(pair, 2)

        def scores(sub):
            s = dot(kext[spans[sub], :], qext_t[pair, :, columns_of[sub]])
            tail = s[last:] + later
            s_ref[sub, 0:last, :] = s[:last]
            s_ref[sub, last:, :] = tail
            top = jnp.maximum(
                jnp.max(s[:last].reshape(last // 8, 8, 256), axis=0),
                jnp.max(tail.reshape(SUB // 8, 8, 256), axis=0),
            )
            return jnp.max(top, axis=0, keepdims=True) * EXP2

        def exponents(sub, shift):
            total = jnp.zeros((8, 256), jnp.float32)
            for c in range(CHUNKS):
                e = jnp.exp2(s_ref[sub, c * SUB : (c + 1) * SUB, :] * EXP2 - shift)
                s_ref[sub, c * SUB : (c + 1) * SUB, :] = e
                total = total + jnp.sum(e.reshape(SUB // 8, 8, 256), axis=0)
            return 1.0 / jnp.sum(total, axis=0, keepdims=True)

        def weigh(sub, inverse):
            for c in range(CHUNKS):
                keys = slice((sub + c) * SUB, (sub + c + 1) * SUB)
                w = s_ref[sub, c * SUB : (c + 1) * SUB, :] * inverse
                w_ref[slot, keys, columns_of[sub]] = w.astype(jnp.bfloat16)

        def attend(sub):
            att_t = dot(v_t[:, spans[sub]], w_ref[slot, spans[sub], columns_of[sub]])
            d_t = dcat_t[pair, :, columns_of[sub]]
            center = jnp.sum(att_t * d_t.astype(jnp.float32), axis=0, keepdims=True)
            tokens = slice(sub * SUB, (sub + 1) * SUB)
            for g in range(2):
                columns = pl.ds(pl.multiple_of(pair * 256 + g * HEAD, HEAD), HEAD)
                att_ref[tokens, columns] = att_t[:, g * SUB : (g + 1) * SUB].T.astype(jnp.bfloat16)
            return center

        def score_terms(sub, center):
            dw = dot(vwin[spans[sub], :], dcat_t[pair, :, columns_of[sub]])
            w = w_ref[slot, spans[sub], columns_of[sub]].astype(jnp.float32)
            ds_ref[slot, spans[sub], columns_of[sub]] = (w * (dw - center)).astype(jnp.bfloat16)

        def query_terms(sub):
            dq_t = dot(khat_t[:, spans[sub]], ds_ref[slot, spans[sub], columns_of[sub]]) * SCALING
            tokens = slice(sub * SUB, (sub + 1) * SUB)
            window_rows = slice(REACH * TOK + sub * SUB, REACH * TOK + (sub + 1) * SUB)
            c_q = cosine[window_rows, :]
            s_q = sine[window_rows, :]
            for g in range(2):
                columns = pl.ds(pl.multiple_of(pair * 256 + g * HEAD, HEAD), HEAD)
                rows = pl.ds(pl.multiple_of(at + sub * 256 + g * SUB, SUB), SUB)
                dq = dq_t[:, g * SUB : (g + 1) * SUB].T
                xh = xh_ref[rows, :]
                dn = dq * c_q - half_turned(dq) * s_q
                qg_acc[...] += jnp.sum((dn * xh).reshape(SUB // 8, 8, HEAD), axis=0)
                dxh = dn * q_gain
                gq = scale_ref[rows, :] * (dxh - xh * jnp.mean(dxh * xh, axis=1, keepdims=True))
                gq_ref[tokens, columns] = gq.astype(jnp.bfloat16)

        shift_0 = scores(0)
        shift_1 = scores(1)
        inverse_0 = exponents(0, shift_0)
        key_terms(jnp.maximum(pair - 1, 0), 1 - slot)
        weigh(0, inverse_0)
        inverse_1 = exponents(1, shift_1)
        center_0 = attend(0)
        score_terms(0, center_0)
        weigh(1, inverse_1)
        query_terms(0)
        center_1 = attend(1)
        score_terms(1, center_1)
        query_terms(1)
        for copy in copies(pair):
            copy.start()

        @pl.when(pair == 0)
        def _():
            for ref in (w_ref, ds_ref):
                ref[1, 0:SUB, 256:512] = zero
                ref[1, SPAN:WINDOW, 0:256] = zero

        return carry

    lax.fori_loop(0, HEADS // 2, pair_step, 0)
    key_terms(HEADS // 2 - 1, 1)

    kg = jnp.zeros((8, HEAD), jnp.float32)
    outs = (r4, r3, r2, r1, own_ref)
    for j in range(parts):
        rows = slice(j * SUB, (j + 1) * SUB)
        here = slice((j % 2) * SUB, (j % 2 + 1) * SUB)
        x = blocks[j // 2][here, :].astype(jnp.float32)
        r = lax.rsqrt(jnp.mean(x * x, axis=1, keepdims=True) + EPSILON)
        xh = x * r
        d = dk[rows, :] * SCALING
        dn = d * cosine[rows, :] - half_turned(d) * sine[rows, :]
        kg = kg + jnp.sum((dn * xh).reshape(SUB // 8, 8, HEAD), axis=0)
        dxh = dn * k_gain
        gk = r * (dxh - xh * jnp.mean(dxh * xh, axis=1, keepdims=True))
        out = outs[j // 2]
        out[here, :] = gk.astype(out.dtype)
        out[TOK + (j % 2) * SUB : TOK + (j % 2 + 1) * SUB, :] = dv[rows, :].astype(out.dtype)
    gains = jnp.concatenate(
        [jnp.sum(qg_acc[...], axis=0, keepdims=True), jnp.sum(kg, axis=0, keepdims=True)]
    )
    for i in range(gain_ref.shape[0]):
        gain_ref[i] = gains
    for pair in range(HEADS // 2):
        for copy in copies(pair):
            copy.wait()


RETURN = jnp.bfloat16
GROUP = 16


def attention(blocks, prepared, q_gain, k_gain, frequency):
    vmem = pl.BlockSpec(memory_space=pltpu.VMEM)
    hbm = pl.BlockSpec(memory_space=pl.ANY)
    f32, bf16 = jnp.float32, jnp.bfloat16
    shape = jax.ShapeDtypeStruct
    return pl.pallas_call(
        kernel,
        out_shape=[
            shape((TOK, HEADS * HEAD), bf16),
            shape((TOK, HEADS * HEAD), bf16),
            *[shape((2 * TOK, HEAD), RETURN) for _ in range(REACH)],
            shape((2 * TOK, HEAD), f32),
            shape((GROUP, 2, HEAD), f32),
        ],
        in_specs=[vmem] * 13,
        out_specs=[hbm] * 2 + [vmem] * 6,
        scratch_shapes=[
            pltpu.VMEM((TOK, HEADS * HEAD), bf16),
            pltpu.VMEM((TOK, HEADS * HEAD), bf16),
            pltpu.VMEM((WINDOW, HEAD), f32),
            pltpu.VMEM((WINDOW, HEAD), f32),
            pltpu.VMEM((WINDOW, 2 * HEAD), bf16),
            pltpu.VMEM((WINDOW, HEAD), bf16),
            pltpu.VMEM((HEAD, WINDOW), bf16),
            pltpu.VMEM((HEAD, WINDOW), bf16),
            pltpu.VMEM((HEADS * TOK, HEAD), bf16),
            pltpu.VMEM((HEADS // 2, 2 * HEAD, 512), bf16),
            pltpu.VMEM((2, SPAN, 256), f32),
            pltpu.VMEM((2, WINDOW, 512), bf16),
            pltpu.VMEM((2, WINDOW, 512), bf16),
            pltpu.VMEM((WINDOW, HEAD), f32),
            pltpu.VMEM((WINDOW, HEAD), f32),
            pltpu.VMEM((8, HEAD), f32),
            pltpu.VMEM((MSG, HEAD), bf16),
            pltpu.VMEM((MSG, HEAD), bf16),
            pltpu.SemaphoreType.DMA((HEADS // 2,)),
            pltpu.SemaphoreType.DMA((HEADS // 2,)),
        ],
        compiler_params=pltpu.CompilerParams(vmem_limit_bytes=40 * 1024 * 1024),
    )(*blocks, *prepared, q_gain, k_gain, frequency)


def pack_kernel(keys, values, ids, out):
    out[0:TOK, :] = keys[...]
    out[TOK : 2 * TOK, :] = values[...]
    marked = (ids[...] + 1).astype(jnp.float32)
    out[2 * TOK :, :] = jnp.concatenate(
        [marked, jnp.zeros((ID_ROWS - 2, HEAD), jnp.float32)]
    ).astype(jnp.bfloat16)


def pack(keys, values, ids):
    vmem = pl.BlockSpec(memory_space=pltpu.VMEM)
    return pl.pallas_call(
        pack_kernel,
        out_shape=jax.ShapeDtypeStruct((MSG, HEAD), jnp.bfloat16),
        in_specs=[vmem] * 3,
        out_specs=vmem,
    )(keys, values, ids)


def swapped(block, ways=(0, 1)):
    route = [(i, i ^ 1) for i in range(lax.axis_size("context")) if i % 2 in ways]
    return lax.ppermute(block, "context", route)


def group_terms(copies, groups):
    everyone = lax.all_to_all(copies, ("context", "tensor"), 0, 0, axis_index_groups=groups)
    return jnp.sum(everyone, axis=0)


def body(queries, keys, values, output_gradient, q_gain, k_gain, doc_ids):
    message = pack(keys, values, doc_ids.reshape(2, HEAD))
    two = passed_along(message, "context", 2)
    first_swap = swapped(message, (0,))
    four = passed_along(message, "context", 4)
    prepared = prepare(queries, output_gradient)
    two, *prepared = lax.optimization_barrier((two, *prepared))
    middle_swap = swapped(two)
    last_swap = swapped(four, (1,))
    blocks = [four, two, message, first_swap, middle_swap, last_swap]
    half = jnp.arange(HEAD // 2, dtype=jnp.float32)
    frequency = THETA ** (-(half * 2.0 / HEAD))
    frequency = jnp.concatenate([frequency, frequency]).reshape(1, HEAD)
    attended, query_gradient, *returns, own, gains = attention(
        blocks,
        prepared,
        q_gain.reshape(1, HEAD),
        k_gain.reshape(1, HEAD),
        frequency,
    )
    total = own
    for distance, block in zip(range(REACH, 0, -1), returns):
        total = total + passed_along(block, "context", -distance)
    total = total.astype(jnp.bfloat16)
    chips = [[GROUP * n + k for k in range(GROUP)] for n in range(GROUP)]
    places = [[GROUP * n + k for n in range(GROUP)] for k in range(GROUP)]
    chip_gains = group_terms(gains, chips)
    gain_total = group_terms(jnp.broadcast_to(chip_gains, gains.shape), places)
    return (
        attended,
        query_gradient,
        total[:TOK],
        total[TOK:],
        gain_total[0],
        gain_total[1],
    )


def solution(mesh):
    placed = (
        P("context", "tensor"),
        P("context", "tensor"),
        P("context", "tensor"),
        P("context", "tensor"),
        P(),
        P(),
        P("context"),
    )
    return jax.shard_map(
        body,
        mesh=mesh,
        in_specs=placed,
        out_specs=(
            P("context", "tensor"),
            P("context", "tensor"),
            P("context", "tensor"),
            P("context", "tensor"),
            P(),
            P(),
        ),
        check_vma=False,
    )
```

```python
import jax
import jax.numpy as jnp
import numpy as np
from jax import lax
from jax.experimental import pallas as pl
from jax.experimental.pallas import tpu as pltpu
from jax.sharding import PartitionSpec as P

REACH = 4
THETA = 500000.0
EPSILON = 1e-06
TOK = 256
HEAD = 128
HEADS = 8
WINDOW = (REACH + 1) * TOK
SUB = 128
SPAN = 1152
CHUNKS = SPAN // SUB
ID_ROWS = 16
MSG = 2 * TOK + ID_ROWS
SCALING = HEAD ** (-0.5)
EXP2 = float(SCALING * np.log2(np.e))

PIO2_A = 1.5703125
PIO2_B = float(np.float32(np.round((np.pi / 2 - PIO2_A) * 2.0**23) / 2.0**23))
PIO2_C = float(np.float32(np.pi / 2 - PIO2_A - PIO2_B))


def passed_along(block, axis, distance):
    devices = range(lax.axis_size(axis))
    route = [(i - distance, i) for i in devices if i - distance in devices]
    return lax.ppermute(block, axis, route)


def dot(a, b):
    return jnp.dot(a, b, preferred_element_type=jnp.float32)


def half_turned(x):
    return pltpu.roll(x, HEAD // 2, 1)


def cos_sin(position, frequency):
    angle = position * frequency
    turns = jnp.floor(angle * np.float32(2.0 / np.pi) + 0.5)
    rest = ((angle - turns * PIO2_A) - turns * PIO2_B) - turns * PIO2_C
    square = rest * rest
    sine = rest + rest * square * (
        np.float32(-1.6666654611e-1)
        + square * (np.float32(8.3321608736e-3) + square * np.float32(-1.9515295891e-4))
    )
    cosine = (1.0 - 0.5 * square) + square * square * (
        np.float32(4.166664568298827e-2)
        + square * (np.float32(-1.388731625493765e-3) + square * np.float32(2.443315711809948e-5))
    )
    lane = lax.broadcasted_iota(jnp.int32, angle.shape, 1)
    quadrant = turns.astype(jnp.int32) + jnp.where(lane < HEAD // 2, 1, 0)
    value = jnp.where((quadrant & 1) == 1, cosine, sine)
    return jnp.where((quadrant & 2) == 2, -value, value)


def prepare_kernel(q_ref, d_ref, qg_ref, kg_ref, xh_ref, scale_ref, dcat, dcat_t, gains):
    gains[0:1, :] = qg_ref[...]
    gains[1:2, :] = kg_ref[...]
    for sub in range(2):
        tokens = slice(sub * SUB, (sub + 1) * SUB)
        for h in range(HEADS):
            at = (h // 2) * 512 + sub * 256 + (h % 2) * SUB
            rows = slice(at, at + SUB)
            x = q_ref[tokens, h * HEAD : (h + 1) * HEAD].astype(jnp.float32)
            r = lax.rsqrt(jnp.mean(x * x, axis=1, keepdims=True) + EPSILON)
            xh_ref[rows, :] = x * r
            scale_ref[rows, :] = jnp.broadcast_to(r, (SUB, HEAD))
            d = d_ref[tokens, h * HEAD : (h + 1) * HEAD]
            dcat[rows, :] = d
            dcat_t[h // 2, :, at % 512 : at % 512 + SUB] = d.astype(jnp.float32).T.astype(jnp.bfloat16)


def prepare(queries, output_gradient, q_gain, k_gain):
    vmem = pl.BlockSpec(memory_space=pltpu.VMEM)
    f32, bf16 = jnp.float32, jnp.bfloat16
    shape = jax.ShapeDtypeStruct
    return pl.pallas_call(
        prepare_kernel,
        out_shape=[
            shape((HEADS * TOK, HEAD), f32),
            shape((HEADS * TOK, HEAD), f32),
            shape((HEADS * TOK, HEAD), bf16),
            shape((HEADS // 2, HEAD, 512), bf16),
            shape((2, HEAD), f32),
        ],
        in_specs=[vmem] * 4,
        out_specs=[vmem] * 5,
        compiler_params=pltpu.CompilerParams(vmem_limit_bytes=16 * 1024 * 1024),
        cost_estimate=pl.CostEstimate(flops=10**9, bytes_accessed=4 * 2**20, transcendentals=0),
    )(queries, output_gradient, q_gain, k_gain)


def kernel(
    b4, b2, b0, first_swap, middle_swap, last_swap, xh_ref, scale_ref, dcat, dcat_t, gains_ref, f_ref,
    att_hbm, gq_hbm, r4, r3, r2, r1, own_ref, gain_ref,
    att_ref, gq_ref, cosine, sine, kext, vwin, khat_t, v_t, qhat, qext_t,
    s_ref, w_ref, ds_ref, dk, dv, qg_acc, b3, b1, att_sem, gq_sem,
):
    even = lax.rem(lax.axis_index("context"), 2) == 0

    @pl.when(even)
    def _():
        b3[...] = last_swap[...]
        b1[...] = middle_swap[...]

    @pl.when(jnp.logical_not(even))
    def _():
        b3[...] = middle_swap[...]
        b1[...] = first_swap[...]

    blocks = (b4, b3, b2, b1, b0)
    lane = lax.broadcasted_iota(jnp.int32, (SUB, HEAD), 1)
    row = lax.broadcasted_iota(jnp.int32, (SUB, HEAD), 0)
    lane_f = lane.astype(jnp.float32)
    row_f = row.astype(jnp.float32)
    left = lane < HEAD // 2
    parts = WINDOW // SUB
    q_gain = gains_ref[0:1, :]
    k_gain = gains_ref[1:2, :]
    frequency = f_ref[...]

    id_rows = []
    for block in blocks:
        both = block[2 * TOK : MSG, :].astype(jnp.float32)
        id_rows += [both[0:1], both[1:2]]
    below = jnp.zeros((SUB, HEAD), jnp.float32)
    for j in range(parts):
        column = jnp.broadcast_to(id_rows[j], (SUB, HEAD)).T
        kext[j * SUB : (j + 1) * SUB, HEAD:] = jnp.where(column == lane_f, 1.0, 0.0).astype(jnp.bfloat16)
        below = below + jnp.where(column < lane_f, 1.0, 0.0)
    first = jnp.sum(below, axis=0, keepdims=True)

    for j in range(parts):
        rows = slice(j * SUB, (j + 1) * SUB)
        here = slice((j % 2) * SUB, (j % 2 + 1) * SUB)
        block = blocks[j // 2]
        member = kext[rows, HEAD:].astype(jnp.float32)
        start = jnp.sum(member * first, axis=1, keepdims=True)
        position = (row + j * SUB).astype(jnp.float32) - start
        both = cos_sin(position, frequency)
        turned = half_turned(both)
        c = jnp.where(left, both, turned)
        s = jnp.where(left, -turned, both)
        cosine[rows, :] = c
        sine[rows, :] = s
        x = block[here, :].astype(jnp.float32)
        normed = x * lax.rsqrt(jnp.mean(x * x, axis=1, keepdims=True) + EPSILON) * k_gain
        hat = normed * c + half_turned(normed) * s
        kext[rows, 0:HEAD] = hat.astype(jnp.bfloat16)
        khat_t[:, rows] = hat.T.astype(jnp.bfloat16)
        values = block[TOK + (j % 2) * SUB : TOK + (j % 2 + 1) * SUB, :]
        vwin[rows, :] = values
        v_t[:, rows] = values.astype(jnp.float32).T.astype(jnp.bfloat16)

    for sub in range(2):
        window_rows = slice(REACH * TOK + sub * SUB, REACH * TOK + (sub + 1) * SUB)
        c_q = cosine[window_rows, :]
        s_q = sine[window_rows, :]
        other = jnp.where(row_f == id_rows[2 * REACH + sub], 0.0, -1e30).astype(jnp.bfloat16)
        for h in range(HEADS):
            at = (h // 2) * 512 + sub * 256 + (h % 2) * SUB
            lanes = slice(at % 512, at % 512 + SUB)
            normed = xh_ref[at : at + SUB, :] * q_gain
            hat = normed * c_q + half_turned(normed) * s_q
            qhat[at : at + SUB, :] = hat.astype(jnp.bfloat16)
            qext_t[h // 2, 0:HEAD, lanes] = hat.T.astype(jnp.bfloat16)
            qext_t[h // 2, HEAD:, lanes] = other

    dk[...] = jnp.zeros_like(dk)
    dv[...] = jnp.zeros_like(dv)
    qg_acc[...] = jnp.zeros_like(qg_acc)
    zero = jnp.zeros((SUB, 256), jnp.bfloat16)
    for ref in (w_ref, ds_ref):
        for slot in range(2):
            ref[slot, 0:SUB, 256:512] = zero
            ref[slot, SPAN:WINDOW, 0:256] = zero
    later = jnp.where(row <= lane, 0.0, -1e30)
    later = jnp.concatenate([later, later], axis=1)
    last = SPAN - SUB
    spans = (slice(0, SPAN), slice(SUB, WINDOW))
    columns_of = (slice(0, 256), slice(256, 512))

    def copies(pair):
        columns = slice(pair * 256, (pair + 1) * 256)
        return (
            pltpu.make_async_copy(att_ref.at[:, columns], att_hbm.at[:, columns], att_sem.at[pair]),
            pltpu.make_async_copy(gq_ref.at[:, columns], gq_hbm.at[:, columns], gq_sem.at[pair]),
        )

    def key_terms(pair, slot):
        rows = slice(pair * 512, (pair + 1) * 512)
        dk[...] += dot(ds_ref[slot], qhat[rows, :])
        dv[...] += dot(w_ref[slot], dcat[rows, :])

    for pair in range(HEADS // 2):
        slot = pair % 2

        def scores(sub):
            s = dot(kext[spans[sub], :], qext_t[pair, :, columns_of[sub]])
            tail = s[last:] + later
            s_ref[sub, 0:last, :] = s[:last]
            s_ref[sub, last:, :] = tail
            top = jnp.maximum(
                jnp.max(s[:last].reshape(last // 8, 8, 256), axis=0),
                jnp.max(tail.reshape(SUB // 8, 8, 256), axis=0),
            )
            return jnp.max(top, axis=0, keepdims=True) * EXP2

        def exponents(sub, shift):
            total = jnp.zeros((8, 256), jnp.float32)
            for c in range(CHUNKS):
                e = jnp.exp2(s_ref[sub, c * SUB : (c + 1) * SUB, :] * EXP2 - shift)
                s_ref[sub, c * SUB : (c + 1) * SUB, :] = e
                total = total + jnp.sum(e.reshape(SUB // 8, 8, 256), axis=0)
            return 1.0 / jnp.sum(total, axis=0, keepdims=True)

        def weigh(sub, inverse):
            for c in range(CHUNKS):
                keys = slice((sub + c) * SUB, (sub + c + 1) * SUB)
                w = s_ref[sub, c * SUB : (c + 1) * SUB, :] * inverse
                w_ref[slot, keys, columns_of[sub]] = w.astype(jnp.bfloat16)

        def attend(sub):
            att_t = dot(v_t[:, spans[sub]], w_ref[slot, spans[sub], columns_of[sub]])
            d_t = dcat_t[pair, :, columns_of[sub]]
            center = jnp.sum(att_t * d_t.astype(jnp.float32), axis=0, keepdims=True)
            tokens = slice(sub * SUB, (sub + 1) * SUB)
            for g in range(2):
                columns = slice(pair * 256 + g * HEAD, pair * 256 + (g + 1) * HEAD)
                att_ref[tokens, columns] = att_t[:, g * SUB : (g + 1) * SUB].T.astype(jnp.bfloat16)
            return center

        def score_terms(sub, center):
            dw = dot(vwin[spans[sub], :], dcat_t[pair, :, columns_of[sub]])
            w = w_ref[slot, spans[sub], columns_of[sub]].astype(jnp.float32)
            ds_ref[slot, spans[sub], columns_of[sub]] = (w * (dw - center)).astype(jnp.bfloat16)

        def query_terms(sub):
            dq_t = dot(khat_t[:, spans[sub]], ds_ref[slot, spans[sub], columns_of[sub]]) * SCALING
            tokens = slice(sub * SUB, (sub + 1) * SUB)
            window_rows = slice(REACH * TOK + sub * SUB, REACH * TOK + (sub + 1) * SUB)
            c_q = cosine[window_rows, :]
            s_q = sine[window_rows, :]
            for g in range(2):
                columns = slice(pair * 256 + g * HEAD, pair * 256 + (g + 1) * HEAD)
                at = pair * 512 + sub * 256 + g * SUB
                rows = slice(at, at + SUB)
                dq = dq_t[:, g * SUB : (g + 1) * SUB].T
                xh = xh_ref[rows, :]
                dn = dq * c_q - half_turned(dq) * s_q
                qg_acc[...] += jnp.sum((dn * xh).reshape(SUB // 8, 8, HEAD), axis=0)
                dxh = dn * q_gain
                gq = scale_ref[rows, :] * (dxh - xh * jnp.mean(dxh * xh, axis=1, keepdims=True))
                gq_ref[tokens, columns] = gq.astype(jnp.bfloat16)

        shift_0 = scores(0)
        shift_1 = scores(1)
        inverse_0 = exponents(0, shift_0)
        if pair > 0:
            key_terms(pair - 1, 1 - slot)
        weigh(0, inverse_0)
        inverse_1 = exponents(1, shift_1)
        center_0 = attend(0)
        score_terms(0, center_0)
        weigh(1, inverse_1)
        query_terms(0)
        center_1 = attend(1)
        score_terms(1, center_1)
        query_terms(1)
        for copy in copies(pair):
            copy.start()

    key_terms(HEADS // 2 - 1, 1)

    kg = jnp.zeros((8, HEAD), jnp.float32)
    outs = (r4, r3, r2, r1, own_ref)
    for j in range(parts):
        rows = slice(j * SUB, (j + 1) * SUB)
        here = slice((j % 2) * SUB, (j % 2 + 1) * SUB)
        x = blocks[j // 2][here, :].astype(jnp.float32)
        r = lax.rsqrt(jnp.mean(x * x, axis=1, keepdims=True) + EPSILON)
        xh = x * r
        d = dk[rows, :] * SCALING
        dn = d * cosine[rows, :] - half_turned(d) * sine[rows, :]
        kg = kg + jnp.sum((dn * xh).reshape(SUB // 8, 8, HEAD), axis=0)
        dxh = dn * k_gain
        gk = r * (dxh - xh * jnp.mean(dxh * xh, axis=1, keepdims=True))
        out = outs[j // 2]
        out[here, :] = gk.astype(out.dtype)
        out[TOK + (j % 2) * SUB : TOK + (j % 2 + 1) * SUB, :] = dv[rows, :].astype(out.dtype)
    gains = jnp.concatenate(
        [jnp.sum(qg_acc[...], axis=0, keepdims=True), jnp.sum(kg, axis=0, keepdims=True)]
    )
    gain_ref[...] = gains
    for pair in range(HEADS // 2):
        for copy in copies(pair):
            copy.wait()


RETURN = jnp.bfloat16


def attention(blocks, prepared, frequency):
    vmem = pl.BlockSpec(memory_space=pltpu.VMEM)
    hbm = pl.BlockSpec(memory_space=pl.ANY)
    f32, bf16 = jnp.float32, jnp.bfloat16
    shape = jax.ShapeDtypeStruct
    return pl.pallas_call(
        kernel,
        out_shape=[
            shape((TOK, HEADS * HEAD), bf16),
            shape((TOK, HEADS * HEAD), bf16),
            *[shape((2 * TOK, HEAD), RETURN) for _ in range(REACH)],
            shape((2 * TOK, HEAD), f32),
            shape((2, HEAD), f32),
        ],
        in_specs=[vmem] * 12,
        out_specs=[hbm] * 2 + [vmem] * 6,
        scratch_shapes=[
            pltpu.VMEM((TOK, HEADS * HEAD), bf16),
            pltpu.VMEM((TOK, HEADS * HEAD), bf16),
            pltpu.VMEM((WINDOW, HEAD), f32),
            pltpu.VMEM((WINDOW, HEAD), f32),
            pltpu.VMEM((WINDOW, 2 * HEAD), bf16),
            pltpu.VMEM((WINDOW, HEAD), bf16),
            pltpu.VMEM((HEAD, WINDOW), bf16),
            pltpu.VMEM((HEAD, WINDOW), bf16),
            pltpu.VMEM((HEADS * TOK, HEAD), bf16),
            pltpu.VMEM((HEADS // 2, 2 * HEAD, 512), bf16),
            pltpu.VMEM((2, SPAN, 256), f32),
            pltpu.VMEM((2, WINDOW, 512), bf16),
            pltpu.VMEM((2, WINDOW, 512), bf16),
            pltpu.VMEM((WINDOW, HEAD), f32),
            pltpu.VMEM((WINDOW, HEAD), f32),
            pltpu.VMEM((8, HEAD), f32),
            pltpu.VMEM((MSG, HEAD), bf16),
            pltpu.VMEM((MSG, HEAD), bf16),
            pltpu.SemaphoreType.DMA((HEADS // 2,)),
            pltpu.SemaphoreType.DMA((HEADS // 2,)),
        ],
        compiler_params=pltpu.CompilerParams(vmem_limit_bytes=40 * 1024 * 1024),
    )(*blocks, *prepared, frequency)


def pack_kernel(keys, values, ids, out):
    out[0:TOK, :] = keys[...]
    out[TOK : 2 * TOK, :] = values[...]
    marked = (ids[...] + 1).astype(jnp.float32)
    out[2 * TOK :, :] = jnp.concatenate(
        [marked, jnp.zeros((ID_ROWS - 2, HEAD), jnp.float32)]
    ).astype(jnp.bfloat16)


def pack(keys, values, ids):
    vmem = pl.BlockSpec(memory_space=pltpu.VMEM)
    return pl.pallas_call(
        pack_kernel,
        out_shape=jax.ShapeDtypeStruct((MSG, HEAD), jnp.bfloat16),
        in_specs=[vmem] * 3,
        out_specs=vmem,
    )(keys, values, ids)


def swapped(block, ways=(0, 1)):
    route = [(i, i ^ 1) for i in range(lax.axis_size("context")) if i % 2 in ways]
    return lax.ppermute(block, "context", route)


def summed_over_all(terms):
    axes = ("context", "tensor")
    copies = jnp.broadcast_to(terms, (lax.axis_size(axes),) + terms.shape)
    return jnp.sum(lax.all_to_all(copies, axes, 0, 0), axis=0)


def body(queries, keys, values, output_gradient, q_gain, k_gain, doc_ids):
    message = pack(keys, values, doc_ids.reshape(2, HEAD))
    two = passed_along(message, "context", 2)
    first_swap = swapped(message, (0,))
    four = passed_along(message, "context", 4)
    prepared = prepare(queries, output_gradient, q_gain.reshape(1, HEAD), k_gain.reshape(1, HEAD))
    two, *prepared = lax.optimization_barrier((two, *prepared))
    middle_swap = swapped(two)
    last_swap = swapped(four, (1,))
    blocks = [four, two, message, first_swap, middle_swap, last_swap]
    half = jnp.arange(HEAD // 2, dtype=jnp.float32)
    frequency = THETA ** (-(half * 2.0 / HEAD))
    frequency = jnp.concatenate([frequency, frequency]).reshape(1, HEAD)
    attended, query_gradient, *returns, own, gains = attention(
        blocks,
        prepared,
        frequency,
    )
    total = own
    for distance, block in zip(range(REACH, 0, -1), returns):
        total = total + passed_along(block, "context", -distance)
    total = total.astype(jnp.bfloat16)
    gain_total = summed_over_all(gains)
    return (
        attended,
        query_gradient,
        total[:TOK],
        total[TOK:],
        gain_total[0],
        gain_total[1],
    )


def solution(mesh):
    placed = (
        P("context", "tensor"),
        P("context", "tensor"),
        P("context", "tensor"),
        P("context", "tensor"),
        P(),
        P(),
        P("context"),
    )
    return jax.shard_map(
        body,
        mesh=mesh,
        in_specs=placed,
        out_specs=(
            P("context", "tensor"),
            P("context", "tensor"),
            P("context", "tensor"),
            P("context", "tensor"),
            P(),
            P(),
        ),
        check_vma=False,
    )
```

```python
import jax
import jax.numpy as jnp
import numpy as np
from jax import lax
from jax.experimental import pallas as pl
from jax.experimental.pallas import tpu as pltpu
from jax.sharding import PartitionSpec as P

REACH = 4
THETA = 500000.0
EPSILON = 1e-06
TOK = 256
HEAD = 128
HEADS = 8
WINDOW = (REACH + 1) * TOK
SUB = 128
SPAN = 1152
CHUNKS = SPAN // SUB
WIDE = 384
ID_ROWS = 16
MSG = 2 * TOK + ID_ROWS
SCALING = HEAD ** (-0.5)
EXP2 = float(SCALING * np.log2(np.e))

PIO2_A = 1.5703125
PIO2_B = float(np.float32(np.round((np.pi / 2 - PIO2_A) * 2.0**23) / 2.0**23))
PIO2_C = float(np.float32(np.pi / 2 - PIO2_A - PIO2_B))


def passed_along(block, axis, distance):
    devices = range(lax.axis_size(axis))
    route = [(i - distance, i) for i in devices if i - distance in devices]
    return lax.ppermute(block, axis, route)


def dot(a, b):
    return jnp.dot(a, b, preferred_element_type=jnp.float32)


def half_turned(x):
    return pltpu.roll(x, HEAD // 2, 1)


def cos_sin(position, frequency):
    angle = position * frequency
    turns = jnp.floor(angle * np.float32(2.0 / np.pi) + 0.5)
    rest = ((angle - turns * PIO2_A) - turns * PIO2_B) - turns * PIO2_C
    square = rest * rest
    sine = rest + rest * square * (
        np.float32(-1.6666654611e-1)
        + square * (np.float32(8.3321608736e-3) + square * np.float32(-1.9515295891e-4))
    )
    cosine = (1.0 - 0.5 * square) + square * square * (
        np.float32(4.166664568298827e-2)
        + square * (np.float32(-1.388731625493765e-3) + square * np.float32(2.443315711809948e-5))
    )
    lane = lax.broadcasted_iota(jnp.int32, angle.shape, 1)
    quadrant = turns.astype(jnp.int32) + jnp.where(lane < HEAD // 2, 1, 0)
    value = jnp.where((quadrant & 1) == 1, cosine, sine)
    return jnp.where((quadrant & 2) == 2, -value, value)


def prepare_kernel(q_ref, d_ref, qg_ref, kg_ref, xh_ref, scale_ref, dcat, dcat_t, gains):
    gains[0:1, :] = qg_ref[...]
    gains[1:2, :] = kg_ref[...]
    for sub in range(2):
        tokens = slice(sub * SUB, (sub + 1) * SUB)
        for h in range(HEADS):
            at = (h // 2) * 512 + sub * 256 + (h % 2) * SUB
            rows = slice(at, at + SUB)
            x = q_ref[tokens, h * HEAD : (h + 1) * HEAD].astype(jnp.float32)
            r = lax.rsqrt(jnp.mean(x * x, axis=1, keepdims=True) + EPSILON)
            xh_ref[rows, :] = x * r
            scale_ref[rows, :] = jnp.broadcast_to(r, (SUB, HEAD))
            d = d_ref[tokens, h * HEAD : (h + 1) * HEAD]
            dcat[rows, :] = d
            dcat_t[h // 2, :, at % 512 : at % 512 + SUB] = d.astype(jnp.float32).T.astype(jnp.bfloat16)


def prepare(queries, output_gradient, q_gain, k_gain):
    vmem = pl.BlockSpec(memory_space=pltpu.VMEM)
    f32, bf16 = jnp.float32, jnp.bfloat16
    shape = jax.ShapeDtypeStruct
    return pl.pallas_call(
        prepare_kernel,
        out_shape=[
            shape((HEADS * TOK, HEAD), f32),
            shape((HEADS * TOK, HEAD), f32),
            shape((HEADS * TOK, HEAD), bf16),
            shape((HEADS // 2, HEAD, 512), bf16),
            shape((2, HEAD), f32),
        ],
        in_specs=[vmem] * 4,
        out_specs=[vmem] * 5,
        compiler_params=pltpu.CompilerParams(vmem_limit_bytes=16 * 1024 * 1024),
        cost_estimate=pl.CostEstimate(flops=10**9, bytes_accessed=4 * 2**20, transcendentals=0),
    )(queries, output_gradient, q_gain, k_gain)


def kernel(
    b4, b2, b0, first_swap, middle_swap, last_swap, xh_ref, scale_ref, dcat, dcat_t, gains_ref, f_ref,
    att_hbm, gq_hbm, four_ref, two_ref, own_ref, swap_ref, gain_ref,
    att_ref, gq_ref, cosine, sine, kext, vwin, khat_t, v_t, qhat, qext_t,
    s_ref, w_ref, ds_ref, dk, dv, qg_acc, b3, b1, att_sem, gq_sem,
):
    even = lax.rem(lax.axis_index("context"), 2) == 0

    @pl.when(even)
    def _():
        b3[...] = last_swap[...]
        b1[...] = middle_swap[...]

    @pl.when(jnp.logical_not(even))
    def _():
        b3[...] = middle_swap[...]
        b1[...] = first_swap[...]

    blocks = (b4, b3, b2, b1, b0)
    lane = lax.broadcasted_iota(jnp.int32, (SUB, HEAD), 1)
    row = lax.broadcasted_iota(jnp.int32, (SUB, HEAD), 0)
    lane_f = lane.astype(jnp.float32)
    row_f = row.astype(jnp.float32)
    left = lane < HEAD // 2
    parts = WINDOW // SUB
    q_gain = gains_ref[0:1, :]
    k_gain = gains_ref[1:2, :]
    frequency = f_ref[...]

    id_rows = []
    for block in blocks:
        both = block[2 * TOK : MSG, :].astype(jnp.float32)
        id_rows += [both[0:1], both[1:2]]
    below = jnp.zeros((SUB, HEAD), jnp.float32)
    for j in range(parts):
        column = jnp.broadcast_to(id_rows[j], (SUB, HEAD)).T
        kext[j * SUB : (j + 1) * SUB, HEAD:] = jnp.where(column == lane_f, 1.0, 0.0).astype(jnp.bfloat16)
        below = below + jnp.where(column < lane_f, 1.0, 0.0)
    first = jnp.sum(below, axis=0, keepdims=True)

    for j in range(parts):
        rows = slice(j * SUB, (j + 1) * SUB)
        here = slice((j % 2) * SUB, (j % 2 + 1) * SUB)
        block = blocks[j // 2]
        member = kext[rows, HEAD:].astype(jnp.float32)
        start = jnp.sum(member * first, axis=1, keepdims=True)
        position = (row + j * SUB).astype(jnp.float32) - start
        both = cos_sin(position, frequency)
        turned = half_turned(both)
        c = jnp.where(left, both, turned)
        s = jnp.where(left, -turned, both)
        cosine[rows, :] = c
        sine[rows, :] = s
        x = block[here, :].astype(jnp.float32)
        normed = x * lax.rsqrt(jnp.mean(x * x, axis=1, keepdims=True) + EPSILON) * k_gain
        hat = normed * c + half_turned(normed) * s
        kext[rows, 0:HEAD] = hat.astype(jnp.bfloat16)
        khat_t[:, rows] = hat.T.astype(jnp.bfloat16)
        values = block[TOK + (j % 2) * SUB : TOK + (j % 2 + 1) * SUB, :]
        vwin[rows, :] = values
        v_t[:, rows] = values.astype(jnp.float32).T.astype(jnp.bfloat16)

    for sub in range(2):
        window_rows = slice(REACH * TOK + sub * SUB, REACH * TOK + (sub + 1) * SUB)
        c_q = cosine[window_rows, :]
        s_q = sine[window_rows, :]
        other = jnp.where(row_f == id_rows[2 * REACH + sub], 0.0, -1e30).astype(jnp.bfloat16)
        for h in range(HEADS):
            at = (h // 2) * 512 + sub * 256 + (h % 2) * SUB
            lanes = slice(at % 512, at % 512 + SUB)
            normed = xh_ref[at : at + SUB, :] * q_gain
            hat = normed * c_q + half_turned(normed) * s_q
            qhat[at : at + SUB, :] = hat.astype(jnp.bfloat16)
            qext_t[h // 2, 0:HEAD, lanes] = hat.T.astype(jnp.bfloat16)
            qext_t[h // 2, HEAD:, lanes] = other

    dk[...] = jnp.zeros_like(dk)
    dv[...] = jnp.zeros_like(dv)
    qg_acc[...] = jnp.zeros_like(qg_acc)
    zero = jnp.zeros((SUB, 256), jnp.bfloat16)
    for ref in (w_ref, ds_ref):
        for slot in range(2):
            ref[slot, 0:SUB, 256:512] = zero
            ref[slot, SPAN:WINDOW, 0:256] = zero
    later = jnp.where(row <= lane, 0.0, -1e30)
    later = jnp.concatenate([later, later], axis=1)
    spans = (slice(0, SPAN), slice(SUB, WINDOW))
    columns_of = (slice(0, 256), slice(256, 512))

    def copies(pair):
        columns = slice(pair * 256, (pair + 1) * 256)
        return (
            pltpu.make_async_copy(att_ref.at[:, columns], att_hbm.at[:, columns], att_sem.at[pair]),
            pltpu.make_async_copy(gq_ref.at[:, columns], gq_hbm.at[:, columns], gq_sem.at[pair]),
        )

    def key_terms(pair, slot):
        rows = slice(pair * 512, (pair + 1) * 512)
        dk[...] += dot(ds_ref[slot], qhat[rows, :])
        dv[...] += dot(w_ref[slot], dcat[rows, :])

    for pair in range(HEADS // 2):
        slot = pair % 2

        def scores(sub):
            q = qext_t[pair, :, columns_of[sub]]
            top = jnp.full((8, 256), -1e30, jnp.float32)
            for start in range(0, SPAN, WIDE):
                s = dot(kext[sub * SUB + start : sub * SUB + start + WIDE, :], q)
                if start + WIDE == SPAN:
                    s = jnp.concatenate([s[: WIDE - SUB], s[WIDE - SUB :] + later])
                s_ref[slot, sub, start : start + WIDE, :] = s
                top = jnp.maximum(top, jnp.max(s.reshape(WIDE // 8, 8, 256), axis=0))
            return jnp.max(top, axis=0, keepdims=True) * EXP2

        def exponents(sub, shift):
            total = jnp.zeros((8, 256), jnp.float32)
            for c in range(CHUNKS):
                e = jnp.exp2(s_ref[slot, sub, c * SUB : (c + 1) * SUB, :] * EXP2 - shift)
                s_ref[slot, sub, c * SUB : (c + 1) * SUB, :] = e
                total = total + jnp.sum(e.reshape(SUB // 8, 8, 256), axis=0)
            return 1.0 / jnp.sum(total, axis=0, keepdims=True)

        def weigh(sub, inverse):
            for c in range(CHUNKS):
                keys = slice((sub + c) * SUB, (sub + c + 1) * SUB)
                w = s_ref[slot, sub, c * SUB : (c + 1) * SUB, :] * inverse
                w_ref[slot, keys, columns_of[sub]] = w.astype(jnp.bfloat16)

        def attend(sub):
            att_t = dot(v_t[:, spans[sub]], w_ref[slot, spans[sub], columns_of[sub]])
            d_t = dcat_t[pair, :, columns_of[sub]]
            center = jnp.sum(att_t * d_t.astype(jnp.float32), axis=0, keepdims=True)
            tokens = slice(sub * SUB, (sub + 1) * SUB)
            for g in range(2):
                columns = slice(pair * 256 + g * HEAD, pair * 256 + (g + 1) * HEAD)
                att_ref[tokens, columns] = att_t[:, g * SUB : (g + 1) * SUB].T.astype(jnp.bfloat16)
            return center

        def score_terms(sub, center):
            d_t = dcat_t[pair, :, columns_of[sub]]
            for start in range(0, SPAN, WIDE):
                keys = slice(sub * SUB + start, sub * SUB + start + WIDE)
                dw = dot(vwin[keys, :], d_t)
                w = w_ref[slot, keys, columns_of[sub]].astype(jnp.float32)
                ds_ref[slot, keys, columns_of[sub]] = (w * (dw - center)).astype(jnp.bfloat16)

        def query_terms(sub):
            dq_t = dot(khat_t[:, spans[sub]], ds_ref[slot, spans[sub], columns_of[sub]]) * SCALING
            tokens = slice(sub * SUB, (sub + 1) * SUB)
            window_rows = slice(REACH * TOK + sub * SUB, REACH * TOK + (sub + 1) * SUB)
            c_q = cosine[window_rows, :]
            s_q = sine[window_rows, :]
            for g in range(2):
                columns = slice(pair * 256 + g * HEAD, pair * 256 + (g + 1) * HEAD)
                at = pair * 512 + sub * 256 + g * SUB
                rows = slice(at, at + SUB)
                dq = dq_t[:, g * SUB : (g + 1) * SUB].T
                xh = xh_ref[rows, :]
                dn = dq * c_q - half_turned(dq) * s_q
                qg_acc[...] += jnp.sum((dn * xh).reshape(SUB // 8, 8, HEAD), axis=0)
                dxh = dn * q_gain
                gq = scale_ref[rows, :] * (dxh - xh * jnp.mean(dxh * xh, axis=1, keepdims=True))
                gq_ref[tokens, columns] = gq.astype(jnp.bfloat16)

        shift_0 = scores(0)
        shift_1 = scores(1)
        inverse_0 = exponents(0, shift_0)
        if pair > 0:
            key_terms(pair - 1, 1 - slot)
        weigh(0, inverse_0)
        inverse_1 = exponents(1, shift_1)
        center_0 = attend(0)
        score_terms(0, center_0)
        weigh(1, inverse_1)
        query_terms(0)
        center_1 = attend(1)
        score_terms(1, center_1)
        query_terms(1)
        for copy in copies(pair):
            copy.start()

    key_terms(HEADS // 2 - 1, 1)

    kg = jnp.zeros((8, HEAD), jnp.float32)
    outs = ((four_ref, 0), (swap_ref, 2 * TOK), (two_ref, 0), (swap_ref, 0), (own_ref, 0))
    for j in range(parts):
        rows = slice(j * SUB, (j + 1) * SUB)
        here = slice((j % 2) * SUB, (j % 2 + 1) * SUB)
        x = blocks[j // 2][here, :].astype(jnp.float32)
        r = lax.rsqrt(jnp.mean(x * x, axis=1, keepdims=True) + EPSILON)
        xh = x * r
        d = dk[rows, :] * SCALING
        dn = d * cosine[rows, :] - half_turned(d) * sine[rows, :]
        kg = kg + jnp.sum((dn * xh).reshape(SUB // 8, 8, HEAD), axis=0)
        dxh = dn * k_gain
        gk = r * (dxh - xh * jnp.mean(dxh * xh, axis=1, keepdims=True))
        out, at = outs[j // 2]
        at = at + (j % 2) * SUB
        out[at : at + SUB, :] = gk.astype(out.dtype)
        out[at + TOK : at + TOK + SUB, :] = dv[rows, :].astype(out.dtype)
    gains = jnp.concatenate(
        [jnp.sum(qg_acc[...], axis=0, keepdims=True), jnp.sum(kg, axis=0, keepdims=True)]
    )
    gain_ref[...] = gains
    high = gains.astype(jnp.bfloat16).astype(jnp.float32)
    middle = (gains - high).astype(jnp.bfloat16).astype(jnp.float32)
    low = gains - high - middle
    swap_ref[4 * TOK :, :] = jnp.concatenate(
        [high, middle, low, jnp.zeros((ID_ROWS - 6, HEAD), jnp.float32)]
    ).astype(jnp.bfloat16)
    for pair in range(HEADS // 2):
        for copy in copies(pair):
            copy.wait()


def attention(blocks, prepared, frequency):
    vmem = pl.BlockSpec(memory_space=pltpu.VMEM)
    hbm = pl.BlockSpec(memory_space=pl.ANY)
    f32, bf16 = jnp.float32, jnp.bfloat16
    shape = jax.ShapeDtypeStruct
    return pl.pallas_call(
        kernel,
        out_shape=[
            shape((TOK, HEADS * HEAD), bf16),
            shape((TOK, HEADS * HEAD), bf16),
            shape((2 * TOK, HEAD), f32),
            shape((2 * TOK, HEAD), f32),
            shape((2 * TOK, HEAD), f32),
            shape((4 * TOK + ID_ROWS, HEAD), bf16),
            shape((2, HEAD), f32),
        ],
        in_specs=[vmem] * 12,
        out_specs=[hbm] * 2 + [vmem] * 5,
        scratch_shapes=[
            pltpu.VMEM((TOK, HEADS * HEAD), bf16),
            pltpu.VMEM((TOK, HEADS * HEAD), bf16),
            pltpu.VMEM((WINDOW, HEAD), f32),
            pltpu.VMEM((WINDOW, HEAD), f32),
            pltpu.VMEM((WINDOW, 2 * HEAD), bf16),
            pltpu.VMEM((WINDOW, HEAD), bf16),
            pltpu.VMEM((HEAD, WINDOW), bf16),
            pltpu.VMEM((HEAD, WINDOW), bf16),
            pltpu.VMEM((HEADS * TOK, HEAD), bf16),
            pltpu.VMEM((HEADS // 2, 2 * HEAD, 512), bf16),
            pltpu.VMEM((2, 2, SPAN, 256), f32),
            pltpu.VMEM((2, WINDOW, 512), bf16),
            pltpu.VMEM((2, WINDOW, 512), bf16),
            pltpu.VMEM((WINDOW, HEAD), f32),
            pltpu.VMEM((WINDOW, HEAD), f32),
            pltpu.VMEM((8, HEAD), f32),
            pltpu.VMEM((MSG, HEAD), bf16),
            pltpu.VMEM((MSG, HEAD), bf16),
            pltpu.SemaphoreType.DMA((HEADS // 2,)),
            pltpu.SemaphoreType.DMA((HEADS // 2,)),
        ],
        compiler_params=pltpu.CompilerParams(vmem_limit_bytes=40 * 1024 * 1024),
    )(*blocks, *prepared, frequency)


def pack_kernel(keys, values, ids, out):
    out[0:TOK, :] = keys[...]
    out[TOK : 2 * TOK, :] = values[...]
    marked = (ids[...] + 1).astype(jnp.float32)
    out[2 * TOK :, :] = jnp.concatenate(
        [marked, jnp.zeros((ID_ROWS - 2, HEAD), jnp.float32)]
    ).astype(jnp.bfloat16)


def pack(keys, values, ids):
    vmem = pl.BlockSpec(memory_space=pltpu.VMEM)
    return pl.pallas_call(
        pack_kernel,
        out_shape=jax.ShapeDtypeStruct((MSG, HEAD), jnp.bfloat16),
        in_specs=[vmem] * 3,
        out_specs=vmem,
    )(keys, values, ids)


def swapped(block, ways=(0, 1)):
    route = [(i, i ^ 1) for i in range(lax.axis_size("context")) if i % 2 in ways]
    return lax.ppermute(block, "context", route)


def chip_kernel(swap, four, two, own, gains, four_out, two_out, own_out, gains_out):
    even = lax.rem(lax.axis_index("context"), 2) == 0
    one, three = slice(0, 2 * TOK), slice(2 * TOK, 4 * TOK)

    @pl.when(even)
    def _():
        four_out[...] = four[...].astype(jnp.bfloat16)
        two_out[...] = (two[...] + swap[three, :].astype(jnp.float32)).astype(jnp.bfloat16)
        own_out[...] = own[...] + swap[one, :].astype(jnp.float32)

    @pl.when(jnp.logical_not(even))
    def _():
        four_out[...] = (four[...] + swap[three, :].astype(jnp.float32)).astype(jnp.bfloat16)
        two_out[...] = (two[...] + swap[one, :].astype(jnp.float32)).astype(jnp.bfloat16)
        own_out[...] = own[...]

    split = swap[4 * TOK :, :].astype(jnp.float32)
    gains_out[...] = gains[...] + ((split[0:2] + split[2:4]) + split[4:6])


def chip_terms(swap, four, two, own, gains):
    vmem = pl.BlockSpec(memory_space=pltpu.VMEM)
    shape = jax.ShapeDtypeStruct
    return pl.pallas_call(
        chip_kernel,
        out_shape=[
            shape((2 * TOK, HEAD), jnp.bfloat16),
            shape((2 * TOK, HEAD), jnp.bfloat16),
            shape((2 * TOK, HEAD), jnp.float32),
            shape((2, HEAD), jnp.float32),
        ],
        in_specs=[vmem] * 5,
        out_specs=[vmem] * 4,
        compiler_params=pltpu.CompilerParams(vmem_limit_bytes=16 * 1024 * 1024),
    )(swap, four, two, own, gains)


def added(terms, axis, bit):
    route = [(i, i ^ bit) for i in range(lax.axis_size(axis))]
    return terms + lax.ppermute(terms, axis, route)


def body(queries, keys, values, output_gradient, q_gain, k_gain, doc_ids):
    message = pack(keys, values, doc_ids.reshape(2, HEAD))
    two = passed_along(message, "context", 2)
    first_swap = swapped(message, (0,))
    four = passed_along(message, "context", 4)
    prepared = prepare(queries, output_gradient, q_gain.reshape(1, HEAD), k_gain.reshape(1, HEAD))
    two, *prepared = lax.optimization_barrier((two, *prepared))
    middle_swap = swapped(two)
    last_swap = swapped(four, (1,))
    blocks = [four, two, message, first_swap, middle_swap, last_swap]
    half = jnp.arange(HEAD // 2, dtype=jnp.float32)
    frequency = THETA ** (-(half * 2.0 / HEAD))
    frequency = jnp.concatenate([frequency, frequency]).reshape(1, HEAD)
    attended, query_gradient, four, two, own, swap, gains = attention(blocks, prepared, frequency)
    four, two, own, gains = chip_terms(swapped(swap), four, two, own, gains)
    four = passed_along(four, "context", -4)
    for bit in (1, 2, 4):
        gains = added(gains, "tensor", bit)
    four, two, gains = lax.optimization_barrier((four, two, gains))
    two = passed_along(two, "context", -2)
    for bit in (8, 16, 2):
        gains = added(gains, "context", bit)
    two, gains = lax.optimization_barrier((two, gains))
    gains = added(gains, "context", 4)
    keys, values = slice(0, TOK), slice(TOK, 2 * TOK)
    return (
        attended,
        query_gradient,
        ((own[keys] + two[keys]) + four[keys]).astype(jnp.bfloat16),
        ((own[values] + two[values]) + four[values]).astype(jnp.bfloat16),
        gains[0],
        gains[1],
    )


def solution(mesh):
    placed = (
        P("context", "tensor"),
        P("context", "tensor"),
        P("context", "tensor"),
        P("context", "tensor"),
        P(),
        P(),
        P("context"),
    )
    return jax.shard_map(
        body,
        mesh=mesh,
        in_specs=placed,
        out_specs=(
            P("context", "tensor"),
            P("context", "tensor"),
            P("context", "tensor"),
            P("context", "tensor"),
            P(),
            P(),
        ),
        check_vma=False,
    )
```

```python
import jax
import jax.numpy as jnp
import numpy as np
from jax import lax
from jax.experimental import pallas as pl
from jax.experimental.pallas import tpu as pltpu
from jax.sharding import PartitionSpec as P

REACH = 4
THETA = 500000.0
EPSILON = 1e-06
TOK = 256
HEAD = 128
HEADS = 8
WINDOW = (REACH + 1) * TOK
SUB = 128
SPAN = 1152
CHUNKS = SPAN // SUB
WIDE = 384
ID_ROWS = 16
MSG = 2 * TOK + ID_ROWS
SCALING = HEAD ** (-0.5)
EXP2 = float(SCALING * np.log2(np.e))

PIO2_A = 1.5703125
PIO2_B = float(np.float32(np.round((np.pi / 2 - PIO2_A) * 2.0**23) / 2.0**23))
PIO2_C = float(np.float32(np.pi / 2 - PIO2_A - PIO2_B))


def passed_along(block, axis, distance):
    devices = range(lax.axis_size(axis))
    route = [(i - distance, i) for i in devices if i - distance in devices]
    return lax.ppermute(block, axis, route)


def dot(a, b):
    return jnp.dot(a, b, preferred_element_type=jnp.float32)


def half_turned(x):
    return pltpu.roll(x, HEAD // 2, 1)


def cos_sin(position, frequency):
    angle = position * frequency
    turns = jnp.floor(angle * np.float32(2.0 / np.pi) + 0.5)
    rest = ((angle - turns * PIO2_A) - turns * PIO2_B) - turns * PIO2_C
    square = rest * rest
    sine = rest + rest * square * (
        np.float32(-1.6666654611e-1)
        + square * (np.float32(8.3321608736e-3) + square * np.float32(-1.9515295891e-4))
    )
    cosine = (1.0 - 0.5 * square) + square * square * (
        np.float32(4.166664568298827e-2)
        + square * (np.float32(-1.388731625493765e-3) + square * np.float32(2.443315711809948e-5))
    )
    lane = lax.broadcasted_iota(jnp.int32, angle.shape, 1)
    quadrant = turns.astype(jnp.int32) + jnp.where(lane < HEAD // 2, 1, 0)
    value = jnp.where((quadrant & 1) == 1, cosine, sine)
    return jnp.where((quadrant & 2) == 2, -value, value)


def prepare_kernel(q_ref, d_ref, qg_ref, kg_ref, xh_ref, scale_ref, dcat, dcat_t, gains):
    gains[0:1, :] = qg_ref[...]
    gains[1:2, :] = kg_ref[...]
    for sub in range(2):
        tokens = slice(sub * SUB, (sub + 1) * SUB)
        for h in range(HEADS):
            at = (h // 2) * 512 + sub * 256 + (h % 2) * SUB
            rows = slice(at, at + SUB)
            x = q_ref[tokens, h * HEAD : (h + 1) * HEAD].astype(jnp.float32)
            r = lax.rsqrt(jnp.mean(x * x, axis=1, keepdims=True) + EPSILON)
            xh_ref[rows, :] = x * r
            scale_ref[rows, :] = jnp.broadcast_to(r, (SUB, HEAD))
            d = d_ref[tokens, h * HEAD : (h + 1) * HEAD]
            dcat[rows, :] = d
            dcat_t[h // 2, :, at % 512 : at % 512 + SUB] = d.astype(jnp.float32).T.astype(jnp.bfloat16)


def prepare(queries, output_gradient, q_gain, k_gain):
    vmem = pl.BlockSpec(memory_space=pltpu.VMEM)
    f32, bf16 = jnp.float32, jnp.bfloat16
    shape = jax.ShapeDtypeStruct
    return pl.pallas_call(
        prepare_kernel,
        out_shape=[
            shape((HEADS * TOK, HEAD), f32),
            shape((HEADS * TOK, HEAD), f32),
            shape((HEADS * TOK, HEAD), bf16),
            shape((HEADS // 2, HEAD, 512), bf16),
            shape((2, HEAD), f32),
        ],
        in_specs=[vmem] * 4,
        out_specs=[vmem] * 5,
        compiler_params=pltpu.CompilerParams(vmem_limit_bytes=16 * 1024 * 1024),
        cost_estimate=pl.CostEstimate(flops=10**9, bytes_accessed=4 * 2**20, transcendentals=0),
    )(queries, output_gradient, q_gain, k_gain)


def kernel(
    b4, b2, b0, first_swap, middle_swap, last_swap, xh_ref, scale_ref, dcat, dcat_t, gains_ref, f_ref,
    att_hbm, gq_hbm, four_ref, two_ref, own_ref, swap_ref, gain_ref,
    att_ref, gq_ref, cosine, sine, kext, vwin, khat_t, v_t, qhat, qext_t,
    s_ref, w_ref, ds_ref, dk, dv, qg_acc, b3, b1, att_sem, gq_sem,
):
    even = lax.rem(lax.axis_index("context"), 2) == 0

    @pl.when(even)
    def _():
        b3[...] = last_swap[...]
        b1[...] = middle_swap[...]

    @pl.when(jnp.logical_not(even))
    def _():
        b3[...] = middle_swap[...]
        b1[...] = first_swap[...]

    blocks = (b4, b3, b2, b1, b0)
    lane = lax.broadcasted_iota(jnp.int32, (SUB, HEAD), 1)
    row = lax.broadcasted_iota(jnp.int32, (SUB, HEAD), 0)
    lane_f = lane.astype(jnp.float32)
    row_f = row.astype(jnp.float32)
    left = lane < HEAD // 2
    parts = WINDOW // SUB
    q_gain = gains_ref[0:1, :]
    k_gain = gains_ref[1:2, :]
    frequency = f_ref[...]

    id_rows = []
    for block in blocks:
        both = block[2 * TOK : MSG, :].astype(jnp.float32)
        id_rows += [both[0:1], both[1:2]]
    below = jnp.zeros((SUB, HEAD), jnp.float32)
    for j in range(parts):
        column = jnp.broadcast_to(id_rows[j], (SUB, HEAD)).T
        kext[j * SUB : (j + 1) * SUB, HEAD:] = jnp.where(column == lane_f, 1.0, 0.0).astype(jnp.bfloat16)
        below = below + jnp.where(column < lane_f, 1.0, 0.0)
    first = jnp.sum(below, axis=0, keepdims=True)

    for j in range(parts):
        rows = slice(j * SUB, (j + 1) * SUB)
        here = slice((j % 2) * SUB, (j % 2 + 1) * SUB)
        block = blocks[j // 2]
        member = kext[rows, HEAD:].astype(jnp.float32)
        start = jnp.sum(member * first, axis=1, keepdims=True)
        position = (row + j * SUB).astype(jnp.float32) - start
        both = cos_sin(position, frequency)
        turned = half_turned(both)
        c = jnp.where(left, both, turned)
        s = jnp.where(left, -turned, both)
        cosine[rows, :] = c
        sine[rows, :] = s
        x = block[here, :].astype(jnp.float32)
        normed = x * lax.rsqrt(jnp.mean(x * x, axis=1, keepdims=True) + EPSILON) * k_gain
        hat = normed * c + half_turned(normed) * s
        kext[rows, 0:HEAD] = hat.astype(jnp.bfloat16)
        khat_t[:, rows] = hat.T.astype(jnp.bfloat16)
        values = block[TOK + (j % 2) * SUB : TOK + (j % 2 + 1) * SUB, :]
        vwin[rows, :] = values
        v_t[:, rows] = values.astype(jnp.float32).T.astype(jnp.bfloat16)

    for sub in range(2):
        window_rows = slice(REACH * TOK + sub * SUB, REACH * TOK + (sub + 1) * SUB)
        c_q = cosine[window_rows, :]
        s_q = sine[window_rows, :]
        other = jnp.where(row_f == id_rows[2 * REACH + sub], 0.0, -1e30).astype(jnp.bfloat16)
        for h in range(HEADS):
            at = (h // 2) * 512 + sub * 256 + (h % 2) * SUB
            lanes = slice(at % 512, at % 512 + SUB)
            normed = xh_ref[at : at + SUB, :] * q_gain
            hat = normed * c_q + half_turned(normed) * s_q
            qhat[at : at + SUB, :] = hat.astype(jnp.bfloat16)
            qext_t[h // 2, 0:HEAD, lanes] = hat.T.astype(jnp.bfloat16)
            qext_t[h // 2, HEAD:, lanes] = other

    dk[...] = jnp.zeros_like(dk)
    dv[...] = jnp.zeros_like(dv)
    qg_acc[...] = jnp.zeros_like(qg_acc)
    zero = jnp.zeros((SUB, 256), jnp.bfloat16)
    for ref in (w_ref, ds_ref):
        for slot in range(2):
            ref[slot, 0:SUB, 256:512] = zero
            ref[slot, SPAN:WINDOW, 0:256] = zero
    later = jnp.where(row <= lane, 0.0, -1e30)
    later = jnp.concatenate([later, later], axis=1)
    spans = (slice(0, SPAN), slice(SUB, WINDOW))
    columns_of = (slice(0, 256), slice(256, 512))

    def copies(pair):
        columns = slice(pair * 256, (pair + 1) * 256)
        return (
            pltpu.make_async_copy(att_ref.at[:, columns], att_hbm.at[:, columns], att_sem.at[pair]),
            pltpu.make_async_copy(gq_ref.at[:, columns], gq_hbm.at[:, columns], gq_sem.at[pair]),
        )

    def key_terms(pair, slot):
        rows = slice(pair * 512, (pair + 1) * 512)
        dk[...] += dot(ds_ref[slot], qhat[rows, :])
        dv[...] += dot(w_ref[slot], dcat[rows, :])

    for pair in range(HEADS // 2):
        slot = pair % 2

        def scores(sub):
            q = qext_t[pair, :, columns_of[sub]]
            top = jnp.full((8, 256), -1e30, jnp.float32)
            for start in range(0, SPAN, WIDE):
                s = dot(kext[sub * SUB + start : sub * SUB + start + WIDE, :], q)
                if start + WIDE == SPAN:
                    s = jnp.concatenate([s[: WIDE - SUB], s[WIDE - SUB :] + later])
                s_ref[slot, sub, start : start + WIDE, :] = s
                top = jnp.maximum(top, jnp.max(s.reshape(WIDE // 8, 8, 256), axis=0))
            return jnp.max(top, axis=0, keepdims=True) * EXP2

        def exponents(sub, shift):
            total = jnp.zeros((8, 256), jnp.float32)
            for c in range(CHUNKS):
                e = jnp.exp2(s_ref[slot, sub, c * SUB : (c + 1) * SUB, :] * EXP2 - shift)
                s_ref[slot, sub, c * SUB : (c + 1) * SUB, :] = e
                total = total + jnp.sum(e.reshape(SUB // 8, 8, 256), axis=0)
            return 1.0 / jnp.sum(total, axis=0, keepdims=True)

        def weigh(sub, inverse):
            for c in range(CHUNKS):
                keys = slice((sub + c) * SUB, (sub + c + 1) * SUB)
                w = s_ref[slot, sub, c * SUB : (c + 1) * SUB, :] * inverse
                w_ref[slot, keys, columns_of[sub]] = w.astype(jnp.bfloat16)

        def attend(sub):
            att_t = dot(v_t[:, spans[sub]], w_ref[slot, spans[sub], columns_of[sub]])
            d_t = dcat_t[pair, :, columns_of[sub]]
            center = jnp.sum(att_t * d_t.astype(jnp.float32), axis=0, keepdims=True)
            tokens = slice(sub * SUB, (sub + 1) * SUB)
            for g in range(2):
                columns = slice(pair * 256 + g * HEAD, pair * 256 + (g + 1) * HEAD)
                att_ref[tokens, columns] = att_t[:, g * SUB : (g + 1) * SUB].T.astype(jnp.bfloat16)
            return center

        def score_terms(sub, center):
            d_t = dcat_t[pair, :, columns_of[sub]]
            for start in range(0, SPAN, WIDE):
                keys = slice(sub * SUB + start, sub * SUB + start + WIDE)
                dw = dot(vwin[keys, :], d_t)
                w = w_ref[slot, keys, columns_of[sub]].astype(jnp.float32)
                ds_ref[slot, keys, columns_of[sub]] = (w * (dw - center)).astype(jnp.bfloat16)

        def query_terms(sub):
            dq_t = dot(khat_t[:, spans[sub]], ds_ref[slot, spans[sub], columns_of[sub]]) * SCALING
            tokens = slice(sub * SUB, (sub + 1) * SUB)
            window_rows = slice(REACH * TOK + sub * SUB, REACH * TOK + (sub + 1) * SUB)
            c_q = cosine[window_rows, :]
            s_q = sine[window_rows, :]
            for g in range(2):
                columns = slice(pair * 256 + g * HEAD, pair * 256 + (g + 1) * HEAD)
                at = pair * 512 + sub * 256 + g * SUB
                rows = slice(at, at + SUB)
                dq = dq_t[:, g * SUB : (g + 1) * SUB].T
                xh = xh_ref[rows, :]
                dn = dq * c_q - half_turned(dq) * s_q
                qg_acc[...] += jnp.sum((dn * xh).reshape(SUB // 8, 8, HEAD), axis=0)
                dxh = dn * q_gain
                gq = scale_ref[rows, :] * (dxh - xh * jnp.mean(dxh * xh, axis=1, keepdims=True))
                gq_ref[tokens, columns] = gq.astype(jnp.bfloat16)

        shift_0 = scores(0)
        shift_1 = scores(1)
        inverse_0 = exponents(0, shift_0)
        if pair > 0:
            key_terms(pair - 1, 1 - slot)
        weigh(0, inverse_0)
        inverse_1 = exponents(1, shift_1)
        center_0 = attend(0)
        score_terms(0, center_0)
        weigh(1, inverse_1)
        query_terms(0)
        center_1 = attend(1)
        score_terms(1, center_1)
        query_terms(1)
        for copy in copies(pair):
            copy.start()

    key_terms(HEADS // 2 - 1, 1)

    kg = jnp.zeros((8, HEAD), jnp.float32)
    outs = ((four_ref, 0), (swap_ref, 2 * TOK), (two_ref, 0), (swap_ref, 0), (own_ref, 0))
    for j in range(parts):
        rows = slice(j * SUB, (j + 1) * SUB)
        here = slice((j % 2) * SUB, (j % 2 + 1) * SUB)
        x = blocks[j // 2][here, :].astype(jnp.float32)
        r = lax.rsqrt(jnp.mean(x * x, axis=1, keepdims=True) + EPSILON)
        xh = x * r
        d = dk[rows, :] * SCALING
        dn = d * cosine[rows, :] - half_turned(d) * sine[rows, :]
        kg = kg + jnp.sum((dn * xh).reshape(SUB // 8, 8, HEAD), axis=0)
        dxh = dn * k_gain
        gk = r * (dxh - xh * jnp.mean(dxh * xh, axis=1, keepdims=True))
        out, at = outs[j // 2]
        at = at + (j % 2) * SUB
        out[at : at + SUB, :] = gk.astype(out.dtype)
        out[at + TOK : at + TOK + SUB, :] = dv[rows, :].astype(out.dtype)
    gains = jnp.concatenate(
        [jnp.sum(qg_acc[...], axis=0, keepdims=True), jnp.sum(kg, axis=0, keepdims=True)]
    )
    gain_ref[...] = gains
    high = gains.astype(jnp.bfloat16).astype(jnp.float32)
    middle = (gains - high).astype(jnp.bfloat16).astype(jnp.float32)
    low = gains - high - middle
    swap_ref[4 * TOK :, :] = jnp.concatenate(
        [high, middle, low, jnp.zeros((ID_ROWS - 6, HEAD), jnp.float32)]
    ).astype(jnp.bfloat16)
    for pair in range(HEADS // 2):
        for copy in copies(pair):
            copy.wait()


def attention(blocks, prepared, frequency):
    vmem = pl.BlockSpec(memory_space=pltpu.VMEM)
    hbm = pl.BlockSpec(memory_space=pl.ANY)
    f32, bf16 = jnp.float32, jnp.bfloat16
    shape = jax.ShapeDtypeStruct
    return pl.pallas_call(
        kernel,
        out_shape=[
            shape((TOK, HEADS * HEAD), bf16),
            shape((TOK, HEADS * HEAD), bf16),
            shape((2 * TOK, HEAD), f32),
            shape((2 * TOK, HEAD), f32),
            shape((2 * TOK, HEAD), f32),
            shape((4 * TOK + ID_ROWS, HEAD), bf16),
            shape((2, HEAD), f32),
        ],
        in_specs=[vmem] * 12,
        out_specs=[hbm] * 2 + [vmem] * 5,
        scratch_shapes=[
            pltpu.VMEM((TOK, HEADS * HEAD), bf16),
            pltpu.VMEM((TOK, HEADS * HEAD), bf16),
            pltpu.VMEM((WINDOW, HEAD), f32),
            pltpu.VMEM((WINDOW, HEAD), f32),
            pltpu.VMEM((WINDOW, 2 * HEAD), bf16),
            pltpu.VMEM((WINDOW, HEAD), bf16),
            pltpu.VMEM((HEAD, WINDOW), bf16),
            pltpu.VMEM((HEAD, WINDOW), bf16),
            pltpu.VMEM((HEADS * TOK, HEAD), bf16),
            pltpu.VMEM((HEADS // 2, 2 * HEAD, 512), bf16),
            pltpu.VMEM((2, 2, SPAN, 256), f32),
            pltpu.VMEM((2, WINDOW, 512), bf16),
            pltpu.VMEM((2, WINDOW, 512), bf16),
            pltpu.VMEM((WINDOW, HEAD), f32),
            pltpu.VMEM((WINDOW, HEAD), f32),
            pltpu.VMEM((8, HEAD), f32),
            pltpu.VMEM((MSG, HEAD), bf16),
            pltpu.VMEM((MSG, HEAD), bf16),
            pltpu.SemaphoreType.DMA((HEADS // 2,)),
            pltpu.SemaphoreType.DMA((HEADS // 2,)),
        ],
        compiler_params=pltpu.CompilerParams(vmem_limit_bytes=40 * 1024 * 1024),
    )(*blocks, *prepared, frequency)


def pack_kernel(keys, values, ids, out):
    out[0:TOK, :] = keys[...]
    out[TOK : 2 * TOK, :] = values[...]
    marked = (ids[...] + 1).astype(jnp.float32)
    out[2 * TOK :, :] = jnp.concatenate(
        [marked, jnp.zeros((ID_ROWS - 2, HEAD), jnp.float32)]
    ).astype(jnp.bfloat16)


def pack(keys, values, ids):
    vmem = pl.BlockSpec(memory_space=pltpu.VMEM)
    return pl.pallas_call(
        pack_kernel,
        out_shape=jax.ShapeDtypeStruct((MSG, HEAD), jnp.bfloat16),
        in_specs=[vmem] * 3,
        out_specs=vmem,
    )(keys, values, ids)


def swapped(block, ways=(0, 1)):
    route = [(i, i ^ 1) for i in range(lax.axis_size("context")) if i % 2 in ways]
    return lax.ppermute(block, "context", route)


def chip_kernel(swap, four, two, own, gains, four_out, two_out, own_out, gains_out):
    even = lax.rem(lax.axis_index("context"), 2) == 0
    one, three = slice(0, 2 * TOK), slice(2 * TOK, 4 * TOK)

    @pl.when(even)
    def _():
        four_out[...] = four[...].astype(jnp.bfloat16)
        two_out[...] = (two[...] + swap[three, :].astype(jnp.float32)).astype(jnp.bfloat16)
        own_out[...] = own[...] + swap[one, :].astype(jnp.float32)

    @pl.when(jnp.logical_not(even))
    def _():
        four_out[...] = (four[...] + swap[three, :].astype(jnp.float32)).astype(jnp.bfloat16)
        two_out[...] = (two[...] + swap[one, :].astype(jnp.float32)).astype(jnp.bfloat16)
        own_out[...] = own[...]

    split = swap[4 * TOK :, :].astype(jnp.float32)
    total = gains[...] + ((split[0:2] + split[2:4]) + split[4:6])
    for i in range(gains_out.shape[0]):
        gains_out[i] = total


def spread_kernel(terms, copies):
    total = sum(terms[i] for i in range(terms.shape[0]))
    for i in range(copies.shape[0]):
        copies[i] = total


def last_kernel(own, four, two, terms, keys, values, q_gain, k_gain):
    total = own[...] + two[...].astype(jnp.float32) + four[...].astype(jnp.float32)
    total = total.astype(jnp.bfloat16)
    keys[...] = total[:TOK]
    values[...] = total[TOK:]
    gains = sum(terms[i] for i in range(terms.shape[0]))
    q_gain[...] = gains[0:1]
    k_gain[...] = gains[1:2]


def small_call(kernel, out_shape, *operands):
    vmem = pl.BlockSpec(memory_space=pltpu.VMEM)
    return pl.pallas_call(
        kernel,
        out_shape=[jax.ShapeDtypeStruct(shape, dtype) for shape, dtype in out_shape],
        in_specs=[vmem] * len(operands),
        out_specs=[vmem] * len(out_shape),
        compiler_params=pltpu.CompilerParams(vmem_limit_bytes=16 * 1024 * 1024),
    )(*operands)


def body(queries, keys, values, output_gradient, q_gain, k_gain, doc_ids):
    f32, bf16 = jnp.float32, jnp.bfloat16
    message = pack(keys, values, doc_ids.reshape(2, HEAD))
    two = passed_along(message, "context", 2)
    first_swap = swapped(message, (0,))
    four = passed_along(message, "context", 4)
    prepared = prepare(queries, output_gradient, q_gain.reshape(1, HEAD), k_gain.reshape(1, HEAD))
    two, *prepared = lax.optimization_barrier((two, *prepared))
    middle_swap = swapped(two)
    last_swap = swapped(four, (1,))
    blocks = [four, two, message, first_swap, middle_swap, last_swap]
    half = jnp.arange(HEAD // 2, dtype=jnp.float32)
    frequency = THETA ** (-(half * 2.0 / HEAD))
    frequency = jnp.concatenate([frequency, frequency]).reshape(1, HEAD)
    attended, query_gradient, four, two, own, swap, gains = attention(blocks, prepared, frequency)

    tensor, context = lax.axis_size("tensor"), lax.axis_size("context")
    block = (2 * TOK, HEAD)
    four, two, own, gains = small_call(
        chip_kernel,
        [(block, bf16), (block, bf16), (block, f32), ((tensor, 2, HEAD), f32)],
        *(swapped(swap), four, two, own, gains),
    )
    four = passed_along(four, "context", -4)
    two = passed_along(two, "context", -2)
    gains = lax.all_to_all(gains, "tensor", 0, 0)
    (gains,) = small_call(spread_kernel, [((context // 2, 2, HEAD), f32)], gains)
    four, two, gains = lax.optimization_barrier((four, two, gains))
    plane = [[2 * n + core for n in range(context // 2)] for core in range(2)]
    gains = lax.all_to_all(gains, "context", 0, 0, axis_index_groups=plane)
    half_block = (TOK, HEAD)
    key_gradient, value_gradient, q_total, k_total = small_call(
        last_kernel,
        [(half_block, bf16), (half_block, bf16), ((1, HEAD), f32), ((1, HEAD), f32)],
        *(own, four, two, gains),
    )
    return (
        attended,
        query_gradient,
        key_gradient,
        value_gradient,
        q_total.reshape(HEAD),
        k_total.reshape(HEAD),
    )


def solution(mesh):
    placed = (
        P("context", "tensor"),
        P("context", "tensor"),
        P("context", "tensor"),
        P("context", "tensor"),
        P(),
        P(),
        P("context"),
    )
    return jax.shard_map(
        body,
        mesh=mesh,
        in_specs=placed,
        out_specs=(
            P("context", "tensor"),
            P("context", "tensor"),
            P("context", "tensor"),
            P("context", "tensor"),
            P(),
            P(),
        ),
        check_vma=False,
    )
```

```python
import jax
import jax.numpy as jnp
import numpy as np
from jax import lax
from jax.experimental import pallas as pl
from jax.experimental.pallas import tpu as pltpu
from jax.sharding import PartitionSpec as P

REACH = 4
THETA = 500000.0
EPSILON = 1e-06
TOK = 256
HEAD = 128
HEADS = 8
WINDOW = (REACH + 1) * TOK
SUB = 128
SPAN = 1152
CHUNKS = SPAN // SUB
WIDE = 128
ID_ROWS = 16
MSG = 2 * TOK + ID_ROWS
SCALING = HEAD ** (-0.5)
EXP2 = float(SCALING * np.log2(np.e))

PIO2_A = 1.5703125
PIO2_B = float(np.float32(np.round((np.pi / 2 - PIO2_A) * 2.0**23) / 2.0**23))
PIO2_C = float(np.float32(np.pi / 2 - PIO2_A - PIO2_B))


def passed_along(block, axis, distance):
    devices = range(lax.axis_size(axis))
    route = [(i - distance, i) for i in devices if i - distance in devices]
    return lax.ppermute(block, axis, route)


def dot(a, b):
    return jnp.dot(a, b, preferred_element_type=jnp.float32)


def half_turned(x):
    return pltpu.roll(x, HEAD // 2, 1)


def cos_sin(position, frequency):
    angle = position * frequency
    turns = jnp.floor(angle * np.float32(2.0 / np.pi) + 0.5)
    rest = ((angle - turns * PIO2_A) - turns * PIO2_B) - turns * PIO2_C
    square = rest * rest
    sine = rest + rest * square * (
        np.float32(-1.6666654611e-1)
        + square * (np.float32(8.3321608736e-3) + square * np.float32(-1.9515295891e-4))
    )
    cosine = (1.0 - 0.5 * square) + square * square * (
        np.float32(4.166664568298827e-2)
        + square * (np.float32(-1.388731625493765e-3) + square * np.float32(2.443315711809948e-5))
    )
    lane = lax.broadcasted_iota(jnp.int32, angle.shape, 1)
    quadrant = turns.astype(jnp.int32) + jnp.where(lane < HEAD // 2, 1, 0)
    value = jnp.where((quadrant & 1) == 1, cosine, sine)
    return jnp.where((quadrant & 2) == 2, -value, value)


def prepare_kernel(q_ref, d_ref, qg_ref, kg_ref, xh_ref, scale_ref, dcat, dcat_t, gains):
    gains[0:1, :] = qg_ref[...]
    gains[1:2, :] = kg_ref[...]
    for sub in range(2):
        tokens = slice(sub * SUB, (sub + 1) * SUB)
        for h in range(HEADS):
            at = (h // 2) * 512 + sub * 256 + (h % 2) * SUB
            rows = slice(at, at + SUB)
            x = q_ref[tokens, h * HEAD : (h + 1) * HEAD].astype(jnp.float32)
            r = lax.rsqrt(jnp.mean(x * x, axis=1, keepdims=True) + EPSILON)
            xh_ref[rows, :] = x * r
            scale_ref[rows, :] = jnp.broadcast_to(r, (SUB, HEAD))
            d = d_ref[tokens, h * HEAD : (h + 1) * HEAD]
            dcat[rows, :] = d
            dcat_t[h // 2, :, at % 512 : at % 512 + SUB] = d.astype(jnp.float32).T.astype(jnp.bfloat16)


def prepare(queries, output_gradient, q_gain, k_gain):
    vmem = pl.BlockSpec(memory_space=pltpu.VMEM)
    f32, bf16 = jnp.float32, jnp.bfloat16
    shape = jax.ShapeDtypeStruct
    return pl.pallas_call(
        prepare_kernel,
        out_shape=[
            shape((HEADS * TOK, HEAD), f32),
            shape((HEADS * TOK, HEAD), f32),
            shape((HEADS * TOK, HEAD), bf16),
            shape((HEADS // 2, HEAD, 512), bf16),
            shape((2, HEAD), f32),
        ],
        in_specs=[vmem] * 4,
        out_specs=[vmem] * 5,
        compiler_params=pltpu.CompilerParams(vmem_limit_bytes=16 * 1024 * 1024),
        cost_estimate=pl.CostEstimate(flops=10**9, bytes_accessed=4 * 2**20, transcendentals=0),
    )(queries, output_gradient, q_gain, k_gain)


def kernel(
    b4, b2, b0, first_swap, middle_swap, last_swap, xh_ref, scale_ref, dcat, dcat_t, gains_ref, f_ref,
    att_hbm, gq_hbm, four_ref, two_ref, own_ref, swap_ref, gain_ref,
    att_ref, gq_ref, cosine, sine, kext, vwin, khat_t, v_t, qhat, qext_t,
    s_ref, w_ref, ds_ref, dk, dv, qg_acc, b3, b1, att_sem, gq_sem,
):
    even = lax.rem(lax.axis_index("context"), 2) == 0

    @pl.when(even)
    def _():
        b3[...] = last_swap[...]
        b1[...] = middle_swap[...]

    @pl.when(jnp.logical_not(even))
    def _():
        b3[...] = middle_swap[...]
        b1[...] = first_swap[...]

    blocks = (b4, b3, b2, b1, b0)
    lane = lax.broadcasted_iota(jnp.int32, (SUB, HEAD), 1)
    row = lax.broadcasted_iota(jnp.int32, (SUB, HEAD), 0)
    lane_f = lane.astype(jnp.float32)
    row_f = row.astype(jnp.float32)
    left = lane < HEAD // 2
    parts = WINDOW // SUB
    q_gain = gains_ref[0:1, :]
    k_gain = gains_ref[1:2, :]
    frequency = f_ref[...]

    id_rows = []
    for block in blocks:
        both = block[2 * TOK : MSG, :].astype(jnp.float32)
        id_rows += [both[0:1], both[1:2]]
    below = jnp.zeros((SUB, HEAD), jnp.float32)
    for j in range(parts):
        column = jnp.broadcast_to(id_rows[j], (SUB, HEAD)).T
        kext[j * SUB : (j + 1) * SUB, HEAD:] = jnp.where(column == lane_f, 1.0, 0.0).astype(jnp.bfloat16)
        below = below + jnp.where(column < lane_f, 1.0, 0.0)
    first = jnp.sum(below, axis=0, keepdims=True)

    for j in range(parts):
        rows = slice(j * SUB, (j + 1) * SUB)
        here = slice((j % 2) * SUB, (j % 2 + 1) * SUB)
        block = blocks[j // 2]
        member = kext[rows, HEAD:].astype(jnp.float32)
        start = jnp.sum(member * first, axis=1, keepdims=True)
        position = (row + j * SUB).astype(jnp.float32) - start
        both = cos_sin(position, frequency)
        turned = half_turned(both)
        c = jnp.where(left, both, turned)
        s = jnp.where(left, -turned, both)
        cosine[rows, :] = c
        sine[rows, :] = s
        x = block[here, :].astype(jnp.float32)
        normed = x * lax.rsqrt(jnp.mean(x * x, axis=1, keepdims=True) + EPSILON) * k_gain
        hat = normed * c + half_turned(normed) * s
        kext[rows, 0:HEAD] = hat.astype(jnp.bfloat16)
        khat_t[:, rows] = hat.T.astype(jnp.bfloat16)
        values = block[TOK + (j % 2) * SUB : TOK + (j % 2 + 1) * SUB, :]
        vwin[rows, :] = values
        v_t[:, rows] = values.astype(jnp.float32).T.astype(jnp.bfloat16)

    for sub in range(2):
        window_rows = slice(REACH * TOK + sub * SUB, REACH * TOK + (sub + 1) * SUB)
        c_q = cosine[window_rows, :]
        s_q = sine[window_rows, :]
        other = jnp.where(row_f == id_rows[2 * REACH + sub], 0.0, -1e30).astype(jnp.bfloat16)
        for h in range(HEADS):
            at = (h // 2) * 512 + sub * 256 + (h % 2) * SUB
            lanes = slice(at % 512, at % 512 + SUB)
            normed = xh_ref[at : at + SUB, :] * q_gain
            hat = normed * c_q + half_turned(normed) * s_q
            qhat[at : at + SUB, :] = hat.astype(jnp.bfloat16)
            qext_t[h // 2, 0:HEAD, lanes] = hat.T.astype(jnp.bfloat16)
            qext_t[h // 2, HEAD:, lanes] = other

    dk[...] = jnp.zeros_like(dk)
    dv[...] = jnp.zeros_like(dv)
    qg_acc[...] = jnp.zeros_like(qg_acc)
    zero = jnp.zeros((SUB, 256), jnp.bfloat16)
    for ref in (w_ref, ds_ref):
        for slot in range(2):
            ref[slot, 0:SUB, 256:512] = zero
            ref[slot, SPAN:WINDOW, 0:256] = zero
    later = jnp.where(row <= lane, 0.0, -1e30)
    later = jnp.concatenate([later, later], axis=1)
    spans = (slice(0, SPAN), slice(SUB, WINDOW))
    columns_of = (slice(0, 256), slice(256, 512))

    def copies(pair):
        columns = slice(pair * 256, (pair + 1) * 256)
        return (
            pltpu.make_async_copy(att_ref.at[:, columns], att_hbm.at[:, columns], att_sem.at[pair]),
            pltpu.make_async_copy(gq_ref.at[:, columns], gq_hbm.at[:, columns], gq_sem.at[pair]),
        )

    def key_terms(pair, slot):
        rows = slice(pair * 512, (pair + 1) * 512)
        dk[...] += dot(ds_ref[slot], qhat[rows, :])
        dv[...] += dot(w_ref[slot], dcat[rows, :])

    for pair in range(HEADS // 2):
        slot = pair % 2

        def scores(sub):
            q = qext_t[pair, :, columns_of[sub]]
            top = jnp.full((8, 256), -1e30, jnp.float32)
            for start in range(0, SPAN, WIDE):
                s = dot(kext[sub * SUB + start : sub * SUB + start + WIDE, :], q)
                if start + WIDE == SPAN:
                    s = s + later
                s_ref[slot, sub, start : start + WIDE, :] = s
                top = jnp.maximum(top, jnp.max(s.reshape(WIDE // 8, 8, 256), axis=0))
            return jnp.max(top, axis=0, keepdims=True) * EXP2

        def exponents(sub, shift):
            total = jnp.zeros((8, 256), jnp.float32)
            for c in range(CHUNKS):
                e = jnp.exp2(s_ref[slot, sub, c * SUB : (c + 1) * SUB, :] * EXP2 - shift)
                s_ref[slot, sub, c * SUB : (c + 1) * SUB, :] = e
                total = total + jnp.sum(e.reshape(SUB // 8, 8, 256), axis=0)
            return 1.0 / jnp.sum(total, axis=0, keepdims=True)

        def weigh(sub, inverse):
            for c in range(CHUNKS):
                keys = slice((sub + c) * SUB, (sub + c + 1) * SUB)
                w = s_ref[slot, sub, c * SUB : (c + 1) * SUB, :] * inverse
                w_ref[slot, keys, columns_of[sub]] = w.astype(jnp.bfloat16)

        def attend(sub):
            att_t = dot(v_t[:, spans[sub]], w_ref[slot, spans[sub], columns_of[sub]])
            d_t = dcat_t[pair, :, columns_of[sub]]
            center = jnp.sum(att_t * d_t.astype(jnp.float32), axis=0, keepdims=True)
            tokens = slice(sub * SUB, (sub + 1) * SUB)
            for g in range(2):
                columns = slice(pair * 256 + g * HEAD, pair * 256 + (g + 1) * HEAD)
                att_ref[tokens, columns] = att_t[:, g * SUB : (g + 1) * SUB].T.astype(jnp.bfloat16)
            return center

        def score_terms(sub, center):
            d_t = dcat_t[pair, :, columns_of[sub]]
            for start in range(0, SPAN, WIDE):
                keys = slice(sub * SUB + start, sub * SUB + start + WIDE)
                dw = dot(vwin[keys, :], d_t)
                w = w_ref[slot, keys, columns_of[sub]].astype(jnp.float32)
                ds_ref[slot, keys, columns_of[sub]] = (w * (dw - center)).astype(jnp.bfloat16)

        def query_terms(sub):
            dq_t = dot(khat_t[:, spans[sub]], ds_ref[slot, spans[sub], columns_of[sub]]) * SCALING
            tokens = slice(sub * SUB, (sub + 1) * SUB)
            window_rows = slice(REACH * TOK + sub * SUB, REACH * TOK + (sub + 1) * SUB)
            c_q = cosine[window_rows, :]
            s_q = sine[window_rows, :]
            for g in range(2):
                columns = slice(pair * 256 + g * HEAD, pair * 256 + (g + 1) * HEAD)
                at = pair * 512 + sub * 256 + g * SUB
                rows = slice(at, at + SUB)
                dq = dq_t[:, g * SUB : (g + 1) * SUB].T
                xh = xh_ref[rows, :]
                dn = dq * c_q - half_turned(dq) * s_q
                qg_acc[...] += jnp.sum((dn * xh).reshape(SUB // 8, 8, HEAD), axis=0)
                dxh = dn * q_gain
                gq = scale_ref[rows, :] * (dxh - xh * jnp.mean(dxh * xh, axis=1, keepdims=True))
                gq_ref[tokens, columns] = gq.astype(jnp.bfloat16)

        shift_0 = scores(0)
        shift_1 = scores(1)
        inverse_0 = exponents(0, shift_0)
        if pair > 0:
            key_terms(pair - 1, 1 - slot)
        weigh(0, inverse_0)
        inverse_1 = exponents(1, shift_1)
        center_0 = attend(0)
        score_terms(0, center_0)
        weigh(1, inverse_1)
        query_terms(0)
        center_1 = attend(1)
        score_terms(1, center_1)
        query_terms(1)
        for copy in copies(pair):
            copy.start()

    key_terms(HEADS // 2 - 1, 1)

    kg = jnp.zeros((8, HEAD), jnp.float32)
    outs = ((four_ref, 0), (swap_ref, 2 * TOK), (two_ref, 0), (swap_ref, 0), (own_ref, 0))
    for j in range(parts):
        rows = slice(j * SUB, (j + 1) * SUB)
        here = slice((j % 2) * SUB, (j % 2 + 1) * SUB)
        x = blocks[j // 2][here, :].astype(jnp.float32)
        r = lax.rsqrt(jnp.mean(x * x, axis=1, keepdims=True) + EPSILON)
        xh = x * r
        d = dk[rows, :] * SCALING
        dn = d * cosine[rows, :] - half_turned(d) * sine[rows, :]
        kg = kg + jnp.sum((dn * xh).reshape(SUB // 8, 8, HEAD), axis=0)
        dxh = dn * k_gain
        gk = r * (dxh - xh * jnp.mean(dxh * xh, axis=1, keepdims=True))
        out, at = outs[j // 2]
        at = at + (j % 2) * SUB
        out[at : at + SUB, :] = gk.astype(out.dtype)
        out[at + TOK : at + TOK + SUB, :] = dv[rows, :].astype(out.dtype)
    gains = jnp.concatenate(
        [jnp.sum(qg_acc[...], axis=0, keepdims=True), jnp.sum(kg, axis=0, keepdims=True)]
    )
    gain_ref[...] = gains
    high = gains.astype(jnp.bfloat16).astype(jnp.float32)
    middle = (gains - high).astype(jnp.bfloat16).astype(jnp.float32)
    low = gains - high - middle
    swap_ref[4 * TOK :, :] = jnp.concatenate(
        [high, middle, low, jnp.zeros((ID_ROWS - 6, HEAD), jnp.float32)]
    ).astype(jnp.bfloat16)
    for pair in range(HEADS // 2):
        for copy in copies(pair):
            copy.wait()


def attention(blocks, prepared, frequency):
    vmem = pl.BlockSpec(memory_space=pltpu.VMEM)
    hbm = pl.BlockSpec(memory_space=pl.ANY)
    f32, bf16 = jnp.float32, jnp.bfloat16
    shape = jax.ShapeDtypeStruct
    return pl.pallas_call(
        kernel,
        out_shape=[
            shape((TOK, HEADS * HEAD), bf16),
            shape((TOK, HEADS * HEAD), bf16),
            shape((2 * TOK, HEAD), f32),
            shape((2 * TOK, HEAD), f32),
            shape((2 * TOK, HEAD), f32),
            shape((4 * TOK + ID_ROWS, HEAD), bf16),
            shape((2, HEAD), f32),
        ],
        in_specs=[vmem] * 12,
        out_specs=[hbm] * 2 + [vmem] * 5,
        scratch_shapes=[
            pltpu.VMEM((TOK, HEADS * HEAD), bf16),
            pltpu.VMEM((TOK, HEADS * HEAD), bf16),
            pltpu.VMEM((WINDOW, HEAD), f32),
            pltpu.VMEM((WINDOW, HEAD), f32),
            pltpu.VMEM((WINDOW, 2 * HEAD), bf16),
            pltpu.VMEM((WINDOW, HEAD), bf16),
            pltpu.VMEM((HEAD, WINDOW), bf16),
            pltpu.VMEM((HEAD, WINDOW), bf16),
            pltpu.VMEM((HEADS * TOK, HEAD), bf16),
            pltpu.VMEM((HEADS // 2, 2 * HEAD, 512), bf16),
            pltpu.VMEM((2, 2, SPAN, 256), f32),
            pltpu.VMEM((2, WINDOW, 512), bf16),
            pltpu.VMEM((2, WINDOW, 512), bf16),
            pltpu.VMEM((WINDOW, HEAD), f32),
            pltpu.VMEM((WINDOW, HEAD), f32),
            pltpu.VMEM((8, HEAD), f32),
            pltpu.VMEM((MSG, HEAD), bf16),
            pltpu.VMEM((MSG, HEAD), bf16),
            pltpu.SemaphoreType.DMA((HEADS // 2,)),
            pltpu.SemaphoreType.DMA((HEADS // 2,)),
        ],
        compiler_params=pltpu.CompilerParams(vmem_limit_bytes=40 * 1024 * 1024),
    )(*blocks, *prepared, frequency)


def pack_kernel(keys, values, ids, out):
    out[0:TOK, :] = keys[...]
    out[TOK : 2 * TOK, :] = values[...]
    marked = (ids[...] + 1).astype(jnp.float32)
    out[2 * TOK :, :] = jnp.concatenate(
        [marked, jnp.zeros((ID_ROWS - 2, HEAD), jnp.float32)]
    ).astype(jnp.bfloat16)


def pack(keys, values, ids):
    vmem = pl.BlockSpec(memory_space=pltpu.VMEM)
    return pl.pallas_call(
        pack_kernel,
        out_shape=jax.ShapeDtypeStruct((MSG, HEAD), jnp.bfloat16),
        in_specs=[vmem] * 3,
        out_specs=vmem,
    )(keys, values, ids)


def swapped(block, ways=(0, 1)):
    route = [(i, i ^ 1) for i in range(lax.axis_size("context")) if i % 2 in ways]
    return lax.ppermute(block, "context", route)


def chip_kernel(swap, four, two, own, gains, four_out, two_out, own_out, gains_out):
    even = lax.rem(lax.axis_index("context"), 2) == 0
    one, three = slice(0, 2 * TOK), slice(2 * TOK, 4 * TOK)

    @pl.when(even)
    def _():
        four_out[...] = four[...].astype(jnp.bfloat16)
        two_out[...] = two[...] + swap[three, :].astype(jnp.float32)
        own_out[...] = own[...] + swap[one, :].astype(jnp.float32)

    @pl.when(jnp.logical_not(even))
    def _():
        four_out[...] = (four[...] + swap[three, :].astype(jnp.float32)).astype(jnp.bfloat16)
        two_out[...] = two[...] + swap[one, :].astype(jnp.float32)
        own_out[...] = own[...]

    split = swap[4 * TOK :, :].astype(jnp.float32)
    total = gains[...] + ((split[0:2] + split[2:4]) + split[4:6])
    for i in range(gains_out.shape[0]):
        gains_out[i] = total


def plane_kernel(two, hop, terms, two_out, copies):
    two_out[...] = (two[...] + hop[...].astype(jnp.float32)).astype(jnp.bfloat16)
    total = sum(terms[i] for i in range(terms.shape[0]))
    for i in range(copies.shape[0]):
        copies[i] = total


def last_kernel(own, hop, terms, keys, values, q_gain, k_gain):
    total = (own[...] + hop[...].astype(jnp.float32)).astype(jnp.bfloat16)
    keys[...] = total[:TOK]
    values[...] = total[TOK:]
    gains = sum(terms[i] for i in range(terms.shape[0]))
    q_gain[...] = gains[0:1]
    k_gain[...] = gains[1:2]


def small_call(kernel, out_shape, *operands):
    vmem = pl.BlockSpec(memory_space=pltpu.VMEM)
    return pl.pallas_call(
        kernel,
        out_shape=[jax.ShapeDtypeStruct(shape, dtype) for shape, dtype in out_shape],
        in_specs=[vmem] * len(operands),
        out_specs=[vmem] * len(out_shape),
        compiler_params=pltpu.CompilerParams(vmem_limit_bytes=16 * 1024 * 1024),
    )(*operands)


def body(queries, keys, values, output_gradient, q_gain, k_gain, doc_ids):
    f32, bf16 = jnp.float32, jnp.bfloat16
    message = pack(keys, values, doc_ids.reshape(2, HEAD))
    two = passed_along(message, "context", 2)
    first_swap = swapped(message, (0,))
    four = passed_along(message, "context", 4)
    prepared = prepare(queries, output_gradient, q_gain.reshape(1, HEAD), k_gain.reshape(1, HEAD))
    two, *prepared = lax.optimization_barrier((two, *prepared))
    middle_swap = swapped(two)
    last_swap = swapped(four, (1,))
    blocks = [four, two, message, first_swap, middle_swap, last_swap]
    half = jnp.arange(HEAD // 2, dtype=jnp.float32)
    frequency = THETA ** (-(half * 2.0 / HEAD))
    frequency = jnp.concatenate([frequency, frequency]).reshape(1, HEAD)
    attended, query_gradient, four, two, own, swap, gains = attention(blocks, prepared, frequency)

    tensor, context = lax.axis_size("tensor"), lax.axis_size("context")
    block = (2 * TOK, HEAD)
    four, two, own, gains = small_call(
        chip_kernel,
        [(block, bf16), (block, f32), (block, f32), ((tensor, 2, HEAD), f32)],
        *(swapped(swap), four, two, own, gains),
    )
    hop = passed_along(four, "context", -2)
    gains = lax.all_to_all(gains, "tensor", 0, 0)
    two, gains = small_call(
        plane_kernel, [(block, bf16), ((context // 2, 2, HEAD), f32)], two, hop, gains
    )
    hop = passed_along(two, "context", -2)
    plane = [[2 * n + core for n in range(context // 2)] for core in range(2)]
    gains = lax.all_to_all(gains, "context", 0, 0, axis_index_groups=plane)
    half_block = (TOK, HEAD)
    key_gradient, value_gradient, q_total, k_total = small_call(
        last_kernel,
        [(half_block, bf16), (half_block, bf16), ((1, HEAD), f32), ((1, HEAD), f32)],
        *(own, hop, gains),
    )
    return (
        attended,
        query_gradient,
        key_gradient,
        value_gradient,
        q_total.reshape(HEAD),
        k_total.reshape(HEAD),
    )


def solution(mesh):
    placed = (
        P("context", "tensor"),
        P("context", "tensor"),
        P("context", "tensor"),
        P("context", "tensor"),
        P(),
        P(),
        P("context"),
    )
    return jax.shard_map(
        body,
        mesh=mesh,
        in_specs=placed,
        out_specs=(
            P("context", "tensor"),
            P("context", "tensor"),
            P("context", "tensor"),
            P("context", "tensor"),
            P(),
            P(),
        ),
        check_vma=False,
    )
```

```python
import jax
import jax.numpy as jnp
import numpy as np
from jax import lax
from jax.experimental import pallas as pl
from jax.experimental.pallas import tpu as pltpu
from jax.sharding import PartitionSpec as P

REACH = 4
THETA = 500000.0
EPSILON = 1e-06
TOK = 256
HEAD = 128
HEADS = 8
WINDOW = (REACH + 1) * TOK
SUB = 128
SPAN = 1152
CHUNKS = SPAN // SUB
WIDE = 128
KEY_BLOCKS = (
    [(0, SUB, 0, 256)]
    + [(start, start + 256, 0, 512) for start in range(SUB, SPAN, 256)]
    + [(SPAN, WINDOW, 256, 512)]
)
ID_ROWS = 16
MSG = 2 * TOK + ID_ROWS
SCALING = HEAD ** (-0.5)
EXP2 = float(SCALING * np.log2(np.e))

PI_A = 3.140625
PI_B = float(np.round((np.pi - PI_A) * 2.0**23) / 2.0**23)
PI_C = float(np.pi - PI_A - PI_B)


def passed_along(block, axis, distance):
    devices = range(lax.axis_size(axis))
    route = [(i - distance, i) for i in devices if i - distance in devices]
    return lax.ppermute(block, axis, route)


def dot(a, b):
    return jnp.dot(a, b, preferred_element_type=jnp.float32)


def half_turned(x):
    return pltpu.roll(x, HEAD // 2, 1)


def cos_sin(position, frequency):
    angle = position * frequency
    lane = lax.broadcasted_iota(jnp.int32, (1, HEAD), 1)
    quarter = jnp.where(lane < HEAD // 2, 0.5, 0.0)
    turns = jnp.floor(angle * np.float32(1.0 / np.pi) + (quarter + 0.5))
    count = turns - quarter
    rest = ((angle - count * PI_A) - count * PI_B) - count * PI_C
    square = rest * rest
    series = np.float32(-1.9806614727713168e-4) + square * np.float32(2.6000534489867277e-6)
    series = np.float32(8.333017118275166e-3) + square * series
    series = np.float32(-1.6666656732559204e-1) + square * series
    value = rest + rest * (square * series)
    return jnp.where((turns.astype(jnp.int32) & 1) == 1, -value, value)


def prepare_kernel(q_ref, d_ref, qg_ref, kg_ref, xh_ref, scale_ref, dcat, dcat_t, gains):
    gains[0:1, :] = qg_ref[...]
    gains[1:2, :] = kg_ref[...]
    for sub in range(2):
        tokens = slice(sub * SUB, (sub + 1) * SUB)
        for h in range(HEADS):
            at = (h // 2) * 512 + sub * 256 + (h % 2) * SUB
            rows = slice(at, at + SUB)
            x = q_ref[tokens, h * HEAD : (h + 1) * HEAD].astype(jnp.float32)
            r = lax.rsqrt(jnp.mean(x * x, axis=1, keepdims=True) + EPSILON)
            xh_ref[rows, :] = x * r
            scale_ref[rows, :] = jnp.broadcast_to(r, (SUB, HEAD))
            d = d_ref[tokens, h * HEAD : (h + 1) * HEAD]
            dcat[rows, :] = d
            dcat_t[h // 2, :, at % 512 : at % 512 + SUB] = d.astype(jnp.float32).T.astype(jnp.bfloat16)


def prepare(queries, output_gradient, q_gain, k_gain):
    vmem = pl.BlockSpec(memory_space=pltpu.VMEM)
    f32, bf16 = jnp.float32, jnp.bfloat16
    shape = jax.ShapeDtypeStruct
    return pl.pallas_call(
        prepare_kernel,
        out_shape=[
            shape((HEADS * TOK, HEAD), f32),
            shape((HEADS * TOK, HEAD), f32),
            shape((HEADS * TOK, HEAD), bf16),
            shape((HEADS // 2, HEAD, 512), bf16),
            shape((2, HEAD), f32),
        ],
        in_specs=[vmem] * 4,
        out_specs=[vmem] * 5,
        compiler_params=pltpu.CompilerParams(vmem_limit_bytes=16 * 1024 * 1024),
        cost_estimate=pl.CostEstimate(flops=10**9, bytes_accessed=4 * 2**20, transcendentals=0),
    )(queries, output_gradient, q_gain, k_gain)


def kernel(
    b4, b2, b0, first_swap, middle_swap, last_swap, xh_ref, scale_ref, dcat, dcat_t, gains_ref, f_ref,
    att_hbm, gq_hbm, four_ref, two_ref, own_ref, swap_ref, gain_ref,
    att_ref, gq_ref, cosine, sine, kext, vwin, khat_t, v_t, qhat, qext_t,
    s_ref, w_ref, ds_ref, dk, dv, qg_acc, b3, b1, att_sem, gq_sem,
):
    even = lax.rem(lax.axis_index("context"), 2) == 0

    @pl.when(even)
    def _():
        b3[...] = last_swap[...]
        b1[...] = middle_swap[...]

    @pl.when(jnp.logical_not(even))
    def _():
        b3[...] = middle_swap[...]
        b1[...] = first_swap[...]

    blocks = (b4, b3, b2, b1, b0)
    lane = lax.broadcasted_iota(jnp.int32, (SUB, HEAD), 1)
    row = lax.broadcasted_iota(jnp.int32, (SUB, HEAD), 0)
    lane_f = lane.astype(jnp.float32)
    row_f = row.astype(jnp.float32)
    left = lane < HEAD // 2
    parts = WINDOW // SUB
    q_gain = gains_ref[0:1, :]
    k_gain = gains_ref[1:2, :]
    frequency = f_ref[...]

    id_rows = []
    for block in blocks:
        both = block[2 * TOK : MSG, :].astype(jnp.float32)
        id_rows += [both[0:1], both[1:2]]
    below = jnp.zeros((SUB, HEAD), jnp.float32)
    for j in range(parts):
        column = jnp.broadcast_to(id_rows[j], (SUB, HEAD)).T
        kext[j * SUB : (j + 1) * SUB, HEAD:] = jnp.where(column == lane_f, 1.0, 0.0).astype(jnp.bfloat16)
        below = below + jnp.where(column < lane_f, 1.0, 0.0)
    first = jnp.sum(below, axis=0, keepdims=True)

    for j in range(parts):
        rows = slice(j * SUB, (j + 1) * SUB)
        here = slice((j % 2) * SUB, (j % 2 + 1) * SUB)
        block = blocks[j // 2]
        member = kext[rows, HEAD:].astype(jnp.float32)
        start = jnp.sum(member * first, axis=1, keepdims=True)
        position = (row + j * SUB).astype(jnp.float32) - start
        both = cos_sin(position, frequency)
        turned = half_turned(both)
        c = jnp.where(left, both, turned)
        s = jnp.where(left, -turned, both)
        cosine[rows, :] = c
        sine[rows, :] = s
        x = block[here, :].astype(jnp.float32)
        normed = x * lax.rsqrt(jnp.mean(x * x, axis=1, keepdims=True) + EPSILON) * k_gain
        hat = normed * c + half_turned(normed) * s
        kext[rows, 0:HEAD] = hat.astype(jnp.bfloat16)
        khat_t[:, rows] = hat.T.astype(jnp.bfloat16)
        values = block[TOK + (j % 2) * SUB : TOK + (j % 2 + 1) * SUB, :]
        vwin[rows, :] = values
        v_t[:, rows] = values.astype(jnp.float32).T.astype(jnp.bfloat16)

    for sub in range(2):
        window_rows = slice(REACH * TOK + sub * SUB, REACH * TOK + (sub + 1) * SUB)
        c_q = cosine[window_rows, :]
        s_q = sine[window_rows, :]
        other = jnp.where(row_f == id_rows[2 * REACH + sub], 0.0, -1e30).astype(jnp.bfloat16)
        for h in range(HEADS):
            at = (h // 2) * 512 + sub * 256 + (h % 2) * SUB
            lanes = slice(at % 512, at % 512 + SUB)
            normed = xh_ref[at : at + SUB, :] * q_gain
            hat = normed * c_q + half_turned(normed) * s_q
            qhat[at : at + SUB, :] = hat.astype(jnp.bfloat16)
            qext_t[h // 2, 0:HEAD, lanes] = hat.T.astype(jnp.bfloat16)
            qext_t[h // 2, HEAD:, lanes] = other

    dk[...] = jnp.zeros_like(dk)
    dv[...] = jnp.zeros_like(dv)
    qg_acc[...] = jnp.zeros_like(qg_acc)
    later = jnp.where(row <= lane, 0.0, -1e30)
    later = jnp.concatenate([later, later], axis=1)
    spans = (slice(0, SPAN), slice(SUB, WINDOW))
    columns_of = (slice(0, 256), slice(256, 512))

    def copies(pair):
        columns = slice(pair * 256, (pair + 1) * 256)
        return (
            pltpu.make_async_copy(att_ref.at[:, columns], att_hbm.at[:, columns], att_sem.at[pair]),
            pltpu.make_async_copy(gq_ref.at[:, columns], gq_hbm.at[:, columns], gq_sem.at[pair]),
        )

    def key_terms(pair, slot):
        for start, stop, low, high in KEY_BLOCKS:
            keys, lanes = slice(start, stop), slice(low, high)
            rows = slice(pair * 512 + low, pair * 512 + high)
            dk[keys, :] += dot(ds_ref[slot, keys, lanes], qhat[rows, :])
            dv[keys, :] += dot(w_ref[slot, keys, lanes], dcat[rows, :])

    for pair in range(HEADS // 2):
        slot = pair % 2

        def scores(sub):
            q = qext_t[pair, :, columns_of[sub]]
            top = jnp.full((8, 256), -1e30, jnp.float32)
            for start in range(0, SPAN, WIDE):
                s = dot(kext[sub * SUB + start : sub * SUB + start + WIDE, :], q)
                if start + WIDE == SPAN:
                    s = s + later
                s_ref[slot, sub, start : start + WIDE, :] = s
                top = jnp.maximum(top, jnp.max(s.reshape(WIDE // 8, 8, 256), axis=0))
            return jnp.max(top, axis=0, keepdims=True) * EXP2

        def exponents(sub, shift):
            total = jnp.zeros((8, 256), jnp.float32)
            for c in range(CHUNKS):
                e = jnp.exp2(s_ref[slot, sub, c * SUB : (c + 1) * SUB, :] * EXP2 - shift)
                s_ref[slot, sub, c * SUB : (c + 1) * SUB, :] = e
                total = total + jnp.sum(e.reshape(SUB // 8, 8, 256), axis=0)
            return 1.0 / jnp.sum(total, axis=0, keepdims=True)

        def weigh(sub, inverse):
            for c in range(CHUNKS):
                keys = slice((sub + c) * SUB, (sub + c + 1) * SUB)
                w = s_ref[slot, sub, c * SUB : (c + 1) * SUB, :] * inverse
                w_ref[slot, keys, columns_of[sub]] = w.astype(jnp.bfloat16)

        def attend(sub):
            att_t = dot(v_t[:, spans[sub]], w_ref[slot, spans[sub], columns_of[sub]])
            d_t = dcat_t[pair, :, columns_of[sub]]
            center = jnp.sum(att_t * d_t.astype(jnp.float32), axis=0, keepdims=True)
            tokens = slice(sub * SUB, (sub + 1) * SUB)
            for g in range(2):
                columns = slice(pair * 256 + g * HEAD, pair * 256 + (g + 1) * HEAD)
                att_ref[tokens, columns] = att_t[:, g * SUB : (g + 1) * SUB].T.astype(jnp.bfloat16)
            return center

        def score_terms(sub, center):
            d_t = dcat_t[pair, :, columns_of[sub]]
            for start in range(0, SPAN, WIDE):
                keys = slice(sub * SUB + start, sub * SUB + start + WIDE)
                dw = dot(vwin[keys, :], d_t)
                w = w_ref[slot, keys, columns_of[sub]].astype(jnp.float32)
                ds_ref[slot, keys, columns_of[sub]] = (w * (dw - center)).astype(jnp.bfloat16)

        def query_terms(sub):
            dq_t = dot(khat_t[:, spans[sub]], ds_ref[slot, spans[sub], columns_of[sub]]) * SCALING
            tokens = slice(sub * SUB, (sub + 1) * SUB)
            window_rows = slice(REACH * TOK + sub * SUB, REACH * TOK + (sub + 1) * SUB)
            c_q = cosine[window_rows, :]
            s_q = sine[window_rows, :]
            for g in range(2):
                columns = slice(pair * 256 + g * HEAD, pair * 256 + (g + 1) * HEAD)
                at = pair * 512 + sub * 256 + g * SUB
                rows = slice(at, at + SUB)
                dq = dq_t[:, g * SUB : (g + 1) * SUB].T
                xh = xh_ref[rows, :]
                dn = dq * c_q - half_turned(dq) * s_q
                qg_acc[...] += jnp.sum((dn * xh).reshape(SUB // 8, 8, HEAD), axis=0)
                dxh = dn * q_gain
                gq = scale_ref[rows, :] * (dxh - xh * jnp.mean(dxh * xh, axis=1, keepdims=True))
                gq_ref[tokens, columns] = gq.astype(jnp.bfloat16)

        shift_0 = scores(0)
        shift_1 = scores(1)
        inverse_0 = exponents(0, shift_0)
        if pair > 0:
            key_terms(pair - 1, 1 - slot)
        weigh(0, inverse_0)
        inverse_1 = exponents(1, shift_1)
        center_0 = attend(0)
        score_terms(0, center_0)
        weigh(1, inverse_1)
        query_terms(0)
        center_1 = attend(1)
        score_terms(1, center_1)
        query_terms(1)
        for copy in copies(pair):
            copy.start()

    key_terms(HEADS // 2 - 1, 1)

    kg = jnp.zeros((8, HEAD), jnp.float32)
    outs = ((four_ref, 0), (swap_ref, 2 * TOK), (two_ref, 0), (swap_ref, 0), (own_ref, 0))
    for j in range(parts):
        rows = slice(j * SUB, (j + 1) * SUB)
        here = slice((j % 2) * SUB, (j % 2 + 1) * SUB)
        x = blocks[j // 2][here, :].astype(jnp.float32)
        r = lax.rsqrt(jnp.mean(x * x, axis=1, keepdims=True) + EPSILON)
        xh = x * r
        d = dk[rows, :] * SCALING
        dn = d * cosine[rows, :] - half_turned(d) * sine[rows, :]
        kg = kg + jnp.sum((dn * xh).reshape(SUB // 8, 8, HEAD), axis=0)
        dxh = dn * k_gain
        gk = r * (dxh - xh * jnp.mean(dxh * xh, axis=1, keepdims=True))
        out, at = outs[j // 2]
        at = at + (j % 2) * SUB
        out[at : at + SUB, :] = gk.astype(out.dtype)
        out[at + TOK : at + TOK + SUB, :] = dv[rows, :].astype(out.dtype)
    gains = jnp.concatenate(
        [jnp.sum(qg_acc[...], axis=0, keepdims=True), jnp.sum(kg, axis=0, keepdims=True)]
    )
    gain_ref[...] = gains
    high = gains.astype(jnp.bfloat16).astype(jnp.float32)
    middle = (gains - high).astype(jnp.bfloat16).astype(jnp.float32)
    low = gains - high - middle
    swap_ref[4 * TOK :, :] = jnp.concatenate(
        [high, middle, low, jnp.zeros((ID_ROWS - 6, HEAD), jnp.float32)]
    ).astype(jnp.bfloat16)
    for pair in range(HEADS // 2):
        for copy in copies(pair):
            copy.wait()


def attention(blocks, prepared, frequency):
    vmem = pl.BlockSpec(memory_space=pltpu.VMEM)
    hbm = pl.BlockSpec(memory_space=pl.ANY)
    f32, bf16 = jnp.float32, jnp.bfloat16
    shape = jax.ShapeDtypeStruct
    return pl.pallas_call(
        kernel,
        out_shape=[
            shape((TOK, HEADS * HEAD), bf16),
            shape((TOK, HEADS * HEAD), bf16),
            shape((2 * TOK, HEAD), f32),
            shape((2 * TOK, HEAD), f32),
            shape((2 * TOK, HEAD), f32),
            shape((4 * TOK + ID_ROWS, HEAD), bf16),
            shape((2, HEAD), f32),
        ],
        in_specs=[vmem] * 12,
        out_specs=[hbm] * 2 + [vmem] * 5,
        scratch_shapes=[
            pltpu.VMEM((TOK, HEADS * HEAD), bf16),
            pltpu.VMEM((TOK, HEADS * HEAD), bf16),
            pltpu.VMEM((WINDOW, HEAD), f32),
            pltpu.VMEM((WINDOW, HEAD), f32),
            pltpu.VMEM((WINDOW, 2 * HEAD), bf16),
            pltpu.VMEM((WINDOW, HEAD), bf16),
            pltpu.VMEM((HEAD, WINDOW), bf16),
            pltpu.VMEM((HEAD, WINDOW), bf16),
            pltpu.VMEM((HEADS * TOK, HEAD), bf16),
            pltpu.VMEM((HEADS // 2, 2 * HEAD, 512), bf16),
            pltpu.VMEM((2, 2, SPAN, 256), f32),
            pltpu.VMEM((2, WINDOW, 512), bf16),
            pltpu.VMEM((2, WINDOW, 512), bf16),
            pltpu.VMEM((WINDOW, HEAD), f32),
            pltpu.VMEM((WINDOW, HEAD), f32),
            pltpu.VMEM((8, HEAD), f32),
            pltpu.VMEM((MSG, HEAD), bf16),
            pltpu.VMEM((MSG, HEAD), bf16),
            pltpu.SemaphoreType.DMA((HEADS // 2,)),
            pltpu.SemaphoreType.DMA((HEADS // 2,)),
        ],
        compiler_params=pltpu.CompilerParams(vmem_limit_bytes=40 * 1024 * 1024),
    )(*blocks, *prepared, frequency)


def pack_kernel(keys, values, ids, out):
    out[0:TOK, :] = keys[...]
    out[TOK : 2 * TOK, :] = values[...]
    marked = (ids[...] + 1).astype(jnp.float32)
    out[2 * TOK :, :] = jnp.concatenate(
        [marked, jnp.zeros((ID_ROWS - 2, HEAD), jnp.float32)]
    ).astype(jnp.bfloat16)


def pack(keys, values, ids):
    vmem = pl.BlockSpec(memory_space=pltpu.VMEM)
    return pl.pallas_call(
        pack_kernel,
        out_shape=jax.ShapeDtypeStruct((MSG, HEAD), jnp.bfloat16),
        in_specs=[vmem] * 3,
        out_specs=vmem,
    )(keys, values, ids)


def swapped(block, ways=(0, 1)):
    route = [(i, i ^ 1) for i in range(lax.axis_size("context")) if i % 2 in ways]
    return lax.ppermute(block, "context", route)


def chip_kernel(swap, four, two, own, gains, four_out, two_out, own_out, gains_out):
    even = lax.rem(lax.axis_index("context"), 2) == 0
    one, three = slice(0, 2 * TOK), slice(2 * TOK, 4 * TOK)

    @pl.when(even)
    def _():
        four_out[...] = four[...].astype(jnp.bfloat16)
        two_out[...] = two[...] + swap[three, :].astype(jnp.float32)
        own_out[...] = own[...] + swap[one, :].astype(jnp.float32)

    @pl.when(jnp.logical_not(even))
    def _():
        four_out[...] = (four[...] + swap[three, :].astype(jnp.float32)).astype(jnp.bfloat16)
        two_out[...] = two[...] + swap[one, :].astype(jnp.float32)
        own_out[...] = own[...]

    split = swap[4 * TOK :, :].astype(jnp.float32)
    total = gains[...] + ((split[0:2] + split[2:4]) + split[4:6])
    for i in range(gains_out.shape[0]):
        gains_out[i] = total


def hop_kernel(two, hop, two_out):
    two_out[...] = (two[...] + hop[...].astype(jnp.float32)).astype(jnp.bfloat16)


def last_kernel(own, hop, terms, keys, values, q_gain, k_gain):
    total = (own[...] + hop[...].astype(jnp.float32)).astype(jnp.bfloat16)
    keys[...] = total[:TOK]
    values[...] = total[TOK:]
    gains = jnp.sum(terms[...], axis=0)
    q_gain[...] = gains[0:1]
    k_gain[...] = gains[1:2]


def small_call(kernel, out_shape, *operands):
    vmem = pl.BlockSpec(memory_space=pltpu.VMEM)
    return pl.pallas_call(
        kernel,
        out_shape=[jax.ShapeDtypeStruct(shape, dtype) for shape, dtype in out_shape],
        in_specs=[vmem] * len(operands),
        out_specs=[vmem] * len(out_shape),
        compiler_params=pltpu.CompilerParams(vmem_limit_bytes=16 * 1024 * 1024),
    )(*operands)


def body(queries, keys, values, output_gradient, q_gain, k_gain, doc_ids):
    f32, bf16 = jnp.float32, jnp.bfloat16
    message = pack(keys, values, doc_ids.reshape(2, HEAD))
    two = passed_along(message, "context", 2)
    first_swap = swapped(message, (0,))
    four = passed_along(message, "context", 4)
    prepared = prepare(queries, output_gradient, q_gain.reshape(1, HEAD), k_gain.reshape(1, HEAD))
    two, *prepared = lax.optimization_barrier((two, *prepared))
    middle_swap = swapped(two)
    last_swap = swapped(four, (1,))
    blocks = [four, two, message, first_swap, middle_swap, last_swap]
    half = jnp.arange(HEAD // 2, dtype=jnp.float32)
    frequency = THETA ** (-(half * 2.0 / HEAD))
    frequency = jnp.concatenate([frequency, frequency]).reshape(1, HEAD)
    attended, query_gradient, four, two, own, swap, gains = attention(blocks, prepared, frequency)

    axes = ("context", "tensor")
    chips = lax.axis_size(axes) // 2
    block = (2 * TOK, HEAD)
    four, two, own, gains = small_call(
        chip_kernel,
        [(block, bf16), (block, f32), (block, f32), ((chips, 2, HEAD), f32)],
        *(swapped(swap), four, two, own, gains),
    )
    hop = passed_along(four, "context", -2)
    width = lax.axis_size("tensor")
    cores = [
        [(2 * n + core) * width + z for n in range(chips // width) for z in range(width)]
        for core in range(2)
    ]
    gains = lax.all_to_all(gains, axes, 0, 0, axis_index_groups=cores)
    (two,) = small_call(hop_kernel, [(block, bf16)], two, hop)
    hop = passed_along(two, "context", -2)
    half_block = (TOK, HEAD)
    key_gradient, value_gradient, q_total, k_total = small_call(
        last_kernel,
        [(half_block, bf16), (half_block, bf16), ((1, HEAD), f32), ((1, HEAD), f32)],
        *(own, hop, gains),
    )
    return (
        attended,
        query_gradient,
        key_gradient,
        value_gradient,
        q_total.reshape(HEAD),
        k_total.reshape(HEAD),
    )


def solution(mesh):
    placed = (
        P("context", "tensor"),
        P("context", "tensor"),
        P("context", "tensor"),
        P("context", "tensor"),
        P(),
        P(),
        P("context"),
    )
    return jax.shard_map(
        body,
        mesh=mesh,
        in_specs=placed,
        out_specs=(
            P("context", "tensor"),
            P("context", "tensor"),
            P("context", "tensor"),
            P("context", "tensor"),
            P(),
            P(),
        ),
        check_vma=False,
    )
```

```python
import jax
import jax.numpy as jnp
import numpy as np
from jax import lax
from jax.experimental import pallas as pl
from jax.experimental.pallas import tpu as pltpu
from jax.sharding import PartitionSpec as P

REACH = 4
THETA = 500000.0
EPSILON = 1e-06
TOK = 256
HEAD = 128
HEADS = 8
WINDOW = (REACH + 1) * TOK
SUB = 128
SPAN = 1152
CHUNKS = SPAN // SUB
KEY_BLOCKS = (
    [(0, SUB, 0, 256)]
    + [(start, start + 256, 0, 512) for start in range(SUB, SPAN, 256)]
    + [(SPAN, WINDOW, 256, 512)]
)
ID_ROWS = 16
MSG = 2 * TOK + ID_ROWS
SCALING = HEAD ** (-0.5)
EXP2 = float(SCALING * np.log2(np.e))

PI_A = 3.140625
PI_B = float(np.round((np.pi - PI_A) * 2.0**23) / 2.0**23)
PI_C = float(np.pi - PI_A - PI_B)


def passed_along(block, axis, distance):
    devices = range(lax.axis_size(axis))
    route = [(i - distance, i) for i in devices if i - distance in devices]
    return lax.ppermute(block, axis, route)


def dot(a, b):
    return jnp.dot(a, b, preferred_element_type=jnp.float32)


def half_turned(x):
    return pltpu.roll(x, HEAD // 2, 1)


def cos_sin(position, frequency):
    angle = position * frequency
    lane = lax.broadcasted_iota(jnp.int32, (1, HEAD), 1)
    quarter = jnp.where(lane < HEAD // 2, 0.5, 0.0)
    turns = jnp.floor(angle * np.float32(1.0 / np.pi) + (quarter + 0.5))
    count = turns - quarter
    rest = ((angle - count * PI_A) - count * PI_B) - count * PI_C
    square = rest * rest
    series = np.float32(-1.9806614727713168e-4) + square * np.float32(2.6000534489867277e-6)
    series = np.float32(8.333017118275166e-3) + square * series
    series = np.float32(-1.6666656732559204e-1) + square * series
    value = rest + rest * (square * series)
    return jnp.where((turns.astype(jnp.int32) & 1) == 1, -value, value)


def prepare_kernel(q_ref, d_ref, qg_ref, kg_ref, xh_ref, scale_ref, dcat, dcat_t, gains):
    gains[0:1, :] = qg_ref[...]
    gains[1:2, :] = kg_ref[...]
    for sub in range(2):
        tokens = slice(sub * SUB, (sub + 1) * SUB)
        for h in range(HEADS):
            at = (h // 2) * 512 + sub * 256 + (h % 2) * SUB
            rows = slice(at, at + SUB)
            x = q_ref[tokens, h * HEAD : (h + 1) * HEAD].astype(jnp.float32)
            r = lax.rsqrt(jnp.mean(x * x, axis=1, keepdims=True) + EPSILON)
            xh_ref[rows, :] = x * r
            scale_ref[rows, :] = jnp.broadcast_to(r, (SUB, HEAD))
            d = d_ref[tokens, h * HEAD : (h + 1) * HEAD]
            dcat[rows, :] = d
            dcat_t[h // 2, :, at % 512 : at % 512 + SUB] = d.astype(jnp.float32).T.astype(jnp.bfloat16)


def prepare(queries, output_gradient, q_gain, k_gain):
    vmem = pl.BlockSpec(memory_space=pltpu.VMEM)
    f32, bf16 = jnp.float32, jnp.bfloat16
    shape = jax.ShapeDtypeStruct
    return pl.pallas_call(
        prepare_kernel,
        out_shape=[
            shape((HEADS * TOK, HEAD), f32),
            shape((HEADS * TOK, HEAD), f32),
            shape((HEADS * TOK, HEAD), bf16),
            shape((HEADS // 2, HEAD, 512), bf16),
            shape((2, HEAD), f32),
        ],
        in_specs=[vmem] * 4,
        out_specs=[vmem] * 5,
        compiler_params=pltpu.CompilerParams(vmem_limit_bytes=16 * 1024 * 1024),
        cost_estimate=pl.CostEstimate(flops=10**9, bytes_accessed=4 * 2**20, transcendentals=0),
    )(queries, output_gradient, q_gain, k_gain)


def kernel(
    b4, b2, b0, first_swap, middle_swap, last_swap, xh_ref, scale_ref, dcat, dcat_t, gains_ref, f_ref,
    att_hbm, gq_hbm, four_ref, two_ref, own_ref, swap_ref, gain_ref,
    att_ref, gq_ref, cosine, sine, kext, vwin, khat_t, v_t, qhat, qext_t,
    s_ref, w_ref, ds_ref, dk, dv, qg_acc, b3, b1, att_sem, gq_sem,
):
    even = lax.rem(lax.axis_index("context"), 2) == 0

    @pl.when(even)
    def _():
        b3[...] = last_swap[...]
        b1[...] = middle_swap[...]

    @pl.when(jnp.logical_not(even))
    def _():
        b3[...] = middle_swap[...]
        b1[...] = first_swap[...]

    blocks = (b4, b3, b2, b1, b0)
    lane = lax.broadcasted_iota(jnp.int32, (SUB, HEAD), 1)
    row = lax.broadcasted_iota(jnp.int32, (SUB, HEAD), 0)
    lane_f = lane.astype(jnp.float32)
    row_f = row.astype(jnp.float32)
    left = lane < HEAD // 2
    parts = WINDOW // SUB
    q_gain = gains_ref[0:1, :]
    k_gain = gains_ref[1:2, :]
    frequency = f_ref[...]

    id_rows = []
    for block in blocks:
        both = block[2 * TOK : MSG, :].astype(jnp.float32)
        id_rows += [both[0:1], both[1:2]]
    below = jnp.zeros((SUB, HEAD), jnp.float32)
    for j in range(parts):
        column = jnp.broadcast_to(id_rows[j], (SUB, HEAD)).T
        kext[j * SUB : (j + 1) * SUB, HEAD:] = jnp.where(column == lane_f, 1.0, 0.0).astype(jnp.bfloat16)
        below = below + jnp.where(column < lane_f, 1.0, 0.0)
    first = jnp.sum(below, axis=0, keepdims=True)

    for j in range(parts):
        rows = slice(j * SUB, (j + 1) * SUB)
        here = slice((j % 2) * SUB, (j % 2 + 1) * SUB)
        block = blocks[j // 2]
        member = kext[rows, HEAD:].astype(jnp.float32)
        start = jnp.sum(member * first, axis=1, keepdims=True)
        position = (row + j * SUB).astype(jnp.float32) - start
        both = cos_sin(position, frequency)
        turned = half_turned(both)
        c = jnp.where(left, both, turned)
        s = jnp.where(left, -turned, both)
        cosine[rows, :] = c
        sine[rows, :] = s
        x = block[here, :].astype(jnp.float32)
        normed = x * lax.rsqrt(jnp.mean(x * x, axis=1, keepdims=True) + EPSILON) * k_gain
        hat = normed * c + half_turned(normed) * s
        kext[rows, 0:HEAD] = hat.astype(jnp.bfloat16)
        khat_t[:, rows] = hat.T.astype(jnp.bfloat16)
        values = block[TOK + (j % 2) * SUB : TOK + (j % 2 + 1) * SUB, :]
        vwin[rows, :] = values
        v_t[:, rows] = values.astype(jnp.float32).T.astype(jnp.bfloat16)

    for sub in range(2):
        window_rows = slice(REACH * TOK + sub * SUB, REACH * TOK + (sub + 1) * SUB)
        c_q = cosine[window_rows, :]
        s_q = sine[window_rows, :]
        other = jnp.where(row_f == id_rows[2 * REACH + sub], 0.0, -1e30).astype(jnp.bfloat16)
        for h in range(HEADS):
            at = (h // 2) * 512 + sub * 256 + (h % 2) * SUB
            lanes = slice(at % 512, at % 512 + SUB)
            normed = xh_ref[at : at + SUB, :] * q_gain
            hat = normed * c_q + half_turned(normed) * s_q
            qhat[at : at + SUB, :] = hat.astype(jnp.bfloat16)
            qext_t[h // 2, 0:HEAD, lanes] = hat.T.astype(jnp.bfloat16)
            qext_t[h // 2, HEAD:, lanes] = other

    dk[...] = jnp.zeros_like(dk)
    dv[...] = jnp.zeros_like(dv)
    qg_acc[...] = jnp.zeros_like(qg_acc)
    later = jnp.where(row <= lane, 0.0, -1e30)
    later = jnp.concatenate([later, later], axis=1)
    spans = (slice(0, SPAN), slice(SUB, WINDOW))
    columns_of = (slice(0, 256), slice(256, 512))

    def copies(pair):
        columns = slice(pair * 256, (pair + 1) * 256)
        return (
            pltpu.make_async_copy(att_ref.at[:, columns], att_hbm.at[:, columns], att_sem.at[pair]),
            pltpu.make_async_copy(gq_ref.at[:, columns], gq_hbm.at[:, columns], gq_sem.at[pair]),
        )

    shifts, inverses, centers = {}, {}, {}

    def scores(pair, sub):
        q = qext_t[pair, :, columns_of[sub]]
        top = jnp.full((8, 256), -1e30, jnp.float32)
        for start in range(0, SPAN, SUB):
            s = dot(kext[sub * SUB + start : sub * SUB + start + SUB, :], q)
            if start + SUB == SPAN:
                s = s + later
            s_ref[pair % 2, sub, start : start + SUB, :] = s
            top = jnp.maximum(top, jnp.max(s.reshape(SUB // 8, 8, 256), axis=0))
            yield
        shifts[pair, sub] = jnp.max(top, axis=0, keepdims=True) * EXP2

    def weights(pair, sub):
        slot = pair % 2
        shift = shifts[pair, sub]
        total = jnp.zeros((8, 256), jnp.float32)
        for c in range(CHUNKS):
            e = jnp.exp2(s_ref[slot, sub, c * SUB : (c + 1) * SUB, :] * EXP2 - shift)
            s_ref[slot, sub, c * SUB : (c + 1) * SUB, :] = e
            total = total + jnp.sum(e.reshape(SUB // 8, 8, 256), axis=0)
            yield
        inverse = 1.0 / jnp.sum(total, axis=0, keepdims=True)
        for c in range(CHUNKS):
            keys = slice((sub + c) * SUB, (sub + c + 1) * SUB)
            w = s_ref[slot, sub, c * SUB : (c + 1) * SUB, :] * inverse
            w_ref[slot, keys, columns_of[sub]] = w.astype(jnp.bfloat16)
            yield

    def attend(pair, sub):
        att_t = dot(v_t[:, spans[sub]], w_ref[pair % 2, spans[sub], columns_of[sub]])
        d_t = dcat_t[pair, :, columns_of[sub]]
        centers[pair, sub] = jnp.sum(att_t * d_t.astype(jnp.float32), axis=0, keepdims=True)
        yield
        tokens = slice(sub * SUB, (sub + 1) * SUB)
        for g in range(2):
            columns = slice(pair * 256 + g * HEAD, pair * 256 + (g + 1) * HEAD)
            att_ref[tokens, columns] = att_t[:, g * SUB : (g + 1) * SUB].T.astype(jnp.bfloat16)
            yield

    def score_terms(pair, sub):
        slot = pair % 2
        d_t = dcat_t[pair, :, columns_of[sub]]
        center = centers[pair, sub]
        for c in range(CHUNKS):
            keys = slice((sub + c) * SUB, (sub + c + 1) * SUB)
            dw = dot(vwin[keys, :], d_t)
            w = w_ref[slot, keys, columns_of[sub]].astype(jnp.float32)
            ds_ref[slot, keys, columns_of[sub]] = (w * (dw - center)).astype(jnp.bfloat16)
            yield

    def query_terms(pair, sub):
        dq_t = dot(khat_t[:, spans[sub]], ds_ref[pair % 2, spans[sub], columns_of[sub]]) * SCALING
        yield
        tokens = slice(sub * SUB, (sub + 1) * SUB)
        window_rows = slice(REACH * TOK + sub * SUB, REACH * TOK + (sub + 1) * SUB)
        c_q = cosine[window_rows, :]
        s_q = sine[window_rows, :]
        for g in range(2):
            columns = slice(pair * 256 + g * HEAD, pair * 256 + (g + 1) * HEAD)
            at = pair * 512 + sub * 256 + g * SUB
            rows = slice(at, at + SUB)
            dq = dq_t[:, g * SUB : (g + 1) * SUB].T
            xh = xh_ref[rows, :]
            dn = dq * c_q - half_turned(dq) * s_q
            qg_acc[...] += jnp.sum((dn * xh).reshape(SUB // 8, 8, HEAD), axis=0)
            dxh = dn * q_gain
            gq = scale_ref[rows, :] * (dxh - xh * jnp.mean(dxh * xh, axis=1, keepdims=True))
            gq_ref[tokens, columns] = gq.astype(jnp.bfloat16)
            yield

    def key_terms(pair):
        for start, stop, low, high in KEY_BLOCKS:
            keys, lanes = slice(start, stop), slice(low, high)
            rows = slice(pair * 512 + low, pair * 512 + high)
            dk[keys, :] += dot(ds_ref[pair % 2, keys, lanes], qhat[rows, :])
            yield
            dv[keys, :] += dot(w_ref[pair % 2, keys, lanes], dcat[rows, :])
            yield

    def in_turn(*streams):
        for stream in streams:
            yield from stream

    def weave(first, second):
        first, second = iter(first), iter(second)
        done = object()
        while True:
            ends = [next(first, done) is done, next(second, done) is done]
            if all(ends):
                return

    chains = [(pair, sub) for pair in range(HEADS // 2) for sub in range(2)]
    weave(scores(*chains[0]), ())
    for i, (pair, sub) in enumerate(chains):
        ahead, behind = [], []
        if i + 1 < len(chains):
            ahead.append(scores(*chains[i + 1]))
        if i > 0:
            behind.append(query_terms(*chains[i - 1]))
        if sub == 0 and pair > 0:
            behind.append(key_terms(pair - 1))
        weave(weights(pair, sub), in_turn(*ahead, *behind[:1]))
        weave(attend(pair, sub), ())
        weave(score_terms(pair, sub), in_turn(*behind[1:]))
        if sub == 0 and pair > 0:
            for copy in copies(pair - 1):
                copy.start()
    last = HEADS // 2 - 1
    weave(query_terms(last, 1), key_terms(last))
    for copy in copies(last):
        copy.start()

    kg = jnp.zeros((8, HEAD), jnp.float32)
    outs = ((four_ref, 0), (swap_ref, 2 * TOK), (two_ref, 0), (swap_ref, 0), (own_ref, 0))
    for j in range(parts):
        rows = slice(j * SUB, (j + 1) * SUB)
        here = slice((j % 2) * SUB, (j % 2 + 1) * SUB)
        x = blocks[j // 2][here, :].astype(jnp.float32)
        r = lax.rsqrt(jnp.mean(x * x, axis=1, keepdims=True) + EPSILON)
        xh = x * r
        d = dk[rows, :] * SCALING
        dn = d * cosine[rows, :] - half_turned(d) * sine[rows, :]
        kg = kg + jnp.sum((dn * xh).reshape(SUB // 8, 8, HEAD), axis=0)
        dxh = dn * k_gain
        gk = r * (dxh - xh * jnp.mean(dxh * xh, axis=1, keepdims=True))
        out, at = outs[j // 2]
        at = at + (j % 2) * SUB
        out[at : at + SUB, :] = gk.astype(out.dtype)
        out[at + TOK : at + TOK + SUB, :] = dv[rows, :].astype(out.dtype)
    gains = jnp.concatenate(
        [jnp.sum(qg_acc[...], axis=0, keepdims=True), jnp.sum(kg, axis=0, keepdims=True)]
    )
    gain_ref[...] = gains
    high = gains.astype(jnp.bfloat16).astype(jnp.float32)
    middle = (gains - high).astype(jnp.bfloat16).astype(jnp.float32)
    low = gains - high - middle
    swap_ref[4 * TOK :, :] = jnp.concatenate(
        [high, middle, low, jnp.zeros((ID_ROWS - 6, HEAD), jnp.float32)]
    ).astype(jnp.bfloat16)
    for pair in range(HEADS // 2):
        for copy in copies(pair):
            copy.wait()


def attention(blocks, prepared, frequency):
    vmem = pl.BlockSpec(memory_space=pltpu.VMEM)
    hbm = pl.BlockSpec(memory_space=pl.ANY)
    f32, bf16 = jnp.float32, jnp.bfloat16
    shape = jax.ShapeDtypeStruct
    return pl.pallas_call(
        kernel,
        out_shape=[
            shape((TOK, HEADS * HEAD), bf16),
            shape((TOK, HEADS * HEAD), bf16),
            shape((2 * TOK, HEAD), f32),
            shape((2 * TOK, HEAD), f32),
            shape((2 * TOK, HEAD), f32),
            shape((4 * TOK + ID_ROWS, HEAD), bf16),
            shape((2, HEAD), f32),
        ],
        in_specs=[vmem] * 12,
        out_specs=[hbm] * 2 + [vmem] * 5,
        scratch_shapes=[
            pltpu.VMEM((TOK, HEADS * HEAD), bf16),
            pltpu.VMEM((TOK, HEADS * HEAD), bf16),
            pltpu.VMEM((WINDOW, HEAD), f32),
            pltpu.VMEM((WINDOW, HEAD), f32),
            pltpu.VMEM((WINDOW, 2 * HEAD), bf16),
            pltpu.VMEM((WINDOW, HEAD), bf16),
            pltpu.VMEM((HEAD, WINDOW), bf16),
            pltpu.VMEM((HEAD, WINDOW), bf16),
            pltpu.VMEM((HEADS * TOK, HEAD), bf16),
            pltpu.VMEM((HEADS // 2, 2 * HEAD, 512), bf16),
            pltpu.VMEM((2, 2, SPAN, 256), f32),
            pltpu.VMEM((2, WINDOW, 512), bf16),
            pltpu.VMEM((2, WINDOW, 512), bf16),
            pltpu.VMEM((WINDOW, HEAD), f32),
            pltpu.VMEM((WINDOW, HEAD), f32),
            pltpu.VMEM((8, HEAD), f32),
            pltpu.VMEM((MSG, HEAD), bf16),
            pltpu.VMEM((MSG, HEAD), bf16),
            pltpu.SemaphoreType.DMA((HEADS // 2,)),
            pltpu.SemaphoreType.DMA((HEADS // 2,)),
        ],
        compiler_params=pltpu.CompilerParams(vmem_limit_bytes=40 * 1024 * 1024),
    )(*blocks, *prepared, frequency)


def pack_kernel(keys, values, ids, out):
    out[0:TOK, :] = keys[...]
    out[TOK : 2 * TOK, :] = values[...]
    marked = (ids[...] + 1).astype(jnp.float32)
    out[2 * TOK :, :] = jnp.concatenate(
        [marked, jnp.zeros((ID_ROWS - 2, HEAD), jnp.float32)]
    ).astype(jnp.bfloat16)


def pack(keys, values, ids):
    vmem = pl.BlockSpec(memory_space=pltpu.VMEM)
    return pl.pallas_call(
        pack_kernel,
        out_shape=jax.ShapeDtypeStruct((MSG, HEAD), jnp.bfloat16),
        in_specs=[vmem] * 3,
        out_specs=vmem,
    )(keys, values, ids)


def swapped(block, ways=(0, 1)):
    route = [(i, i ^ 1) for i in range(lax.axis_size("context")) if i % 2 in ways]
    return lax.ppermute(block, "context", route)


def chip_kernel(swap, four, two, own, gains, four_out, two_out, own_out, gains_out):
    even = lax.rem(lax.axis_index("context"), 2) == 0
    one, three = slice(0, 2 * TOK), slice(2 * TOK, 4 * TOK)

    @pl.when(even)
    def _():
        four_out[...] = four[...].astype(jnp.bfloat16)
        two_out[...] = two[...] + swap[three, :].astype(jnp.float32)
        own_out[...] = own[...] + swap[one, :].astype(jnp.float32)

    @pl.when(jnp.logical_not(even))
    def _():
        four_out[...] = (four[...] + swap[three, :].astype(jnp.float32)).astype(jnp.bfloat16)
        two_out[...] = two[...] + swap[one, :].astype(jnp.float32)
        own_out[...] = own[...]

    split = swap[4 * TOK :, :].astype(jnp.float32)
    total = gains[...] + ((split[0:2] + split[2:4]) + split[4:6])
    gains_out[...] = jnp.concatenate([total] * (gains_out.shape[0] // 2))


def hop_kernel(two, hop, two_out):
    two_out[...] = (two[...] + hop[...].astype(jnp.float32)).astype(jnp.bfloat16)


def last_kernel(own, hop, terms, keys, values, q_gain, k_gain):
    total = (own[...] + hop[...].astype(jnp.float32)).astype(jnp.bfloat16)
    keys[...] = total[:TOK]
    values[...] = total[TOK:]
    gains = jnp.sum(terms[...].reshape(-1, 8, HEAD), axis=0)
    q_gain[...] = (gains[0:1] + gains[2:3]) + (gains[4:5] + gains[6:7])
    k_gain[...] = (gains[1:2] + gains[3:4]) + (gains[5:6] + gains[7:8])


def small_call(kernel, out_shape, *operands):
    vmem = pl.BlockSpec(memory_space=pltpu.VMEM)
    return pl.pallas_call(
        kernel,
        out_shape=[jax.ShapeDtypeStruct(shape, dtype) for shape, dtype in out_shape],
        in_specs=[vmem] * len(operands),
        out_specs=[vmem] * len(out_shape),
        compiler_params=pltpu.CompilerParams(vmem_limit_bytes=16 * 1024 * 1024),
    )(*operands)


def body(queries, keys, values, output_gradient, q_gain, k_gain, doc_ids):
    f32, bf16 = jnp.float32, jnp.bfloat16
    message = pack(keys, values, doc_ids.reshape(2, HEAD))
    two = passed_along(message, "context", 2)
    first_swap = swapped(message, (0,))
    four = passed_along(message, "context", 4)
    prepared = prepare(queries, output_gradient, q_gain.reshape(1, HEAD), k_gain.reshape(1, HEAD))
    two, *prepared = lax.optimization_barrier((two, *prepared))
    middle_swap = swapped(two)
    last_swap = swapped(four, (1,))
    blocks = [four, two, message, first_swap, middle_swap, last_swap]
    half = jnp.arange(HEAD // 2, dtype=jnp.float32)
    frequency = THETA ** (-(half * 2.0 / HEAD))
    frequency = jnp.concatenate([frequency, frequency]).reshape(1, HEAD)
    attended, query_gradient, four, two, own, swap, gains = attention(blocks, prepared, frequency)

    axes = ("context", "tensor")
    chips = lax.axis_size(axes) // 2
    block = (2 * TOK, HEAD)
    four, two, own, gains = small_call(
        chip_kernel,
        [(block, bf16), (block, f32), (block, f32), ((2 * chips, HEAD), f32)],
        *(swapped(swap), four, two, own, gains),
    )
    hop = passed_along(four, "context", -2)
    width = lax.axis_size("tensor")
    cores = [
        [(2 * n + core) * width + z for n in range(chips // width) for z in range(width)]
        for core in range(2)
    ]
    gains = lax.all_to_all(gains.reshape(chips, 2, HEAD), axes, 0, 0, axis_index_groups=cores)
    gains = gains.reshape(2 * chips, HEAD)
    (two,) = small_call(hop_kernel, [(block, bf16)], two, hop)
    hop = passed_along(two, "context", -2)
    half_block = (TOK, HEAD)
    key_gradient, value_gradient, q_total, k_total = small_call(
        last_kernel,
        [(half_block, bf16), (half_block, bf16), ((1, HEAD), f32), ((1, HEAD), f32)],
        *(own, hop, gains),
    )
    return (
        attended,
        query_gradient,
        key_gradient,
        value_gradient,
        q_total.reshape(HEAD),
        k_total.reshape(HEAD),
    )


def solution(mesh):
    placed = (
        P("context", "tensor"),
        P("context", "tensor"),
        P("context", "tensor"),
        P("context", "tensor"),
        P(),
        P(),
        P("context"),
    )
    return jax.shard_map(
        body,
        mesh=mesh,
        in_specs=placed,
        out_specs=(
            P("context", "tensor"),
            P("context", "tensor"),
            P("context", "tensor"),
            P("context", "tensor"),
            P(),
            P(),
        ),
        check_vma=False,
    )
```

```python
import jax
import jax.numpy as jnp
import numpy as np
from jax import lax
from jax.experimental import pallas as pl
from jax.experimental.pallas import tpu as pltpu
from jax.sharding import PartitionSpec as P

REACH = 4
THETA = 500000.0
EPSILON = 1e-06
TOK = 256
HEAD = 128
HEADS = 8
WINDOW = (REACH + 1) * TOK
SUB = 128
SPAN = 1152
CHUNKS = SPAN // SUB
FINE = 64
KEY_BLOCKS = (
    [(0, SUB, 0, 256)]
    + [(start, start + 256, 0, 512) for start in range(SUB, SPAN, 256)]
    + [(SPAN, WINDOW, 256, 512)]
)
ID_ROWS = 16
MSG = 2 * TOK + ID_ROWS
SCALING = HEAD ** (-0.5)
EXP2 = float(SCALING * np.log2(np.e))

PI_A = 3.140625
PI_B = float(np.round((np.pi - PI_A) * 2.0**23) / 2.0**23)
PI_C = float(np.pi - PI_A - PI_B)


def passed_along(block, axis, distance):
    devices = range(lax.axis_size(axis))
    route = [(i - distance, i) for i in devices if i - distance in devices]
    return lax.ppermute(block, axis, route)


def dot(a, b):
    return jnp.dot(a, b, preferred_element_type=jnp.float32)


def half_turned(x):
    return pltpu.roll(x, HEAD // 2, 1)


def cos_sin(position, frequency):
    angle = position * frequency
    lane = lax.broadcasted_iota(jnp.int32, (1, HEAD), 1)
    quarter = jnp.where(lane < HEAD // 2, 0.5, 0.0)
    turns = jnp.floor(angle * np.float32(1.0 / np.pi) + (quarter + 0.5))
    count = turns - quarter
    rest = ((angle - count * PI_A) - count * PI_B) - count * PI_C
    square = rest * rest
    series = np.float32(-1.9806614727713168e-4) + square * np.float32(2.6000534489867277e-6)
    series = np.float32(8.333017118275166e-3) + square * series
    series = np.float32(-1.6666656732559204e-1) + square * series
    value = rest + rest * (square * series)
    return jnp.where((turns.astype(jnp.int32) & 1) == 1, -value, value)


def prepare_kernel(q_ref, d_ref, qg_ref, kg_ref, xh_ref, scale_ref, dcat, dcat_t, gains):
    gains[0:1, :] = qg_ref[...]
    gains[1:2, :] = kg_ref[...]
    for sub in range(2):
        tokens = slice(sub * SUB, (sub + 1) * SUB)
        for h in range(HEADS):
            at = (h // 2) * 512 + sub * 256 + (h % 2) * SUB
            rows = slice(at, at + SUB)
            x = q_ref[tokens, h * HEAD : (h + 1) * HEAD].astype(jnp.float32)
            r = lax.rsqrt(jnp.mean(x * x, axis=1, keepdims=True) + EPSILON)
            xh_ref[rows, :] = x * r
            scale_ref[rows, :] = jnp.broadcast_to(r, (SUB, HEAD))
            d = d_ref[tokens, h * HEAD : (h + 1) * HEAD]
            dcat[rows, :] = d
            dcat_t[h // 2, :, at % 512 : at % 512 + SUB] = d.astype(jnp.float32).T.astype(jnp.bfloat16)


def prepare(queries, output_gradient, q_gain, k_gain):
    vmem = pl.BlockSpec(memory_space=pltpu.VMEM)
    f32, bf16 = jnp.float32, jnp.bfloat16
    shape = jax.ShapeDtypeStruct
    return pl.pallas_call(
        prepare_kernel,
        out_shape=[
            shape((HEADS * TOK, HEAD), f32),
            shape((HEADS * TOK, HEAD), f32),
            shape((HEADS * TOK, HEAD), bf16),
            shape((HEADS // 2, HEAD, 512), bf16),
            shape((2, HEAD), f32),
        ],
        in_specs=[vmem] * 4,
        out_specs=[vmem] * 5,
        compiler_params=pltpu.CompilerParams(vmem_limit_bytes=16 * 1024 * 1024),
        cost_estimate=pl.CostEstimate(flops=10**9, bytes_accessed=4 * 2**20, transcendentals=0),
    )(queries, output_gradient, q_gain, k_gain)


def kernel(
    b4, b2, b0, first_swap, middle_swap, last_swap, xh_ref, scale_ref, dcat, dcat_t, gains_ref, f_ref,
    att_hbm, gq_hbm, four_ref, two_ref, own_ref, swap_ref, gain_ref,
    att_ref, gq_ref, cosine, sine, kext, vwin, khat_t, v_t, qhat, qext_t,
    s_ref, w_ref, ds_ref, dk, dv, qg_acc, b3, b1, att_sem, gq_sem,
):
    even = lax.rem(lax.axis_index("context"), 2) == 0

    @pl.when(even)
    def _():
        b3[...] = last_swap[...]
        b1[...] = middle_swap[...]

    @pl.when(jnp.logical_not(even))
    def _():
        b3[...] = middle_swap[...]
        b1[...] = first_swap[...]

    blocks = (b4, b3, b2, b1, b0)
    lane = lax.broadcasted_iota(jnp.int32, (SUB, HEAD), 1)
    row = lax.broadcasted_iota(jnp.int32, (SUB, HEAD), 0)
    lane_f = lane.astype(jnp.float32)
    row_f = row.astype(jnp.float32)
    left = lane < HEAD // 2
    parts = WINDOW // SUB
    q_gain = gains_ref[0:1, :]
    k_gain = gains_ref[1:2, :]
    frequency = f_ref[...]

    id_rows = []
    for block in blocks:
        both = block[2 * TOK : MSG, :].astype(jnp.float32)
        id_rows += [both[0:1], both[1:2]]
    below = jnp.zeros((SUB, HEAD), jnp.float32)
    for j in range(parts):
        column = jnp.broadcast_to(id_rows[j], (SUB, HEAD)).T
        kext[j * SUB : (j + 1) * SUB, HEAD:] = jnp.where(column == lane_f, 1.0, 0.0).astype(jnp.bfloat16)
        below = below + jnp.where(column < lane_f, 1.0, 0.0)
    first = jnp.sum(below, axis=0, keepdims=True)

    for j in range(parts):
        rows = slice(j * SUB, (j + 1) * SUB)
        here = slice((j % 2) * SUB, (j % 2 + 1) * SUB)
        block = blocks[j // 2]
        member = kext[rows, HEAD:].astype(jnp.float32)
        start = jnp.sum(member * first, axis=1, keepdims=True)
        position = (row + j * SUB).astype(jnp.float32) - start
        both = cos_sin(position, frequency)
        turned = half_turned(both)
        c = jnp.where(left, both, turned)
        s = jnp.where(left, -turned, both)
        cosine[rows, :] = c
        sine[rows, :] = s
        x = block[here, :].astype(jnp.float32)
        normed = x * lax.rsqrt(jnp.mean(x * x, axis=1, keepdims=True) + EPSILON) * k_gain
        hat = normed * c + half_turned(normed) * s
        kext[rows, 0:HEAD] = hat.astype(jnp.bfloat16)
        khat_t[:, rows] = hat.T.astype(jnp.bfloat16)
        values = block[TOK + (j % 2) * SUB : TOK + (j % 2 + 1) * SUB, :]
        vwin[rows, :] = values
        v_t[:, rows] = values.astype(jnp.float32).T.astype(jnp.bfloat16)

    for sub in range(2):
        window_rows = slice(REACH * TOK + sub * SUB, REACH * TOK + (sub + 1) * SUB)
        c_q = cosine[window_rows, :]
        s_q = sine[window_rows, :]
        other = jnp.where(row_f == id_rows[2 * REACH + sub], 0.0, -1e30).astype(jnp.bfloat16)
        for h in range(HEADS):
            at = (h // 2) * 512 + sub * 256 + (h % 2) * SUB
            lanes = slice(at % 512, at % 512 + SUB)
            normed = xh_ref[at : at + SUB, :] * q_gain
            hat = normed * c_q + half_turned(normed) * s_q
            qhat[at : at + SUB, :] = hat.astype(jnp.bfloat16)
            qext_t[h // 2, 0:HEAD, lanes] = hat.T.astype(jnp.bfloat16)
            qext_t[h // 2, HEAD:, lanes] = other

    dk[...] = jnp.zeros_like(dk)
    dv[...] = jnp.zeros_like(dv)
    qg_acc[...] = jnp.zeros_like(qg_acc)
    later = jnp.where(row <= lane, 0.0, -1e30)
    later = jnp.concatenate([later, later], axis=1)
    spans = (slice(0, SPAN), slice(SUB, WINDOW))
    columns_of = (slice(0, 256), slice(256, 512))

    def copies(pair):
        columns = slice(pair * 256, (pair + 1) * 256)
        return (
            pltpu.make_async_copy(att_ref.at[:, columns], att_hbm.at[:, columns], att_sem.at[pair]),
            pltpu.make_async_copy(gq_ref.at[:, columns], gq_hbm.at[:, columns], gq_sem.at[pair]),
        )

    shifts, inverses, centers, queries_t = {}, {}, {}, {}

    def scores(pair, sub):
        q = qext_t[pair, :, columns_of[sub]]
        top = jnp.full((8, 256), -1e30, jnp.float32)
        for start in range(0, SPAN, SUB):
            s = dot(kext[sub * SUB + start : sub * SUB + start + SUB, :], q)
            if start + SUB == SPAN:
                s = s + later
            s_ref[pair % 2, sub, start : start + SUB, :] = s
            top = jnp.maximum(top, jnp.max(s.reshape(SUB // 8, 8, 256), axis=0))
            yield
        shifts[pair, sub] = jnp.max(top, axis=0, keepdims=True) * EXP2

    def exponents(pair, sub):
        slot = pair % 2
        shift = shifts[pair, sub]
        total = jnp.zeros((8, 256), jnp.float32)
        for at in range(0, SPAN, FINE):
            rows = slice(at, at + FINE)
            e = jnp.exp2(s_ref[slot, sub, rows, :] * EXP2 - shift)
            s_ref[slot, sub, rows, :] = e
            total = total + jnp.sum(e.reshape(FINE // 8, 8, 256), axis=0)
            yield
        inverses[pair, sub] = 1.0 / jnp.sum(total, axis=0, keepdims=True)

    def weights(pair, sub):
        inverse = inverses[pair, sub]
        for at in range(0, SPAN, FINE):
            w = s_ref[pair % 2, sub, at : at + FINE, :] * inverse
            keys = slice(sub * SUB + at, sub * SUB + at + FINE)
            w_ref[pair % 2, keys, columns_of[sub]] = w.astype(jnp.bfloat16)
            yield

    def attend(pair, sub):
        att_t = dot(v_t[:, spans[sub]], w_ref[pair % 2, spans[sub], columns_of[sub]])
        d_t = dcat_t[pair, :, columns_of[sub]]
        centers[pair, sub] = jnp.sum(att_t * d_t.astype(jnp.float32), axis=0, keepdims=True)
        yield
        tokens = slice(sub * SUB, (sub + 1) * SUB)
        for g in range(2):
            columns = slice(pair * 256 + g * HEAD, pair * 256 + (g + 1) * HEAD)
            att_ref[tokens, columns] = att_t[:, g * SUB : (g + 1) * SUB].T.astype(jnp.bfloat16)
            yield

    def score_terms(pair, sub):
        slot = pair % 2
        d_t = dcat_t[pair, :, columns_of[sub]]
        center = centers[pair, sub]
        for c in range(CHUNKS):
            keys = slice((sub + c) * SUB, (sub + c + 1) * SUB)
            dw = dot(vwin[keys, :], d_t)
            w = w_ref[slot, keys, columns_of[sub]].astype(jnp.float32)
            ds_ref[slot, keys, columns_of[sub]] = (w * (dw - center)).astype(jnp.bfloat16)
            yield

    def query_sums(pair, sub):
        dq_t = dot(khat_t[:, spans[sub]], ds_ref[pair % 2, spans[sub], columns_of[sub]])
        queries_t[pair, sub] = dq_t * SCALING
        yield

    def query_terms(pair, sub):
        dq_t = queries_t[pair, sub]
        tokens = slice(sub * SUB, (sub + 1) * SUB)
        window_rows = slice(REACH * TOK + sub * SUB, REACH * TOK + (sub + 1) * SUB)
        c_q = cosine[window_rows, :]
        s_q = sine[window_rows, :]
        for g in range(2):
            columns = slice(pair * 256 + g * HEAD, pair * 256 + (g + 1) * HEAD)
            at = pair * 512 + sub * 256 + g * SUB
            rows = slice(at, at + SUB)
            dq = dq_t[:, g * SUB : (g + 1) * SUB].T
            xh = xh_ref[rows, :]
            dn = dq * c_q - half_turned(dq) * s_q
            qg_acc[...] += jnp.sum((dn * xh).reshape(SUB // 8, 8, HEAD), axis=0)
            dxh = dn * q_gain
            gq = scale_ref[rows, :] * (dxh - xh * jnp.mean(dxh * xh, axis=1, keepdims=True))
            gq_ref[tokens, columns] = gq.astype(jnp.bfloat16)
            yield

    def key_terms(pair):
        for start, stop, low, high in KEY_BLOCKS:
            keys, lanes = slice(start, stop), slice(low, high)
            rows = slice(pair * 512 + low, pair * 512 + high)
            dk[keys, :] += dot(ds_ref[pair % 2, keys, lanes], qhat[rows, :])
            yield
            dv[keys, :] += dot(w_ref[pair % 2, keys, lanes], dcat[rows, :])
            yield

    def first_of(stream, count):
        for _ in range(count):
            if next(stream, stop) is stop:
                return
            yield

    def weave(*streams):
        streams = [iter(stream) for stream in streams]
        while streams:
            streams = [stream for stream in streams if next(stream, stop) is not stop]

    stop = object()
    chains = [(pair, sub) for pair in range(HEADS // 2) for sub in range(2)]
    keys_before = iter(())
    weave(scores(*chains[0]))
    for i, (pair, sub) in enumerate(chains):
        if sub == 0 and pair > 0:
            keys_before = key_terms(pair - 1)
        ahead = [scores(*chains[i + 1])] if i + 1 < len(chains) else []
        weave(exponents(pair, sub), *ahead)
        behind = [query_sums(*chains[i - 1])] if i > 0 else []
        weave(weights(pair, sub), *behind, first_of(keys_before, 3))
        behind = [query_terms(*chains[i - 1])] if i > 0 else []
        weave(attend(pair, sub), *behind)
        weave(score_terms(pair, sub), first_of(keys_before, 3))
        if sub == 0 and pair > 0:
            for copy in copies(pair - 1):
                copy.start()
    last = HEADS // 2 - 1
    weave(query_sums(last, 1))

    outs = ((four_ref, 0), (swap_ref, 2 * TOK), (two_ref, 0), (swap_ref, 0), (own_ref, 0))
    k_sums = [jnp.zeros((8, HEAD), jnp.float32)]

    def key_ends(j):
        rows = slice(j * SUB, (j + 1) * SUB)
        here = slice((j % 2) * SUB, (j % 2 + 1) * SUB)
        x = blocks[j // 2][here, :].astype(jnp.float32)
        r = lax.rsqrt(jnp.mean(x * x, axis=1, keepdims=True) + EPSILON)
        xh = x * r
        d = dk[rows, :] * SCALING
        dn = d * cosine[rows, :] - half_turned(d) * sine[rows, :]
        k_sums[0] = k_sums[0] + jnp.sum((dn * xh).reshape(SUB // 8, 8, HEAD), axis=0)
        dxh = dn * k_gain
        gk = r * (dxh - xh * jnp.mean(dxh * xh, axis=1, keepdims=True))
        out, at = outs[j // 2]
        at = at + (j % 2) * SUB
        out[at : at + SUB, :] = gk.astype(out.dtype)
        out[at + TOK : at + TOK + SUB, :] = dv[rows, :].astype(out.dtype)

    def all_key_ends():
        yield
        yield
        yield
        key_ends(0)
        yield
        for j in range(1, parts - 1):
            key_ends(j)
            yield

    weave(key_terms(last), all_key_ends(), query_terms(last, 1))
    key_ends(parts - 1)
    for copy in copies(last):
        copy.start()
    kg = k_sums[0]
    gains = jnp.concatenate(
        [jnp.sum(qg_acc[...], axis=0, keepdims=True), jnp.sum(kg, axis=0, keepdims=True)]
    )
    gain_ref[...] = gains
    high = gains.astype(jnp.bfloat16).astype(jnp.float32)
    middle = (gains - high).astype(jnp.bfloat16).astype(jnp.float32)
    low = gains - high - middle
    swap_ref[4 * TOK :, :] = jnp.concatenate(
        [high, middle, low, jnp.zeros((ID_ROWS - 6, HEAD), jnp.float32)]
    ).astype(jnp.bfloat16)
    for pair in range(HEADS // 2):
        for copy in copies(pair):
            copy.wait()


def attention(blocks, prepared, frequency):
    vmem = pl.BlockSpec(memory_space=pltpu.VMEM)
    hbm = pl.BlockSpec(memory_space=pl.ANY)
    f32, bf16 = jnp.float32, jnp.bfloat16
    shape = jax.ShapeDtypeStruct
    return pl.pallas_call(
        kernel,
        out_shape=[
            shape((TOK, HEADS * HEAD), bf16),
            shape((TOK, HEADS * HEAD), bf16),
            shape((2 * TOK, HEAD), f32),
            shape((2 * TOK, HEAD), f32),
            shape((2 * TOK, HEAD), f32),
            shape((4 * TOK + ID_ROWS, HEAD), bf16),
            shape((2, HEAD), f32),
        ],
        in_specs=[vmem] * 12,
        out_specs=[hbm] * 2 + [vmem] * 5,
        scratch_shapes=[
            pltpu.VMEM((TOK, HEADS * HEAD), bf16),
            pltpu.VMEM((TOK, HEADS * HEAD), bf16),
            pltpu.VMEM((WINDOW, HEAD), f32),
            pltpu.VMEM((WINDOW, HEAD), f32),
            pltpu.VMEM((WINDOW, 2 * HEAD), bf16),
            pltpu.VMEM((WINDOW, HEAD), bf16),
            pltpu.VMEM((HEAD, WINDOW), bf16),
            pltpu.VMEM((HEAD, WINDOW), bf16),
            pltpu.VMEM((HEADS * TOK, HEAD), bf16),
            pltpu.VMEM((HEADS // 2, 2 * HEAD, 512), bf16),
            pltpu.VMEM((2, 2, SPAN, 256), f32),
            pltpu.VMEM((2, WINDOW, 512), bf16),
            pltpu.VMEM((2, WINDOW, 512), bf16),
            pltpu.VMEM((WINDOW, HEAD), f32),
            pltpu.VMEM((WINDOW, HEAD), f32),
            pltpu.VMEM((8, HEAD), f32),
            pltpu.VMEM((MSG, HEAD), bf16),
            pltpu.VMEM((MSG, HEAD), bf16),
            pltpu.SemaphoreType.DMA((HEADS // 2,)),
            pltpu.SemaphoreType.DMA((HEADS // 2,)),
        ],
        compiler_params=pltpu.CompilerParams(vmem_limit_bytes=40 * 1024 * 1024),
    )(*blocks, *prepared, frequency)


def pack_kernel(keys, values, ids, out, marks, sems):
    parts = ((keys, 0, TOK), (values, TOK, TOK), (marks, 2 * TOK, ID_ROWS))
    moves = [
        pltpu.make_async_copy(part, out.at[pl.ds(at, size)], sems.at[i])
        for i, (part, at, size) in enumerate(parts)
    ]
    moves[0].start()
    moves[1].start()
    marked = (ids[...] + 1).astype(jnp.float32)
    rest = jnp.zeros((ID_ROWS - 2, HEAD), jnp.float32)
    marks[...] = jnp.concatenate([marked, rest]).astype(jnp.bfloat16)
    moves[2].start()
    for move in moves:
        move.wait()


def pack(keys, values, ids):
    anywhere = pl.BlockSpec(memory_space=pl.ANY)
    return pl.pallas_call(
        pack_kernel,
        out_shape=jax.ShapeDtypeStruct((MSG, HEAD), jnp.bfloat16),
        in_specs=[anywhere, anywhere, pl.BlockSpec(memory_space=pltpu.VMEM)],
        out_specs=anywhere,
        scratch_shapes=[pltpu.VMEM((ID_ROWS, HEAD), jnp.bfloat16), pltpu.SemaphoreType.DMA((3,))],
    )(keys, values, ids)


def swapped(block, ways=(0, 1)):
    route = [(i, i ^ 1) for i in range(lax.axis_size("context")) if i % 2 in ways]
    return lax.ppermute(block, "context", route)


def chip_kernel(swap, four, two, own, gains, four_out, two_out, own_out, gains_out):
    even = lax.rem(lax.axis_index("context"), 2) == 0
    one, three = slice(0, 2 * TOK), slice(2 * TOK, 4 * TOK)

    @pl.when(even)
    def _():
        four_out[...] = four[...].astype(jnp.bfloat16)
        two_out[...] = two[...] + swap[three, :].astype(jnp.float32)
        own_out[...] = own[...] + swap[one, :].astype(jnp.float32)

    @pl.when(jnp.logical_not(even))
    def _():
        four_out[...] = (four[...] + swap[three, :].astype(jnp.float32)).astype(jnp.bfloat16)
        two_out[...] = two[...] + swap[one, :].astype(jnp.float32)
        own_out[...] = own[...]

    split = swap[4 * TOK :, :].astype(jnp.float32)
    total = gains[...] + ((split[0:2] + split[2:4]) + split[4:6])
    gains_out[...] = jnp.concatenate([total] * (gains_out.shape[0] // 2))


def hop_kernel(two, hop, two_out):
    two_out[...] = (two[...] + hop[...].astype(jnp.float32)).astype(jnp.bfloat16)


def last_kernel(own, hop, terms, keys, values, q_gain, k_gain):
    total = (own[...] + hop[...].astype(jnp.float32)).astype(jnp.bfloat16)
    keys[...] = total[:TOK]
    values[...] = total[TOK:]
    gains = jnp.sum(terms[...].reshape(-1, 8, HEAD), axis=0)
    q_gain[...] = (gains[0:1] + gains[2:3]) + (gains[4:5] + gains[6:7])
    k_gain[...] = (gains[1:2] + gains[3:4]) + (gains[5:6] + gains[7:8])


def small_call(kernel, out_shape, *operands):
    vmem = pl.BlockSpec(memory_space=pltpu.VMEM)
    return pl.pallas_call(
        kernel,
        out_shape=[jax.ShapeDtypeStruct(shape, dtype) for shape, dtype in out_shape],
        in_specs=[vmem] * len(operands),
        out_specs=[vmem] * len(out_shape),
        compiler_params=pltpu.CompilerParams(vmem_limit_bytes=16 * 1024 * 1024),
    )(*operands)


def body(queries, keys, values, output_gradient, q_gain, k_gain, doc_ids):
    f32, bf16 = jnp.float32, jnp.bfloat16
    message = pack(keys, values, doc_ids.reshape(2, HEAD))
    two = passed_along(message, "context", 2)
    first_swap = swapped(message, (0,))
    four = passed_along(message, "context", 4)
    prepared = prepare(queries, output_gradient, q_gain.reshape(1, HEAD), k_gain.reshape(1, HEAD))
    two, *prepared = lax.optimization_barrier((two, *prepared))
    middle_swap = swapped(two)
    last_swap = swapped(four, (1,))
    blocks = [four, two, message, first_swap, middle_swap, last_swap]
    half = jnp.arange(HEAD // 2, dtype=jnp.float32)
    frequency = THETA ** (-(half * 2.0 / HEAD))
    frequency = jnp.concatenate([frequency, frequency]).reshape(1, HEAD)
    attended, query_gradient, four, two, own, swap, gains = attention(blocks, prepared, frequency)

    axes = ("context", "tensor")
    chips = lax.axis_size(axes) // 2
    block = (2 * TOK, HEAD)
    four, two, own, gains = small_call(
        chip_kernel,
        [(block, bf16), (block, f32), (block, f32), ((2 * chips, HEAD), f32)],
        *(swapped(swap), four, two, own, gains),
    )
    hop = passed_along(four, "context", -2)
    width = lax.axis_size("tensor")
    cores = [
        [(2 * n + core) * width + z for n in range(chips // width) for z in range(width)]
        for core in range(2)
    ]
    gains = lax.all_to_all(gains.reshape(chips, 2, HEAD), axes, 0, 0, axis_index_groups=cores)
    gains = gains.reshape(2 * chips, HEAD)
    (two,) = small_call(hop_kernel, [(block, bf16)], two, hop)
    hop = passed_along(two, "context", -2)
    half_block = (TOK, HEAD)
    key_gradient, value_gradient, q_total, k_total = small_call(
        last_kernel,
        [(half_block, bf16), (half_block, bf16), ((1, HEAD), f32), ((1, HEAD), f32)],
        *(own, hop, gains),
    )
    return (
        attended,
        query_gradient,
        key_gradient,
        value_gradient,
        q_total.reshape(HEAD),
        k_total.reshape(HEAD),
    )


def solution(mesh):
    placed = (
        P("context", "tensor"),
        P("context", "tensor"),
        P("context", "tensor"),
        P("context", "tensor"),
        P(),
        P(),
        P("context"),
    )
    return jax.shard_map(
        body,
        mesh=mesh,
        in_specs=placed,
        out_specs=(
            P("context", "tensor"),
            P("context", "tensor"),
            P("context", "tensor"),
            P("context", "tensor"),
            P(),
            P(),
        ),
        check_vma=False,
    )
```

```python
import jax
import jax.numpy as jnp
import numpy as np
from jax import lax
from jax.experimental import pallas as pl
from jax.experimental.pallas import tpu as pltpu
from jax.sharding import PartitionSpec as P

REACH = 4
THETA = 500000.0
EPSILON = 1e-06
TOK = 256
HEAD = 128
HEADS = 8
WINDOW = (REACH + 1) * TOK
SUB = 128
SPAN = 1152
CHUNKS = SPAN // SUB
FINE = 64
KEY_BLOCKS = (
    [(0, SUB, 0, 256)]
    + [(start, start + 256, 0, 512) for start in range(SUB, SPAN, 256)]
    + [(SPAN, WINDOW, 256, 512)]
)
ID_ROWS = 16
MSG = 2 * TOK + ID_ROWS
SCALING = HEAD ** (-0.5)
EXP2 = float(SCALING * np.log2(np.e))

PI_A = 3.140625
PI_B = float(np.round((np.pi - PI_A) * 2.0**23) / 2.0**23)
PI_C = float(np.pi - PI_A - PI_B)


def passed_along(block, axis, distance):
    devices = range(lax.axis_size(axis))
    route = [(i - distance, i) for i in devices if i - distance in devices]
    return lax.ppermute(block, axis, route)


def dot(a, b):
    return jnp.dot(a, b, preferred_element_type=jnp.float32)


def half_turned(x):
    return pltpu.roll(x, HEAD // 2, 1)


def cos_sin(position, frequency):
    angle = position * frequency
    lane = lax.broadcasted_iota(jnp.int32, (1, HEAD), 1)
    quarter = jnp.where(lane < HEAD // 2, 0.5, 0.0)
    turns = jnp.floor(angle * np.float32(1.0 / np.pi) + (quarter + 0.5))
    count = turns - quarter
    rest = ((angle - count * PI_A) - count * PI_B) - count * PI_C
    square = rest * rest
    series = np.float32(-1.9806614727713168e-4) + square * np.float32(2.6000534489867277e-6)
    series = np.float32(8.333017118275166e-3) + square * series
    series = np.float32(-1.6666656732559204e-1) + square * series
    value = rest + rest * (square * series)
    return jnp.where((turns.astype(jnp.int32) & 1) == 1, -value, value)


def prepare_kernel(q_ref, d_ref, qg_ref, kg_ref, xh_ref, scale_ref, dcat, dcat_t, gains):
    gains[0:1, :] = qg_ref[...]
    gains[1:2, :] = kg_ref[...]
    for sub in range(2):
        tokens = slice(sub * SUB, (sub + 1) * SUB)
        for h in range(HEADS):
            at = (h // 2) * 512 + sub * 256 + (h % 2) * SUB
            rows = slice(at, at + SUB)
            x = q_ref[tokens, h * HEAD : (h + 1) * HEAD].astype(jnp.float32)
            r = lax.rsqrt(jnp.mean(x * x, axis=1, keepdims=True) + EPSILON)
            xh_ref[rows, :] = x * r
            scale_ref[rows, :] = jnp.broadcast_to(r, (SUB, HEAD))
            d = d_ref[tokens, h * HEAD : (h + 1) * HEAD]
            dcat[rows, :] = d
            dcat_t[h // 2, :, at % 512 : at % 512 + SUB] = d.astype(jnp.float32).T.astype(jnp.bfloat16)


def prepare(queries, output_gradient, q_gain, k_gain):
    vmem = pl.BlockSpec(memory_space=pltpu.VMEM)
    f32, bf16 = jnp.float32, jnp.bfloat16
    shape = jax.ShapeDtypeStruct
    return pl.pallas_call(
        prepare_kernel,
        out_shape=[
            shape((HEADS * TOK, HEAD), f32),
            shape((HEADS * TOK, HEAD), f32),
            shape((HEADS * TOK, HEAD), bf16),
            shape((HEADS // 2, HEAD, 512), bf16),
            shape((2, HEAD), f32),
        ],
        in_specs=[vmem] * 4,
        out_specs=[vmem] * 5,
        compiler_params=pltpu.CompilerParams(vmem_limit_bytes=16 * 1024 * 1024),
        cost_estimate=pl.CostEstimate(flops=10**9, bytes_accessed=4 * 2**20, transcendentals=0),
    )(queries, output_gradient, q_gain, k_gain)


def kernel(
    b4, b2, b0, first_swap, middle_swap, last_swap, xh_ref, scale_ref, dcat, dcat_t, gains_ref, f_ref,
    att_hbm, gq_hbm, four_ref, two_ref, own_ref, swap_ref, gain_ref,
    att_ref, gq_ref, cosine, sine, kext, vwin, khat_t, v_t, qhat, qext_t,
    s_ref, w_ref, ds_ref, dk, dv, qg_acc, b3, b1, att_sem, gq_sem,
):
    even = lax.rem(lax.axis_index("context"), 2) == 0

    @pl.when(even)
    def _():
        b3[...] = last_swap[...]
        b1[...] = middle_swap[...]

    @pl.when(jnp.logical_not(even))
    def _():
        b3[...] = middle_swap[...]
        b1[...] = first_swap[...]

    blocks = (b4, b3, b2, b1, b0)
    lane = lax.broadcasted_iota(jnp.int32, (SUB, HEAD), 1)
    row = lax.broadcasted_iota(jnp.int32, (SUB, HEAD), 0)
    lane_f = lane.astype(jnp.float32)
    row_f = row.astype(jnp.float32)
    left = lane < HEAD // 2
    parts = WINDOW // SUB
    q_gain = gains_ref[0:1, :]
    k_gain = gains_ref[1:2, :]
    frequency = f_ref[...]

    id_rows = []
    for block in blocks:
        both = block[2 * TOK : MSG, :].astype(jnp.float32)
        id_rows += [both[0:1], both[1:2]]
    below = jnp.zeros((SUB, HEAD), jnp.float32)
    for j in range(parts):
        column = jnp.broadcast_to(id_rows[j], (SUB, HEAD)).T
        kext[j * SUB : (j + 1) * SUB, HEAD:] = jnp.where(column == lane_f, 1.0, 0.0).astype(jnp.bfloat16)
        below = below + jnp.where(column < lane_f, 1.0, 0.0)
    first = jnp.sum(below, axis=0, keepdims=True)

    for j in range(parts):
        rows = slice(j * SUB, (j + 1) * SUB)
        here = slice((j % 2) * SUB, (j % 2 + 1) * SUB)
        block = blocks[j // 2]
        member = kext[rows, HEAD:].astype(jnp.float32)
        start = jnp.sum(member * first, axis=1, keepdims=True)
        position = (row + j * SUB).astype(jnp.float32) - start
        both = cos_sin(position, frequency)
        turned = half_turned(both)
        c = jnp.where(left, both, turned)
        s = jnp.where(left, -turned, both)
        cosine[rows, :] = c
        sine[rows, :] = s
        x = block[here, :].astype(jnp.float32)
        normed = x * lax.rsqrt(jnp.mean(x * x, axis=1, keepdims=True) + EPSILON) * k_gain
        hat = normed * c + half_turned(normed) * s
        kext[rows, 0:HEAD] = hat.astype(jnp.bfloat16)
        khat_t[:, rows] = hat.T.astype(jnp.bfloat16)
        values = block[TOK + (j % 2) * SUB : TOK + (j % 2 + 1) * SUB, :]
        vwin[rows, :] = values
        v_t[:, rows] = values.astype(jnp.float32).T.astype(jnp.bfloat16)

    for sub in range(2):
        window_rows = slice(REACH * TOK + sub * SUB, REACH * TOK + (sub + 1) * SUB)
        c_q = cosine[window_rows, :]
        s_q = sine[window_rows, :]
        other = jnp.where(row_f == id_rows[2 * REACH + sub], 0.0, -1e30).astype(jnp.bfloat16)
        for h in range(HEADS):
            at = (h // 2) * 512 + sub * 256 + (h % 2) * SUB
            lanes = slice(at % 512, at % 512 + SUB)
            normed = xh_ref[at : at + SUB, :] * q_gain
            hat = normed * c_q + half_turned(normed) * s_q
            qhat[at : at + SUB, :] = hat.astype(jnp.bfloat16)
            qext_t[h // 2, 0:HEAD, lanes] = hat.T.astype(jnp.bfloat16)
            qext_t[h // 2, HEAD:, lanes] = other

    dk[...] = jnp.zeros_like(dk)
    dv[...] = jnp.zeros_like(dv)
    qg_acc[...] = jnp.zeros_like(qg_acc)
    later = jnp.where(row <= lane, 0.0, -1e30)
    later = jnp.concatenate([later, later], axis=1)
    spans = (slice(0, SPAN), slice(SUB, WINDOW))
    columns_of = (slice(0, 256), slice(256, 512))

    def copies(pair):
        columns = slice(pair * 256, (pair + 1) * 256)
        return (
            pltpu.make_async_copy(att_ref.at[:, columns], att_hbm.at[:, columns], att_sem.at[pair]),
            pltpu.make_async_copy(gq_ref.at[:, columns], gq_hbm.at[:, columns], gq_sem.at[pair]),
        )

    shifts, inverses, centers, queries_t = {}, {}, {}, {}

    def scores(pair, sub):
        q = qext_t[pair, :, columns_of[sub]]
        top = jnp.full((8, 256), -1e30, jnp.float32)
        for start in range(0, SPAN, SUB):
            s = dot(kext[sub * SUB + start : sub * SUB + start + SUB, :], q)
            if start + SUB == SPAN:
                s = s + later
            s_ref[pair % 2, sub, start : start + SUB, :] = s
            top = jnp.maximum(top, jnp.max(s.reshape(SUB // 8, 8, 256), axis=0))
            yield
        shifts[pair, sub] = jnp.max(top, axis=0, keepdims=True) * EXP2

    def exponents(pair, sub):
        slot = pair % 2
        shift = shifts[pair, sub]
        total = jnp.zeros((8, 256), jnp.float32)
        for at in range(0, SPAN, FINE):
            rows = slice(at, at + FINE)
            e = jnp.exp2(s_ref[slot, sub, rows, :] * EXP2 - shift)
            s_ref[slot, sub, rows, :] = e
            total = total + jnp.sum(e.reshape(FINE // 8, 8, 256), axis=0)
            yield
        inverses[pair, sub] = 1.0 / jnp.sum(total, axis=0, keepdims=True)

    def weights(pair, sub):
        inverse = inverses[pair, sub]
        for at in range(0, SPAN, FINE):
            w = s_ref[pair % 2, sub, at : at + FINE, :] * inverse
            keys = slice(sub * SUB + at, sub * SUB + at + FINE)
            w_ref[pair % 2, keys, columns_of[sub]] = w.astype(jnp.bfloat16)
            yield

    def attend(pair, sub):
        att_t = dot(v_t[:, spans[sub]], w_ref[pair % 2, spans[sub], columns_of[sub]])
        d_t = dcat_t[pair, :, columns_of[sub]]
        centers[pair, sub] = jnp.sum(att_t * d_t.astype(jnp.float32), axis=0, keepdims=True)
        yield
        tokens = slice(sub * SUB, (sub + 1) * SUB)
        for g in range(2):
            columns = slice(pair * 256 + g * HEAD, pair * 256 + (g + 1) * HEAD)
            att_ref[tokens, columns] = att_t[:, g * SUB : (g + 1) * SUB].T.astype(jnp.bfloat16)
            yield

    def score_terms(pair, sub):
        slot = pair % 2
        d_t = dcat_t[pair, :, columns_of[sub]]
        center = centers[pair, sub]
        for c in range(CHUNKS):
            keys = slice((sub + c) * SUB, (sub + c + 1) * SUB)
            dw = dot(vwin[keys, :], d_t)
            w = w_ref[slot, keys, columns_of[sub]].astype(jnp.float32)
            ds_ref[slot, keys, columns_of[sub]] = (w * (dw - center)).astype(jnp.bfloat16)
            yield

    def query_sums(pair, sub):
        dq_t = dot(khat_t[:, spans[sub]], ds_ref[pair % 2, spans[sub], columns_of[sub]])
        queries_t[pair, sub] = dq_t * SCALING
        yield

    def query_terms(pair, sub):
        dq_t = queries_t[pair, sub]
        tokens = slice(sub * SUB, (sub + 1) * SUB)
        window_rows = slice(REACH * TOK + sub * SUB, REACH * TOK + (sub + 1) * SUB)
        c_q = cosine[window_rows, :]
        s_q = sine[window_rows, :]
        for g in range(2):
            columns = slice(pair * 256 + g * HEAD, pair * 256 + (g + 1) * HEAD)
            at = pair * 512 + sub * 256 + g * SUB
            rows = slice(at, at + SUB)
            dq = dq_t[:, g * SUB : (g + 1) * SUB].T
            xh = xh_ref[rows, :]
            dn = dq * c_q - half_turned(dq) * s_q
            qg_acc[...] += jnp.sum((dn * xh).reshape(SUB // 8, 8, HEAD), axis=0)
            dxh = dn * q_gain
            gq = scale_ref[rows, :] * (dxh - xh * jnp.mean(dxh * xh, axis=1, keepdims=True))
            gq_ref[tokens, columns] = gq.astype(jnp.bfloat16)
            yield

    def key_terms(pair):
        for start, stop, low, high in KEY_BLOCKS:
            keys, lanes = slice(start, stop), slice(low, high)
            rows = slice(pair * 512 + low, pair * 512 + high)
            dk[keys, :] += dot(ds_ref[pair % 2, keys, lanes], qhat[rows, :])
            yield
            dv[keys, :] += dot(w_ref[pair % 2, keys, lanes], dcat[rows, :])
            yield

    def first_of(stream, count):
        for _ in range(count):
            if next(stream, stop) is stop:
                return
            yield

    def weave(*streams):
        streams = [iter(stream) for stream in streams]
        while streams:
            streams = [stream for stream in streams if next(stream, stop) is not stop]

    stop = object()
    chains = [(pair, sub) for pair in range(HEADS // 2) for sub in range(2)]
    keys_before = iter(())
    weave(scores(*chains[0]))
    for i, (pair, sub) in enumerate(chains):
        if sub == 0 and pair > 0:
            keys_before = key_terms(pair - 1)
        ahead = [scores(*chains[i + 1])] if i + 1 < len(chains) else []
        weave(exponents(pair, sub), *ahead)
        behind = [query_sums(*chains[i - 1])] if i > 0 else []
        weave(weights(pair, sub), *behind, first_of(keys_before, 3))
        behind = [query_terms(*chains[i - 1])] if i > 0 else []
        weave(attend(pair, sub), *behind)
        weave(score_terms(pair, sub), first_of(keys_before, 3))
        if sub == 0 and pair > 0:
            for copy in copies(pair - 1):
                copy.start()
    last = HEADS // 2 - 1
    weave(query_sums(last, 1))

    outs = ((four_ref, 0), (swap_ref, 2 * TOK), (two_ref, 0), (swap_ref, 0), (own_ref, 0))
    k_sums = [jnp.zeros((8, HEAD), jnp.float32)]

    def key_ends(j):
        rows = slice(j * SUB, (j + 1) * SUB)
        here = slice((j % 2) * SUB, (j % 2 + 1) * SUB)
        x = blocks[j // 2][here, :].astype(jnp.float32)
        r = lax.rsqrt(jnp.mean(x * x, axis=1, keepdims=True) + EPSILON)
        xh = x * r
        d = dk[rows, :] * SCALING
        dn = d * cosine[rows, :] - half_turned(d) * sine[rows, :]
        k_sums[0] = k_sums[0] + jnp.sum((dn * xh).reshape(SUB // 8, 8, HEAD), axis=0)
        dxh = dn * k_gain
        gk = r * (dxh - xh * jnp.mean(dxh * xh, axis=1, keepdims=True))
        out, at = outs[j // 2]
        at = at + (j % 2) * SUB
        out[at : at + SUB, :] = gk.astype(out.dtype)
        out[at + TOK : at + TOK + SUB, :] = dv[rows, :].astype(out.dtype)

    def all_key_ends():
        yield
        yield
        yield
        key_ends(0)
        yield
        for j in range(1, parts - 1):
            key_ends(j)
            yield

    weave(key_terms(last), all_key_ends(), query_terms(last, 1))
    key_ends(parts - 1)
    for copy in copies(last):
        copy.start()
    kg = k_sums[0]
    gains = jnp.concatenate(
        [jnp.sum(qg_acc[...], axis=0, keepdims=True), jnp.sum(kg, axis=0, keepdims=True)]
    )
    gain_ref[...] = jnp.concatenate([gains, jnp.zeros((6, HEAD), jnp.float32)])
    for pair in range(HEADS // 2):
        for copy in copies(pair):
            copy.wait()


def attention(blocks, prepared, frequency):
    vmem = pl.BlockSpec(memory_space=pltpu.VMEM)
    hbm = pl.BlockSpec(memory_space=pl.ANY)
    f32, bf16 = jnp.float32, jnp.bfloat16
    shape = jax.ShapeDtypeStruct
    return pl.pallas_call(
        kernel,
        out_shape=[
            shape((TOK, HEADS * HEAD), bf16),
            shape((TOK, HEADS * HEAD), bf16),
            shape((2 * TOK, HEAD), f32),
            shape((2 * TOK, HEAD), f32),
            shape((2 * TOK, HEAD), f32),
            shape((4 * TOK, HEAD), bf16),
            shape((8, HEAD), f32),
        ],
        in_specs=[vmem] * 12,
        out_specs=[hbm] * 2 + [vmem] * 5,
        scratch_shapes=[
            pltpu.VMEM((TOK, HEADS * HEAD), bf16),
            pltpu.VMEM((TOK, HEADS * HEAD), bf16),
            pltpu.VMEM((WINDOW, HEAD), f32),
            pltpu.VMEM((WINDOW, HEAD), f32),
            pltpu.VMEM((WINDOW, 2 * HEAD), bf16),
            pltpu.VMEM((WINDOW, HEAD), bf16),
            pltpu.VMEM((HEAD, WINDOW), bf16),
            pltpu.VMEM((HEAD, WINDOW), bf16),
            pltpu.VMEM((HEADS * TOK, HEAD), bf16),
            pltpu.VMEM((HEADS // 2, 2 * HEAD, 512), bf16),
            pltpu.VMEM((2, 2, SPAN, 256), f32),
            pltpu.VMEM((2, WINDOW, 512), bf16),
            pltpu.VMEM((2, WINDOW, 512), bf16),
            pltpu.VMEM((WINDOW, HEAD), f32),
            pltpu.VMEM((WINDOW, HEAD), f32),
            pltpu.VMEM((8, HEAD), f32),
            pltpu.VMEM((MSG, HEAD), bf16),
            pltpu.VMEM((MSG, HEAD), bf16),
            pltpu.SemaphoreType.DMA((HEADS // 2,)),
            pltpu.SemaphoreType.DMA((HEADS // 2,)),
        ],
        compiler_params=pltpu.CompilerParams(vmem_limit_bytes=40 * 1024 * 1024),
    )(*blocks, *prepared, frequency)


def pack_kernel(keys, values, ids, out):
    out[0:TOK, :] = keys[...]
    out[TOK : 2 * TOK, :] = values[...]
    marked = (ids[...] + 1).astype(jnp.float32)
    out[2 * TOK :, :] = jnp.concatenate(
        [marked, jnp.zeros((ID_ROWS - 2, HEAD), jnp.float32)]
    ).astype(jnp.bfloat16)


def pack(keys, values, ids):
    vmem = pl.BlockSpec(memory_space=pltpu.VMEM)
    return pl.pallas_call(
        pack_kernel,
        out_shape=jax.ShapeDtypeStruct((MSG, HEAD), jnp.bfloat16),
        in_specs=[vmem] * 3,
        out_specs=vmem,
    )(keys, values, ids)


def swapped(block, ways=(0, 1)):
    route = [(i, i ^ 1) for i in range(lax.axis_size("context")) if i % 2 in ways]
    return lax.ppermute(block, "context", route)


def chip_kernel(swap, four, two, own, four_out, two_out, own_out):
    even = lax.rem(lax.axis_index("context"), 2) == 0
    one, three = slice(0, 2 * TOK), slice(2 * TOK, 4 * TOK)

    @pl.when(even)
    def _():
        four_out[...] = four[...].astype(jnp.bfloat16)
        two_out[...] = two[...] + swap[three, :].astype(jnp.float32)
        own_out[...] = own[...] + swap[one, :].astype(jnp.float32)

    @pl.when(jnp.logical_not(even))
    def _():
        four_out[...] = (four[...] + swap[three, :].astype(jnp.float32)).astype(jnp.bfloat16)
        two_out[...] = two[...] + swap[one, :].astype(jnp.float32)
        own_out[...] = own[...]


def hop_kernel(two, hop, two_out):
    two_out[...] = (two[...] + hop[...].astype(jnp.float32)).astype(jnp.bfloat16)


def last_kernel(own, hop, terms, keys, values, q_gain, k_gain):
    total = (own[...] + hop[...].astype(jnp.float32)).astype(jnp.bfloat16)
    keys[...] = total[:TOK]
    values[...] = total[TOK:]
    gains = jnp.sum(terms[...].reshape(-1, 8, HEAD), axis=0)
    q_gain[...] = gains[0:1]
    k_gain[...] = gains[1:2]


def small_call(kernel, out_shape, *operands):
    vmem = pl.BlockSpec(memory_space=pltpu.VMEM)
    return pl.pallas_call(
        kernel,
        out_shape=[jax.ShapeDtypeStruct(shape, dtype) for shape, dtype in out_shape],
        in_specs=[vmem] * len(operands),
        out_specs=[vmem] * len(out_shape),
        compiler_params=pltpu.CompilerParams(vmem_limit_bytes=16 * 1024 * 1024),
    )(*operands)


def body(queries, keys, values, output_gradient, q_gain, k_gain, doc_ids):
    f32, bf16 = jnp.float32, jnp.bfloat16
    message = pack(keys, values, doc_ids.reshape(2, HEAD))
    two = passed_along(message, "context", 2)
    first_swap = swapped(message, (0,))
    four = passed_along(message, "context", 4)
    prepared = prepare(queries, output_gradient, q_gain.reshape(1, HEAD), k_gain.reshape(1, HEAD))
    two, *prepared = lax.optimization_barrier((two, *prepared))
    middle_swap = swapped(two)
    last_swap = swapped(four, (1,))
    blocks = [four, two, message, first_swap, middle_swap, last_swap]
    half = jnp.arange(HEAD // 2, dtype=jnp.float32)
    frequency = THETA ** (-(half * 2.0 / HEAD))
    frequency = jnp.concatenate([frequency, frequency]).reshape(1, HEAD)
    attended, query_gradient, four, two, own, swap, gains = attention(blocks, prepared, frequency)

    gains = lax.all_gather(gains, ("context", "tensor"), tiled=True)
    block = (2 * TOK, HEAD)
    four, two, own = small_call(
        chip_kernel,
        [(block, bf16), (block, f32), (block, f32)],
        *(swapped(swap), four, two, own),
    )
    hop = passed_along(four, "context", -2)
    (two,) = small_call(hop_kernel, [(block, bf16)], two, hop)
    hop = passed_along(two, "context", -2)
    half_block = (TOK, HEAD)
    key_gradient, value_gradient, q_total, k_total = small_call(
        last_kernel,
        [(half_block, bf16), (half_block, bf16), ((1, HEAD), f32), ((1, HEAD), f32)],
        *(own, hop, gains),
    )
    return (
        attended,
        query_gradient,
        key_gradient,
        value_gradient,
        q_total.reshape(HEAD),
        k_total.reshape(HEAD),
    )


def solution(mesh):
    placed = (
        P("context", "tensor"),
        P("context", "tensor"),
        P("context", "tensor"),
        P("context", "tensor"),
        P(),
        P(),
        P("context"),
    )
    return jax.shard_map(
        body,
        mesh=mesh,
        in_specs=placed,
        out_specs=(
            P("context", "tensor"),
            P("context", "tensor"),
            P("context", "tensor"),
            P("context", "tensor"),
            P(),
            P(),
        ),
        check_vma=False,
    )
```

```python
import jax
import jax.numpy as jnp
import numpy as np
from jax import lax
from jax.experimental import pallas as pl
from jax.experimental.pallas import tpu as pltpu
from jax.sharding import PartitionSpec as P

REACH = 4
THETA = 500000.0
EPSILON = 1e-06
TOK = 256
HEAD = 128
HEADS = 8
WINDOW = (REACH + 1) * TOK
SUB = 128
SPAN = 1152
CHUNKS = SPAN // SUB
FINE = 64
KEY_BLOCKS = (
    [(0, SUB, 0, 256)]
    + [(start, start + 256, 0, 512) for start in range(SUB, SPAN, 256)]
    + [(SPAN, WINDOW, 256, 512)]
)
ID_ROWS = 16
MSG = 2 * TOK + ID_ROWS
SCALING = HEAD ** (-0.5)
EXP2 = float(SCALING * np.log2(np.e))

PI_A = 3.140625
PI_B = float(np.round((np.pi - PI_A) * 2.0**23) / 2.0**23)
PI_C = float(np.pi - PI_A - PI_B)


def passed_along(block, axis, distance):
    devices = range(lax.axis_size(axis))
    route = [(i - distance, i) for i in devices if i - distance in devices]
    return lax.ppermute(block, axis, route)


def dot(a, b):
    return jnp.dot(a, b, preferred_element_type=jnp.float32)


def half_turned(x):
    return pltpu.roll(x, HEAD // 2, 1)


def cos_sin(position, frequency):
    angle = position * frequency
    lane = lax.broadcasted_iota(jnp.int32, (1, HEAD), 1)
    quarter = jnp.where(lane < HEAD // 2, 0.5, 0.0)
    turns = jnp.floor(angle * np.float32(1.0 / np.pi) + (quarter + 0.5))
    count = turns - quarter
    rest = ((angle - count * PI_A) - count * PI_B) - count * PI_C
    square = rest * rest
    series = np.float32(-1.9806614727713168e-4) + square * np.float32(2.6000534489867277e-6)
    series = np.float32(8.333017118275166e-3) + square * series
    series = np.float32(-1.6666656732559204e-1) + square * series
    value = rest + rest * (square * series)
    return jnp.where((turns.astype(jnp.int32) & 1) == 1, -value, value)


def prepare_kernel(q_ref, d_ref, qg_ref, kg_ref, xh_ref, scale_ref, dcat, dcat_t, gains):
    gains[0:1, :] = qg_ref[...]
    gains[1:2, :] = kg_ref[...]
    for sub in range(2):
        tokens = slice(sub * SUB, (sub + 1) * SUB)
        for h in range(HEADS):
            at = (h // 2) * 512 + sub * 256 + (h % 2) * SUB
            rows = slice(at, at + SUB)
            x = q_ref[tokens, h * HEAD : (h + 1) * HEAD].astype(jnp.float32)
            r = lax.rsqrt(jnp.mean(x * x, axis=1, keepdims=True) + EPSILON)
            xh_ref[rows, :] = x * r
            scale_ref[rows, :] = jnp.broadcast_to(r, (SUB, HEAD))
            d = d_ref[tokens, h * HEAD : (h + 1) * HEAD]
            dcat[rows, :] = d
            dcat_t[h // 2, :, at % 512 : at % 512 + SUB] = d.astype(jnp.float32).T.astype(jnp.bfloat16)


def prepare(queries, output_gradient, q_gain, k_gain):
    vmem = pl.BlockSpec(memory_space=pltpu.VMEM)
    f32, bf16 = jnp.float32, jnp.bfloat16
    shape = jax.ShapeDtypeStruct
    return pl.pallas_call(
        prepare_kernel,
        out_shape=[
            shape((HEADS * TOK, HEAD), f32),
            shape((HEADS * TOK, HEAD), f32),
            shape((HEADS * TOK, HEAD), bf16),
            shape((HEADS // 2, HEAD, 512), bf16),
            shape((2, HEAD), f32),
        ],
        in_specs=[vmem] * 4,
        out_specs=[vmem] * 5,
        compiler_params=pltpu.CompilerParams(vmem_limit_bytes=16 * 1024 * 1024),
        cost_estimate=pl.CostEstimate(flops=10**9, bytes_accessed=4 * 2**20, transcendentals=0),
    )(queries, output_gradient, q_gain, k_gain)


def kernel(
    b4, b2, b0, first_swap, middle_swap, last_swap, xh_ref, scale_ref, dcat, dcat_t, gains_ref, f_ref,
    att_hbm, gq_hbm, four_ref, two_ref, own_ref, swap_ref, gain_ref,
    att_ref, gq_ref, cosine, sine, kext, vwin, khat_t, v_t, qhat, qext_t,
    s_ref, w_ref, ds_ref, dk, dv, qg_acc, b3, b1, att_sem, gq_sem,
):
    even = lax.rem(lax.axis_index("context"), 2) == 0

    @pl.when(even)
    def _():
        b3[...] = last_swap[...]
        b1[...] = middle_swap[...]

    @pl.when(jnp.logical_not(even))
    def _():
        b3[...] = middle_swap[...]
        b1[...] = first_swap[...]

    blocks = (b4, b3, b2, b1, b0)
    lane = lax.broadcasted_iota(jnp.int32, (SUB, HEAD), 1)
    row = lax.broadcasted_iota(jnp.int32, (SUB, HEAD), 0)
    lane_f = lane.astype(jnp.float32)
    row_f = row.astype(jnp.float32)
    left = lane < HEAD // 2
    parts = WINDOW // SUB
    q_gain = gains_ref[0:1, :]
    k_gain = gains_ref[1:2, :]
    frequency = f_ref[...]

    id_rows = []
    for block in blocks:
        both = block[2 * TOK : MSG, :].astype(jnp.float32)
        id_rows += [both[0:1], both[1:2]]
    below = jnp.zeros((SUB, HEAD), jnp.float32)
    for j in range(parts):
        column = jnp.broadcast_to(id_rows[j], (SUB, HEAD)).T
        kext[j * SUB : (j + 1) * SUB, HEAD:] = jnp.where(column == lane_f, 1.0, 0.0).astype(jnp.bfloat16)
        below = below + jnp.where(column < lane_f, 1.0, 0.0)
    first = jnp.sum(below, axis=0, keepdims=True)

    def key_part(j):
        rows = slice(j * SUB, (j + 1) * SUB)
        here = slice((j % 2) * SUB, (j % 2 + 1) * SUB)
        block = blocks[j // 2]
        member = kext[rows, HEAD:].astype(jnp.float32)
        start = jnp.sum(member * first, axis=1, keepdims=True)
        position = (row + j * SUB).astype(jnp.float32) - start
        both = cos_sin(position, frequency)
        turned = half_turned(both)
        c = jnp.where(left, both, turned)
        s = jnp.where(left, -turned, both)
        cosine[rows, :] = c
        sine[rows, :] = s
        x = block[here, :].astype(jnp.float32)
        normed = x * lax.rsqrt(jnp.mean(x * x, axis=1, keepdims=True) + EPSILON) * k_gain
        hat = normed * c + half_turned(normed) * s
        kext[rows, 0:HEAD] = hat.astype(jnp.bfloat16)
        khat_t[:, rows] = hat.T.astype(jnp.bfloat16)
        values = block[TOK + (j % 2) * SUB : TOK + (j % 2 + 1) * SUB, :]
        vwin[rows, :] = values
        v_t[:, rows] = values.astype(jnp.float32).T.astype(jnp.bfloat16)

    def query_part(pair):
        for sub in range(2):
            window_rows = slice(REACH * TOK + sub * SUB, REACH * TOK + (sub + 1) * SUB)
            other = jnp.where(row_f == id_rows[2 * REACH + sub], 0.0, -1e30).astype(jnp.bfloat16)
            for g in range(2):
                at = pair * 512 + sub * 256 + g * SUB
                lanes = slice(at % 512, at % 512 + SUB)
                normed = xh_ref[at : at + SUB, :] * q_gain
                hat = normed * cosine[window_rows, :] + half_turned(normed) * sine[window_rows, :]
                qhat[at : at + SUB, :] = hat.astype(jnp.bfloat16)
                qext_t[pair, 0:HEAD, lanes] = hat.T.astype(jnp.bfloat16)
                qext_t[pair, HEAD:, lanes] = other
                yield

    dk[...] = jnp.zeros_like(dk)
    dv[...] = jnp.zeros_like(dv)
    qg_acc[...] = jnp.zeros_like(qg_acc)
    later = jnp.where(row <= lane, 0.0, -1e30)
    later = jnp.concatenate([later, later], axis=1)
    spans = (slice(0, SPAN), slice(SUB, WINDOW))
    columns_of = (slice(0, 256), slice(256, 512))

    def copies(pair):
        columns = slice(pair * 256, (pair + 1) * 256)
        return (
            pltpu.make_async_copy(att_ref.at[:, columns], att_hbm.at[:, columns], att_sem.at[pair]),
            pltpu.make_async_copy(gq_ref.at[:, columns], gq_hbm.at[:, columns], gq_sem.at[pair]),
        )

    shifts, inverses, centers, queries_t = {}, {}, {}, {}

    def scores(pair, sub):
        q = qext_t[pair, :, columns_of[sub]]
        top = jnp.full((8, 256), -1e30, jnp.float32)
        for start in range(0, SPAN, SUB):
            s = dot(kext[sub * SUB + start : sub * SUB + start + SUB, :], q)
            if start + SUB == SPAN:
                s = s + later
            s_ref[pair % 2, sub, start : start + SUB, :] = s
            top = jnp.maximum(top, jnp.max(s.reshape(SUB // 8, 8, 256), axis=0))
            yield
        shifts[pair, sub] = jnp.max(top, axis=0, keepdims=True) * EXP2

    def exponents(pair, sub):
        slot = pair % 2
        shift = shifts[pair, sub]
        total = jnp.zeros((8, 256), jnp.float32)
        for at in range(0, SPAN, FINE):
            rows = slice(at, at + FINE)
            e = jnp.exp2(s_ref[slot, sub, rows, :] * EXP2 - shift)
            s_ref[slot, sub, rows, :] = e
            total = total + jnp.sum(e.reshape(FINE // 8, 8, 256), axis=0)
            yield
        inverses[pair, sub] = 1.0 / jnp.sum(total, axis=0, keepdims=True)

    def weights(pair, sub):
        inverse = inverses[pair, sub]
        for at in range(0, SPAN, FINE):
            w = s_ref[pair % 2, sub, at : at + FINE, :] * inverse
            keys = slice(sub * SUB + at, sub * SUB + at + FINE)
            w_ref[pair % 2, keys, columns_of[sub]] = w.astype(jnp.bfloat16)
            yield

    def attend(pair, sub):
        att_t = dot(v_t[:, spans[sub]], w_ref[pair % 2, spans[sub], columns_of[sub]])
        d_t = dcat_t[pair, :, columns_of[sub]]
        centers[pair, sub] = jnp.sum(att_t * d_t.astype(jnp.float32), axis=0, keepdims=True)
        yield
        tokens = slice(sub * SUB, (sub + 1) * SUB)
        for g in range(2):
            columns = slice(pair * 256 + g * HEAD, pair * 256 + (g + 1) * HEAD)
            att_ref[tokens, columns] = att_t[:, g * SUB : (g + 1) * SUB].T.astype(jnp.bfloat16)
            yield

    def score_terms(pair, sub):
        slot = pair % 2
        d_t = dcat_t[pair, :, columns_of[sub]]
        center = centers[pair, sub]
        for c in range(CHUNKS):
            keys = slice((sub + c) * SUB, (sub + c + 1) * SUB)
            dw = dot(vwin[keys, :], d_t)
            w = w_ref[slot, keys, columns_of[sub]].astype(jnp.float32)
            ds_ref[slot, keys, columns_of[sub]] = (w * (dw - center)).astype(jnp.bfloat16)
            yield

    def query_sums(pair, sub):
        dq_t = dot(khat_t[:, spans[sub]], ds_ref[pair % 2, spans[sub], columns_of[sub]])
        queries_t[pair, sub] = dq_t * SCALING
        yield

    def query_terms(pair, sub):
        dq_t = queries_t[pair, sub]
        tokens = slice(sub * SUB, (sub + 1) * SUB)
        window_rows = slice(REACH * TOK + sub * SUB, REACH * TOK + (sub + 1) * SUB)
        c_q = cosine[window_rows, :]
        s_q = sine[window_rows, :]
        for g in range(2):
            columns = slice(pair * 256 + g * HEAD, pair * 256 + (g + 1) * HEAD)
            at = pair * 512 + sub * 256 + g * SUB
            rows = slice(at, at + SUB)
            dq = dq_t[:, g * SUB : (g + 1) * SUB].T
            xh = xh_ref[rows, :]
            dn = dq * c_q - half_turned(dq) * s_q
            qg_acc[...] += jnp.sum((dn * xh).reshape(SUB // 8, 8, HEAD), axis=0)
            dxh = dn * q_gain
            gq = scale_ref[rows, :] * (dxh - xh * jnp.mean(dxh * xh, axis=1, keepdims=True))
            gq_ref[tokens, columns] = gq.astype(jnp.bfloat16)
            yield

    def key_terms(pair):
        for start, stop, low, high in KEY_BLOCKS:
            keys, lanes = slice(start, stop), slice(low, high)
            rows = slice(pair * 512 + low, pair * 512 + high)
            dk[keys, :] += dot(ds_ref[pair % 2, keys, lanes], qhat[rows, :])
            yield
            dv[keys, :] += dot(w_ref[pair % 2, keys, lanes], dcat[rows, :])
            yield

    def first_of(stream, count):
        for _ in range(count):
            if next(stream, stop) is stop:
                return
            yield

    def weave(*streams):
        streams = [iter(stream) for stream in streams]
        while streams:
            streams = [stream for stream in streams if next(stream, stop) is not stop]

    stop = object()
    chains = [(pair, sub) for pair in range(HEADS // 2) for sub in range(2)]
    keys_before = iter(())

    def first_keys():
        for j in range(parts - 2):
            key_part(j)
            yield

    key_part(parts - 2)
    key_part(parts - 1)
    weave(query_part(0))
    weave(first_keys(), scores(*chains[0]))
    for i, (pair, sub) in enumerate(chains):
        if sub == 0 and pair > 0:
            keys_before = key_terms(pair - 1)
        ahead = [scores(*chains[i + 1])] if i + 1 < len(chains) else []
        weave(exponents(pair, sub), *ahead)
        behind = [query_sums(*chains[i - 1])] if i > 0 else []
        weave(weights(pair, sub), *behind, first_of(keys_before, 3))
        behind = [query_terms(*chains[i - 1])] if i > 0 else []
        if sub == 0 and pair + 1 < HEADS // 2:
            behind.append(query_part(pair + 1))
        weave(attend(pair, sub), *behind)
        weave(score_terms(pair, sub), first_of(keys_before, 3))
        if sub == 0 and pair > 0:
            for copy in copies(pair - 1):
                copy.start()
    last = HEADS // 2 - 1
    weave(query_sums(last, 1))

    outs = ((four_ref, 0), (swap_ref, 2 * TOK), (two_ref, 0), (swap_ref, 0), (own_ref, 0))
    k_sums = [jnp.zeros((8, HEAD), jnp.float32)]

    def key_ends(j):
        rows = slice(j * SUB, (j + 1) * SUB)
        here = slice((j % 2) * SUB, (j % 2 + 1) * SUB)
        x = blocks[j // 2][here, :].astype(jnp.float32)
        r = lax.rsqrt(jnp.mean(x * x, axis=1, keepdims=True) + EPSILON)
        xh = x * r
        d = dk[rows, :] * SCALING
        dn = d * cosine[rows, :] - half_turned(d) * sine[rows, :]
        k_sums[0] = k_sums[0] + jnp.sum((dn * xh).reshape(SUB // 8, 8, HEAD), axis=0)
        dxh = dn * k_gain
        gk = r * (dxh - xh * jnp.mean(dxh * xh, axis=1, keepdims=True))
        out, at = outs[j // 2]
        at = at + (j % 2) * SUB
        out[at : at + SUB, :] = gk.astype(out.dtype)
        out[at + TOK : at + TOK + SUB, :] = dv[rows, :].astype(out.dtype)

    def all_key_ends():
        yield
        yield
        yield
        key_ends(0)
        yield
        for j in range(1, parts - 1):
            key_ends(j)
            yield

    weave(key_terms(last), all_key_ends(), query_terms(last, 1))
    key_ends(parts - 1)
    for copy in copies(last):
        copy.start()
    kg = k_sums[0]
    gains = jnp.concatenate(
        [jnp.sum(qg_acc[...], axis=0, keepdims=True), jnp.sum(kg, axis=0, keepdims=True)]
    )
    gain_ref[...] = gains
    high = gains.astype(jnp.bfloat16).astype(jnp.float32)
    middle = (gains - high).astype(jnp.bfloat16).astype(jnp.float32)
    low = gains - high - middle
    swap_ref[4 * TOK :, :] = jnp.concatenate(
        [high, middle, low, jnp.zeros((ID_ROWS - 6, HEAD), jnp.float32)]
    ).astype(jnp.bfloat16)
    for pair in range(HEADS // 2):
        for copy in copies(pair):
            copy.wait()


def attention(blocks, prepared, frequency):
    vmem = pl.BlockSpec(memory_space=pltpu.VMEM)
    hbm = pl.BlockSpec(memory_space=pl.ANY)
    f32, bf16 = jnp.float32, jnp.bfloat16
    shape = jax.ShapeDtypeStruct
    return pl.pallas_call(
        kernel,
        out_shape=[
            shape((TOK, HEADS * HEAD), bf16),
            shape((TOK, HEADS * HEAD), bf16),
            shape((2 * TOK, HEAD), f32),
            shape((2 * TOK, HEAD), f32),
            shape((2 * TOK, HEAD), f32),
            shape((4 * TOK + ID_ROWS, HEAD), bf16),
            shape((2, HEAD), f32),
        ],
        in_specs=[vmem] * 12,
        out_specs=[hbm] * 2 + [vmem] * 5,
        scratch_shapes=[
            pltpu.VMEM((TOK, HEADS * HEAD), bf16),
            pltpu.VMEM((TOK, HEADS * HEAD), bf16),
            pltpu.VMEM((WINDOW, HEAD), f32),
            pltpu.VMEM((WINDOW, HEAD), f32),
            pltpu.VMEM((WINDOW, 2 * HEAD), bf16),
            pltpu.VMEM((WINDOW, HEAD), bf16),
            pltpu.VMEM((HEAD, WINDOW), bf16),
            pltpu.VMEM((HEAD, WINDOW), bf16),
            pltpu.VMEM((HEADS * TOK, HEAD), bf16),
            pltpu.VMEM((HEADS // 2, 2 * HEAD, 512), bf16),
            pltpu.VMEM((2, 2, SPAN, 256), f32),
            pltpu.VMEM((2, WINDOW, 512), bf16),
            pltpu.VMEM((2, WINDOW, 512), bf16),
            pltpu.VMEM((WINDOW, HEAD), f32),
            pltpu.VMEM((WINDOW, HEAD), f32),
            pltpu.VMEM((8, HEAD), f32),
            pltpu.VMEM((MSG, HEAD), bf16),
            pltpu.VMEM((MSG, HEAD), bf16),
            pltpu.SemaphoreType.DMA((HEADS // 2,)),
            pltpu.SemaphoreType.DMA((HEADS // 2,)),
        ],
        compiler_params=pltpu.CompilerParams(vmem_limit_bytes=40 * 1024 * 1024),
    )(*blocks, *prepared, frequency)


def pack_kernel(keys, values, ids, out):
    out[0:TOK, :] = keys[...]
    out[TOK : 2 * TOK, :] = values[...]
    marked = (ids[...] + 1).astype(jnp.float32)
    out[2 * TOK :, :] = jnp.concatenate(
        [marked, jnp.zeros((ID_ROWS - 2, HEAD), jnp.float32)]
    ).astype(jnp.bfloat16)


def pack(keys, values, ids):
    vmem = pl.BlockSpec(memory_space=pltpu.VMEM)
    return pl.pallas_call(
        pack_kernel,
        out_shape=jax.ShapeDtypeStruct((MSG, HEAD), jnp.bfloat16),
        in_specs=[vmem] * 3,
        out_specs=vmem,
    )(keys, values, ids)


def swapped(block, ways=(0, 1)):
    route = [(i, i ^ 1) for i in range(lax.axis_size("context")) if i % 2 in ways]
    return lax.ppermute(block, "context", route)


def chip_kernel(swap, four, two, own, gains, four_out, two_out, own_out, gains_out):
    even = lax.rem(lax.axis_index("context"), 2) == 0
    one, three = slice(0, 2 * TOK), slice(2 * TOK, 4 * TOK)

    @pl.when(even)
    def _():
        four_out[...] = four[...].astype(jnp.bfloat16)
        two_out[...] = two[...] + swap[three, :].astype(jnp.float32)
        own_out[...] = own[...] + swap[one, :].astype(jnp.float32)

    @pl.when(jnp.logical_not(even))
    def _():
        four_out[...] = (four[...] + swap[three, :].astype(jnp.float32)).astype(jnp.bfloat16)
        two_out[...] = two[...] + swap[one, :].astype(jnp.float32)
        own_out[...] = own[...]

    split = swap[4 * TOK :, :].astype(jnp.float32)
    total = gains[...] + ((split[0:2] + split[2:4]) + split[4:6])
    gains_out[...] = jnp.concatenate([total] * (gains_out.shape[0] // 2))


def hop_kernel(two, hop, two_out):
    two_out[...] = (two[...] + hop[...].astype(jnp.float32)).astype(jnp.bfloat16)


def last_kernel(own, hop, terms, keys, values, q_gain, k_gain):
    total = (own[...] + hop[...].astype(jnp.float32)).astype(jnp.bfloat16)
    keys[...] = total[:TOK]
    values[...] = total[TOK:]
    gains = jnp.sum(terms[...].reshape(-1, 8, HEAD), axis=0)
    q_gain[...] = (gains[0:1] + gains[2:3]) + (gains[4:5] + gains[6:7])
    k_gain[...] = (gains[1:2] + gains[3:4]) + (gains[5:6] + gains[7:8])


def small_call(kernel, out_shape, *operands):
    vmem = pl.BlockSpec(memory_space=pltpu.VMEM)
    return pl.pallas_call(
        kernel,
        out_shape=[jax.ShapeDtypeStruct(shape, dtype) for shape, dtype in out_shape],
        in_specs=[vmem] * len(operands),
        out_specs=[vmem] * len(out_shape),
        compiler_params=pltpu.CompilerParams(vmem_limit_bytes=16 * 1024 * 1024),
    )(*operands)


def body(queries, keys, values, output_gradient, q_gain, k_gain, doc_ids):
    f32, bf16 = jnp.float32, jnp.bfloat16
    message = pack(keys, values, doc_ids.reshape(2, HEAD))
    two = passed_along(message, "context", 2)
    first_swap = swapped(message, (0,))
    four = passed_along(message, "context", 4)
    prepared = prepare(queries, output_gradient, q_gain.reshape(1, HEAD), k_gain.reshape(1, HEAD))
    two, *prepared = lax.optimization_barrier((two, *prepared))
    middle_swap = swapped(two)
    last_swap = swapped(four, (1,))
    blocks = [four, two, message, first_swap, middle_swap, last_swap]
    half = jnp.arange(HEAD // 2, dtype=jnp.float32)
    frequency = THETA ** (-(half * 2.0 / HEAD))
    frequency = jnp.concatenate([frequency, frequency]).reshape(1, HEAD)
    attended, query_gradient, four, two, own, swap, gains = attention(blocks, prepared, frequency)

    axes = ("context", "tensor")
    chips = lax.axis_size(axes) // 2
    block = (2 * TOK, HEAD)
    four, two, own, gains = small_call(
        chip_kernel,
        [(block, bf16), (block, f32), (block, f32), ((2 * chips, HEAD), f32)],
        *(swapped(swap), four, two, own, gains),
    )
    hop = passed_along(four, "context", -2)
    width = lax.axis_size("tensor")
    cores = [
        [(2 * n + core) * width + z for n in range(chips // width) for z in range(width)]
        for core in range(2)
    ]
    gains = lax.all_to_all(gains.reshape(chips, 2, HEAD), axes, 0, 0, axis_index_groups=cores)
    gains = gains.reshape(2 * chips, HEAD)
    (two,) = small_call(hop_kernel, [(block, bf16)], two, hop)
    hop = passed_along(two, "context", -2)
    half_block = (TOK, HEAD)
    key_gradient, value_gradient, q_total, k_total = small_call(
        last_kernel,
        [(half_block, bf16), (half_block, bf16), ((1, HEAD), f32), ((1, HEAD), f32)],
        *(own, hop, gains),
    )
    return (
        attended,
        query_gradient,
        key_gradient,
        value_gradient,
        q_total.reshape(HEAD),
        k_total.reshape(HEAD),
    )


def solution(mesh):
    placed = (
        P("context", "tensor"),
        P("context", "tensor"),
        P("context", "tensor"),
        P("context", "tensor"),
        P(),
        P(),
        P("context"),
    )
    return jax.shard_map(
        body,
        mesh=mesh,
        in_specs=placed,
        out_specs=(
            P("context", "tensor"),
            P("context", "tensor"),
            P("context", "tensor"),
            P("context", "tensor"),
            P(),
            P(),
        ),
        check_vma=False,
    )
```

```python
import jax
import jax.numpy as jnp
import numpy as np
from jax import lax
from jax.experimental import pallas as pl
from jax.experimental.pallas import tpu as pltpu
from jax.sharding import PartitionSpec as P

REACH = 4
THETA = 500000.0
EPSILON = 1e-06
TOK = 256
HEAD = 128
HEADS = 8
WINDOW = (REACH + 1) * TOK
SUB = 128
SPAN = 1152
WIDE = 192
FINE = 64
KEY_BLOCKS = (
    [(0, SUB, 0, 256)]
    + [(start, start + 512, 0, 512) for start in range(SUB, SPAN, 512)]
    + [(SPAN, WINDOW, 256, 512)]
)
ID_ROWS = 16
MSG = 2 * TOK + ID_ROWS
SCALING = HEAD ** (-0.5)
EXP2 = float(SCALING * np.log2(np.e))

PI_A = 3.140625
PI_B = float(np.round((np.pi - PI_A) * 2.0**23) / 2.0**23)
PI_C = float(np.pi - PI_A - PI_B)


def passed_along(block, axis, distance):
    devices = range(lax.axis_size(axis))
    route = [(i - distance, i) for i in devices if i - distance in devices]
    return lax.ppermute(block, axis, route)


def dot(a, b):
    return jnp.dot(a, b, preferred_element_type=jnp.float32)


def half_turned(x):
    return pltpu.roll(x, HEAD // 2, 1)


def cos_sin(position, frequency):
    angle = position * frequency
    lane = lax.broadcasted_iota(jnp.int32, (1, HEAD), 1)
    quarter = jnp.where(lane < HEAD // 2, 0.5, 0.0)
    turns = jnp.floor(angle * np.float32(1.0 / np.pi) + (quarter + 0.5))
    count = turns - quarter
    rest = ((angle - count * PI_A) - count * PI_B) - count * PI_C
    square = rest * rest
    series = np.float32(-1.9806614727713168e-4) + square * np.float32(2.6000534489867277e-6)
    series = np.float32(8.333017118275166e-3) + square * series
    series = np.float32(-1.6666656732559204e-1) + square * series
    value = rest + rest * (square * series)
    return jnp.where((turns.astype(jnp.int32) & 1) == 1, -value, value)


def prepare_kernel(q_ref, d_ref, qg_ref, kg_ref, xh_ref, scale_ref, dcat, dcat_t, gains):
    gains[0:1, :] = qg_ref[...]
    gains[1:2, :] = kg_ref[...]
    for sub in range(2):
        tokens = slice(sub * SUB, (sub + 1) * SUB)
        for h in range(HEADS):
            at = (h // 2) * 512 + sub * 256 + (h % 2) * SUB
            rows = slice(at, at + SUB)
            x = q_ref[tokens, h * HEAD : (h + 1) * HEAD].astype(jnp.float32)
            r = lax.rsqrt(jnp.mean(x * x, axis=1, keepdims=True) + EPSILON)
            xh_ref[rows, :] = x * r
            scale_ref[rows, :] = jnp.broadcast_to(r, (SUB, HEAD))
            d = d_ref[tokens, h * HEAD : (h + 1) * HEAD]
            dcat[rows, :] = d
            dcat_t[h // 2, :, at % 512 : at % 512 + SUB] = d.astype(jnp.float32).T.astype(jnp.bfloat16)


def prepare(queries, output_gradient, q_gain, k_gain):
    vmem = pl.BlockSpec(memory_space=pltpu.VMEM)
    f32, bf16 = jnp.float32, jnp.bfloat16
    shape = jax.ShapeDtypeStruct
    return pl.pallas_call(
        prepare_kernel,
        out_shape=[
            shape((HEADS * TOK, HEAD), f32),
            shape((HEADS * TOK, HEAD), f32),
            shape((HEADS * TOK, HEAD), bf16),
            shape((HEADS // 2, HEAD, 512), bf16),
            shape((2, HEAD), f32),
        ],
        in_specs=[vmem] * 4,
        out_specs=[vmem] * 5,
        compiler_params=pltpu.CompilerParams(vmem_limit_bytes=16 * 1024 * 1024),
        cost_estimate=pl.CostEstimate(flops=10**9, bytes_accessed=4 * 2**20, transcendentals=0),
    )(queries, output_gradient, q_gain, k_gain)


def kernel(
    b4, b2, b0, first_swap, middle_swap, last_swap, xh_ref, scale_ref, dcat, dcat_t, gains_ref, f_ref,
    att_hbm, gq_hbm, four_ref, two_ref, own_ref, swap_ref, gain_ref,
    att_ref, gq_ref, cosine, sine, kext, vwin, khat_t, v_t, qhat, qext_t,
    s_ref, w_ref, ds_ref, dk, dv, qg_acc, b3, b1, att_sem, gq_sem,
):
    even = lax.rem(lax.axis_index("context"), 2) == 0

    @pl.when(even)
    def _():
        b3[...] = last_swap[...]
        b1[...] = middle_swap[...]

    @pl.when(jnp.logical_not(even))
    def _():
        b3[...] = middle_swap[...]
        b1[...] = first_swap[...]

    blocks = (b4, b3, b2, b1, b0)
    lane = lax.broadcasted_iota(jnp.int32, (SUB, HEAD), 1)
    row = lax.broadcasted_iota(jnp.int32, (SUB, HEAD), 0)
    lane_f = lane.astype(jnp.float32)
    row_f = row.astype(jnp.float32)
    left = lane < HEAD // 2
    parts = WINDOW // SUB
    q_gain = gains_ref[0:1, :]
    k_gain = gains_ref[1:2, :]
    frequency = f_ref[...]

    id_rows = []
    for block in blocks:
        both = block[2 * TOK : MSG, :].astype(jnp.float32)
        id_rows += [both[0:1], both[1:2]]
    below = jnp.zeros((SUB, HEAD), jnp.float32)
    for j in range(parts):
        column = jnp.broadcast_to(id_rows[j], (SUB, HEAD)).T
        kext[j * SUB : (j + 1) * SUB, HEAD:] = jnp.where(column == lane_f, 1.0, 0.0).astype(jnp.bfloat16)
        below = below + jnp.where(column < lane_f, 1.0, 0.0)
    first = jnp.sum(below, axis=0, keepdims=True)

    def key_part(j):
        rows = slice(j * SUB, (j + 1) * SUB)
        here = slice((j % 2) * SUB, (j % 2 + 1) * SUB)
        block = blocks[j // 2]
        member = kext[rows, HEAD:].astype(jnp.float32)
        start = jnp.sum(member * first, axis=1, keepdims=True)
        position = (row + j * SUB).astype(jnp.float32) - start
        both = cos_sin(position, frequency)
        turned = half_turned(both)
        c = jnp.where(left, both, turned)
        s = jnp.where(left, -turned, both)
        cosine[rows, :] = c
        sine[rows, :] = s
        x = block[here, :].astype(jnp.float32)
        normed = x * lax.rsqrt(jnp.mean(x * x, axis=1, keepdims=True) + EPSILON) * k_gain
        hat = normed * c + half_turned(normed) * s
        kext[rows, 0:HEAD] = hat.astype(jnp.bfloat16)
        khat_t[:, rows] = hat.T.astype(jnp.bfloat16)
        values = block[TOK + (j % 2) * SUB : TOK + (j % 2 + 1) * SUB, :]
        vwin[rows, :] = values
        v_t[:, rows] = values.astype(jnp.float32).T.astype(jnp.bfloat16)

    def query_part(pair):
        for sub in range(2):
            window_rows = slice(REACH * TOK + sub * SUB, REACH * TOK + (sub + 1) * SUB)
            other = jnp.where(row_f == id_rows[2 * REACH + sub], 0.0, -1e30).astype(jnp.bfloat16)
            for g in range(2):
                at = pair * 512 + sub * 256 + g * SUB
                lanes = slice(at % 512, at % 512 + SUB)
                normed = xh_ref[at : at + SUB, :] * q_gain
                hat = normed * cosine[window_rows, :] + half_turned(normed) * sine[window_rows, :]
                qhat[at : at + SUB, :] = hat.astype(jnp.bfloat16)
                qext_t[pair, 0:HEAD, lanes] = hat.T.astype(jnp.bfloat16)
                qext_t[pair, HEAD:, lanes] = other
                yield

    dk[...] = jnp.zeros_like(dk)
    dv[...] = jnp.zeros_like(dv)
    qg_acc[...] = jnp.zeros_like(qg_acc)
    later = jnp.where(row <= lane, 0.0, -1e30)
    later = jnp.concatenate([later, later], axis=1)
    spans = (slice(0, SPAN), slice(SUB, WINDOW))
    columns_of = (slice(0, 256), slice(256, 512))

    def copies(pair):
        columns = slice(pair * 256, (pair + 1) * 256)
        return (
            pltpu.make_async_copy(att_ref.at[:, columns], att_hbm.at[:, columns], att_sem.at[pair]),
            pltpu.make_async_copy(gq_ref.at[:, columns], gq_hbm.at[:, columns], gq_sem.at[pair]),
        )

    shifts, inverses, centers, queries_t = {}, {}, {}, {}

    def scores(pair, sub):
        q = qext_t[pair, :, columns_of[sub]]
        top = jnp.full((8, 256), -1e30, jnp.float32)
        for start in range(0, SPAN, WIDE):
            s = dot(kext[sub * SUB + start : sub * SUB + start + WIDE, :], q)
            if start + WIDE == SPAN:
                s = jnp.concatenate([s[: WIDE - SUB], s[WIDE - SUB :] + later])
            s_ref[pair % 2, sub, start : start + WIDE, :] = s
            top = jnp.maximum(top, jnp.max(s.reshape(WIDE // 8, 8, 256), axis=0))
            yield
        shifts[pair, sub] = jnp.max(top, axis=0, keepdims=True) * EXP2

    def exponents(pair, sub):
        slot = pair % 2
        shift = shifts[pair, sub]
        total = jnp.zeros((8, 256), jnp.float32)
        for at in range(0, SPAN, FINE):
            rows = slice(at, at + FINE)
            e = jnp.exp2(s_ref[slot, sub, rows, :] * EXP2 - shift)
            s_ref[slot, sub, rows, :] = e
            total = total + jnp.sum(e.reshape(FINE // 8, 8, 256), axis=0)
            yield
        inverses[pair, sub] = 1.0 / jnp.sum(total, axis=0, keepdims=True)

    def weights(pair, sub):
        inverse = inverses[pair, sub]
        for at in range(0, SPAN, FINE):
            w = s_ref[pair % 2, sub, at : at + FINE, :] * inverse
            keys = slice(sub * SUB + at, sub * SUB + at + FINE)
            w_ref[pair % 2, keys, columns_of[sub]] = w.astype(jnp.bfloat16)
            yield

    def attend(pair, sub):
        att_t = dot(v_t[:, spans[sub]], w_ref[pair % 2, spans[sub], columns_of[sub]])
        d_t = dcat_t[pair, :, columns_of[sub]]
        centers[pair, sub] = jnp.sum(att_t * d_t.astype(jnp.float32), axis=0, keepdims=True)
        yield
        tokens = slice(sub * SUB, (sub + 1) * SUB)
        for g in range(2):
            columns = slice(pair * 256 + g * HEAD, pair * 256 + (g + 1) * HEAD)
            att_ref[tokens, columns] = att_t[:, g * SUB : (g + 1) * SUB].T.astype(jnp.bfloat16)
            yield

    def score_terms(pair, sub):
        slot = pair % 2
        d_t = dcat_t[pair, :, columns_of[sub]]
        center = centers[pair, sub]
        for start in range(0, SPAN, WIDE):
            keys = slice(sub * SUB + start, sub * SUB + start + WIDE)
            dw = dot(vwin[keys, :], d_t)
            w = w_ref[slot, keys, columns_of[sub]].astype(jnp.float32)
            ds_ref[slot, keys, columns_of[sub]] = (w * (dw - center)).astype(jnp.bfloat16)
            yield

    def query_sums(pair, sub):
        dq_t = dot(khat_t[:, spans[sub]], ds_ref[pair % 2, spans[sub], columns_of[sub]])
        queries_t[pair, sub] = dq_t * SCALING
        yield

    def query_terms(pair, sub):
        dq_t = queries_t[pair, sub]
        tokens = slice(sub * SUB, (sub + 1) * SUB)
        window_rows = slice(REACH * TOK + sub * SUB, REACH * TOK + (sub + 1) * SUB)
        c_q = cosine[window_rows, :]
        s_q = sine[window_rows, :]
        for g in range(2):
            columns = slice(pair * 256 + g * HEAD, pair * 256 + (g + 1) * HEAD)
            at = pair * 512 + sub * 256 + g * SUB
            rows = slice(at, at + SUB)
            dq = dq_t[:, g * SUB : (g + 1) * SUB].T
            xh = xh_ref[rows, :]
            dn = dq * c_q - half_turned(dq) * s_q
            qg_acc[...] += jnp.sum((dn * xh).reshape(SUB // 8, 8, HEAD), axis=0)
            dxh = dn * q_gain
            gq = scale_ref[rows, :] * (dxh - xh * jnp.mean(dxh * xh, axis=1, keepdims=True))
            gq_ref[tokens, columns] = gq.astype(jnp.bfloat16)
            yield

    def key_terms(pair):
        for start, stop, low, high in KEY_BLOCKS:
            keys, lanes = slice(start, stop), slice(low, high)
            rows = slice(pair * 512 + low, pair * 512 + high)
            dk[keys, :] += dot(ds_ref[pair % 2, keys, lanes], qhat[rows, :])
            yield
            dv[keys, :] += dot(w_ref[pair % 2, keys, lanes], dcat[rows, :])
            yield

    def first_of(stream, count):
        for _ in range(count):
            if next(stream, stop) is stop:
                return
            yield

    def weave(*streams):
        streams = [iter(stream) for stream in streams]
        while streams:
            streams = [stream for stream in streams if next(stream, stop) is not stop]

    stop = object()
    chains = [(pair, sub) for pair in range(HEADS // 2) for sub in range(2)]
    keys_before = iter(())

    def first_keys():
        for j in range(0, parts - 2, 2):
            key_part(j)
            key_part(j + 1)
            yield

    key_part(parts - 2)
    key_part(parts - 1)
    weave(query_part(0))
    weave(first_keys(), scores(*chains[0]))
    for i, (pair, sub) in enumerate(chains):
        if sub == 0 and pair > 0:
            keys_before = key_terms(pair - 1)
        ahead = [scores(*chains[i + 1])] if i + 1 < len(chains) else []
        weave(exponents(pair, sub), *ahead)
        behind = [query_sums(*chains[i - 1])] if i > 0 else []
        weave(weights(pair, sub), *behind, first_of(keys_before, 2))
        behind = [query_terms(*chains[i - 1])] if i > 0 else []
        if sub == 0 and pair + 1 < HEADS // 2:
            behind.append(query_part(pair + 1))
        weave(attend(pair, sub), *behind)
        weave(score_terms(pair, sub), first_of(keys_before, 2))
        if sub == 0 and pair > 0:
            for copy in copies(pair - 1):
                copy.start()
    last = HEADS // 2 - 1
    weave(query_sums(last, 1))

    outs = ((four_ref, 0), (swap_ref, 2 * TOK), (two_ref, 0), (swap_ref, 0), (own_ref, 0))
    k_sums = [jnp.zeros((8, HEAD), jnp.float32)]

    def key_ends(j):
        rows = slice(j * SUB, (j + 1) * SUB)
        here = slice((j % 2) * SUB, (j % 2 + 1) * SUB)
        x = blocks[j // 2][here, :].astype(jnp.float32)
        r = lax.rsqrt(jnp.mean(x * x, axis=1, keepdims=True) + EPSILON)
        xh = x * r
        d = dk[rows, :] * SCALING
        dn = d * cosine[rows, :] - half_turned(d) * sine[rows, :]
        k_sums[0] = k_sums[0] + jnp.sum((dn * xh).reshape(SUB // 8, 8, HEAD), axis=0)
        dxh = dn * k_gain
        gk = r * (dxh - xh * jnp.mean(dxh * xh, axis=1, keepdims=True))
        out, at = outs[j // 2]
        at = at + (j % 2) * SUB
        out[at : at + SUB, :] = gk.astype(out.dtype)
        out[at + TOK : at + TOK + SUB, :] = dv[rows, :].astype(out.dtype)

    def all_key_ends():
        yield
        yield
        key_ends(0)
        yield
        yield
        for j in range(1, 5):
            key_ends(j)
            yield

    weave(key_terms(last), all_key_ends(), query_terms(last, 1))
    for j in range(5, parts):
        key_ends(j)
    for copy in copies(last):
        copy.start()
    kg = k_sums[0]
    gains = jnp.concatenate(
        [jnp.sum(qg_acc[...], axis=0, keepdims=True), jnp.sum(kg, axis=0, keepdims=True)]
    )
    gain_ref[...] = gains
    high = gains.astype(jnp.bfloat16).astype(jnp.float32)
    middle = (gains - high).astype(jnp.bfloat16).astype(jnp.float32)
    low = gains - high - middle
    swap_ref[4 * TOK :, :] = jnp.concatenate(
        [high, middle, low, jnp.zeros((ID_ROWS - 6, HEAD), jnp.float32)]
    ).astype(jnp.bfloat16)
    for pair in range(HEADS // 2):
        for copy in copies(pair):
            copy.wait()


def attention(blocks, prepared, frequency):
    vmem = pl.BlockSpec(memory_space=pltpu.VMEM)
    hbm = pl.BlockSpec(memory_space=pl.ANY)
    f32, bf16 = jnp.float32, jnp.bfloat16
    shape = jax.ShapeDtypeStruct
    return pl.pallas_call(
        kernel,
        out_shape=[
            shape((TOK, HEADS * HEAD), bf16),
            shape((TOK, HEADS * HEAD), bf16),
            shape((2 * TOK, HEAD), f32),
            shape((2 * TOK, HEAD), f32),
            shape((2 * TOK, HEAD), f32),
            shape((4 * TOK + ID_ROWS, HEAD), bf16),
            shape((2, HEAD), f32),
        ],
        in_specs=[vmem] * 12,
        out_specs=[hbm] * 2 + [vmem] * 5,
        scratch_shapes=[
            pltpu.VMEM((TOK, HEADS * HEAD), bf16),
            pltpu.VMEM((TOK, HEADS * HEAD), bf16),
            pltpu.VMEM((WINDOW, HEAD), f32),
            pltpu.VMEM((WINDOW, HEAD), f32),
            pltpu.VMEM((WINDOW, 2 * HEAD), bf16),
            pltpu.VMEM((WINDOW, HEAD), bf16),
            pltpu.VMEM((HEAD, WINDOW), bf16),
            pltpu.VMEM((HEAD, WINDOW), bf16),
            pltpu.VMEM((HEADS * TOK, HEAD), bf16),
            pltpu.VMEM((HEADS // 2, 2 * HEAD, 512), bf16),
            pltpu.VMEM((2, 2, SPAN, 256), f32),
            pltpu.VMEM((2, WINDOW, 512), bf16),
            pltpu.VMEM((2, WINDOW, 512), bf16),
            pltpu.VMEM((WINDOW, HEAD), f32),
            pltpu.VMEM((WINDOW, HEAD), f32),
            pltpu.VMEM((8, HEAD), f32),
            pltpu.VMEM((MSG, HEAD), bf16),
            pltpu.VMEM((MSG, HEAD), bf16),
            pltpu.SemaphoreType.DMA((HEADS // 2,)),
            pltpu.SemaphoreType.DMA((HEADS // 2,)),
        ],
        compiler_params=pltpu.CompilerParams(vmem_limit_bytes=40 * 1024 * 1024),
    )(*blocks, *prepared, frequency)


def pack_kernel(keys, values, ids, out):
    out[0:TOK, :] = keys[...]
    out[TOK : 2 * TOK, :] = values[...]
    marked = (ids[...] + 1).astype(jnp.float32)
    out[2 * TOK :, :] = jnp.concatenate(
        [marked, jnp.zeros((ID_ROWS - 2, HEAD), jnp.float32)]
    ).astype(jnp.bfloat16)


def pack(keys, values, ids):
    vmem = pl.BlockSpec(memory_space=pltpu.VMEM)
    return pl.pallas_call(
        pack_kernel,
        out_shape=jax.ShapeDtypeStruct((MSG, HEAD), jnp.bfloat16),
        in_specs=[vmem] * 3,
        out_specs=vmem,
    )(keys, values, ids)


def swapped(block, ways=(0, 1)):
    route = [(i, i ^ 1) for i in range(lax.axis_size("context")) if i % 2 in ways]
    return lax.ppermute(block, "context", route)


def chip_kernel(swap, four, two, own, gains, four_out, two_out, own_out, gains_out):
    even = lax.rem(lax.axis_index("context"), 2) == 0
    one, three = slice(0, 2 * TOK), slice(2 * TOK, 4 * TOK)

    @pl.when(even)
    def _():
        four_out[...] = four[...].astype(jnp.bfloat16)
        two_out[...] = two[...] + swap[three, :].astype(jnp.float32)
        own_out[...] = own[...] + swap[one, :].astype(jnp.float32)

    @pl.when(jnp.logical_not(even))
    def _():
        four_out[...] = (four[...] + swap[three, :].astype(jnp.float32)).astype(jnp.bfloat16)
        two_out[...] = two[...] + swap[one, :].astype(jnp.float32)
        own_out[...] = own[...]

    split = swap[4 * TOK :, :].astype(jnp.float32)
    total = gains[...] + ((split[0:2] + split[2:4]) + split[4:6])
    gains_out[...] = jnp.concatenate([total] * (gains_out.shape[0] // 2))


def hop_kernel(two, hop, two_out):
    two_out[...] = (two[...] + hop[...].astype(jnp.float32)).astype(jnp.bfloat16)


def last_kernel(own, hop, terms, keys, values, q_gain, k_gain):
    total = (own[...] + hop[...].astype(jnp.float32)).astype(jnp.bfloat16)
    keys[...] = total[:TOK]
    values[...] = total[TOK:]
    gains = jnp.sum(terms[...].reshape(-1, 8, HEAD), axis=0)
    q_gain[...] = (gains[0:1] + gains[2:3]) + (gains[4:5] + gains[6:7])
    k_gain[...] = (gains[1:2] + gains[3:4]) + (gains[5:6] + gains[7:8])


def small_call(kernel, out_shape, *operands):
    vmem = pl.BlockSpec(memory_space=pltpu.VMEM)
    return pl.pallas_call(
        kernel,
        out_shape=[jax.ShapeDtypeStruct(shape, dtype) for shape, dtype in out_shape],
        in_specs=[vmem] * len(operands),
        out_specs=[vmem] * len(out_shape),
        compiler_params=pltpu.CompilerParams(vmem_limit_bytes=16 * 1024 * 1024),
    )(*operands)


def body(queries, keys, values, output_gradient, q_gain, k_gain, doc_ids):
    f32, bf16 = jnp.float32, jnp.bfloat16
    message = pack(keys, values, doc_ids.reshape(2, HEAD))
    two = passed_along(message, "context", 2)
    first_swap = swapped(message, (0,))
    four = passed_along(message, "context", 4)
    prepared = prepare(queries, output_gradient, q_gain.reshape(1, HEAD), k_gain.reshape(1, HEAD))
    two, *prepared = lax.optimization_barrier((two, *prepared))
    middle_swap = swapped(two)
    last_swap = swapped(four, (1,))
    blocks = [four, two, message, first_swap, middle_swap, last_swap]
    half = jnp.arange(HEAD // 2, dtype=jnp.float32)
    frequency = THETA ** (-(half * 2.0 / HEAD))
    frequency = jnp.concatenate([frequency, frequency]).reshape(1, HEAD)
    attended, query_gradient, four, two, own, swap, gains = attention(blocks, prepared, frequency)

    axes = ("context", "tensor")
    chips = lax.axis_size(axes) // 2
    block = (2 * TOK, HEAD)
    four, two, own, gains = small_call(
        chip_kernel,
        [(block, bf16), (block, f32), (block, f32), ((2 * chips, HEAD), f32)],
        *(swapped(swap), four, two, own, gains),
    )
    hop = passed_along(four, "context", -2)
    width = lax.axis_size("tensor")
    cores = [
        [(2 * n + core) * width + z for n in range(chips // width) for z in range(width)]
        for core in range(2)
    ]
    gains = lax.all_to_all(gains.reshape(chips, 2, HEAD), axes, 0, 0, axis_index_groups=cores)
    gains = gains.reshape(2 * chips, HEAD)
    (two,) = small_call(hop_kernel, [(block, bf16)], two, hop)
    hop = passed_along(two, "context", -2)
    half_block = (TOK, HEAD)
    key_gradient, value_gradient, q_total, k_total = small_call(
        last_kernel,
        [(half_block, bf16), (half_block, bf16), ((1, HEAD), f32), ((1, HEAD), f32)],
        *(own, hop, gains),
    )
    return (
        attended,
        query_gradient,
        key_gradient,
        value_gradient,
        q_total.reshape(HEAD),
        k_total.reshape(HEAD),
    )


def solution(mesh):
    placed = (
        P("context", "tensor"),
        P("context", "tensor"),
        P("context", "tensor"),
        P("context", "tensor"),
        P(),
        P(),
        P("context"),
    )
    return jax.shard_map(
        body,
        mesh=mesh,
        in_specs=placed,
        out_specs=(
            P("context", "tensor"),
            P("context", "tensor"),
            P("context", "tensor"),
            P("context", "tensor"),
            P(),
            P(),
        ),
        check_vma=False,
    )
```

```python
import jax
import jax.numpy as jnp
import numpy as np
from jax import lax
from jax.experimental import pallas as pl
from jax.experimental.pallas import tpu as pltpu
from jax.sharding import PartitionSpec as P

REACH = 4
THETA = 500000.0
EPSILON = 1e-06
TOK = 256
HEAD = 128
HEADS = 8
WINDOW = (REACH + 1) * TOK
SUB = 128
SPAN = 1152
CHUNKS = SPAN // SUB
FINE = 64
KEY_BLOCKS = (
    [(0, SUB, 0, 256)]
    + [(start, start + 256, 0, 512) for start in range(SUB, SPAN, 256)]
    + [(SPAN, WINDOW, 256, 512)]
)
ID_ROWS = 16
MSG = 2 * TOK + ID_ROWS
SCALING = HEAD ** (-0.5)
EXP2 = float(SCALING * np.log2(np.e))

PI_A = 3.140625
PI_B = float(np.round((np.pi - PI_A) * 2.0**23) / 2.0**23)
PI_C = float(np.pi - PI_A - PI_B)


def passed_along(block, axis, distance):
    devices = range(lax.axis_size(axis))
    route = [(i - distance, i) for i in devices if i - distance in devices]
    return lax.ppermute(block, axis, route)


def dot(a, b):
    return jnp.dot(a, b, preferred_element_type=jnp.float32)


def half_turned(x):
    return pltpu.roll(x, HEAD // 2, 1)


def cos_sin(position, frequency):
    angle = position * frequency
    lane = lax.broadcasted_iota(jnp.int32, (1, HEAD), 1)
    quarter = jnp.where(lane < HEAD // 2, 0.5, 0.0)
    turns = jnp.floor(angle * np.float32(1.0 / np.pi) + (quarter + 0.5))
    count = turns - quarter
    rest = ((angle - count * PI_A) - count * PI_B) - count * PI_C
    square = rest * rest
    series = np.float32(-1.9806614727713168e-4) + square * np.float32(2.6000534489867277e-6)
    series = np.float32(8.333017118275166e-3) + square * series
    series = np.float32(-1.6666656732559204e-1) + square * series
    value = rest + rest * (square * series)
    return jnp.where((turns.astype(jnp.int32) & 1) == 1, -value, value)


def prepare_kernel(q_ref, d_ref, qg_ref, kg_ref, xh_ref, scale_ref, dcat, dcat_t, gains):
    gains[0:1, :] = qg_ref[...]
    gains[1:2, :] = kg_ref[...]
    for sub in range(2):
        tokens = slice(sub * SUB, (sub + 1) * SUB)
        for h in range(HEADS):
            at = (h // 2) * 512 + sub * 256 + (h % 2) * SUB
            rows = slice(at, at + SUB)
            x = q_ref[tokens, h * HEAD : (h + 1) * HEAD].astype(jnp.float32)
            r = lax.rsqrt(jnp.mean(x * x, axis=1, keepdims=True) + EPSILON)
            xh_ref[rows, :] = x * r
            scale_ref[rows, :] = jnp.broadcast_to(r, (SUB, HEAD))
            d = d_ref[tokens, h * HEAD : (h + 1) * HEAD]
            dcat[rows, :] = d
            dcat_t[h // 2, :, at % 512 : at % 512 + SUB] = d.astype(jnp.float32).T.astype(jnp.bfloat16)


def prepare(queries, output_gradient, q_gain, k_gain):
    vmem = pl.BlockSpec(memory_space=pltpu.VMEM)
    f32, bf16 = jnp.float32, jnp.bfloat16
    shape = jax.ShapeDtypeStruct
    return pl.pallas_call(
        prepare_kernel,
        out_shape=[
            shape((HEADS * TOK, HEAD), f32),
            shape((HEADS * TOK, HEAD), f32),
            shape((HEADS * TOK, HEAD), bf16),
            shape((HEADS // 2, HEAD, 512), bf16),
            shape((2, HEAD), f32),
        ],
        in_specs=[vmem] * 4,
        out_specs=[vmem] * 5,
        compiler_params=pltpu.CompilerParams(vmem_limit_bytes=16 * 1024 * 1024),
        cost_estimate=pl.CostEstimate(flops=10**9, bytes_accessed=4 * 2**20, transcendentals=0),
    )(queries, output_gradient, q_gain, k_gain)


def kernel(
    b4, b2, b0, first_swap, middle_swap, last_swap, xh_ref, scale_ref, dcat, dcat_t, gains_ref, f_ref,
    att_hbm, gq_hbm, four_ref, two_ref, own_ref, swap_ref, gain_ref,
    att_ref, gq_ref, cosine, sine, kext, vwin, khat_t, v_t, qhat, qext_t,
    s_ref, w_ref, ds_ref, dk, dv, qg_acc, b3, b1, bounds, att_sem, gq_sem,
):
    even = lax.rem(lax.axis_index("context"), 2) == 0

    @pl.when(even)
    def _():
        b3[...] = last_swap[...]
        b1[...] = middle_swap[...]

    @pl.when(jnp.logical_not(even))
    def _():
        b3[...] = middle_swap[...]
        b1[...] = first_swap[...]

    blocks = (b4, b3, b2, b1, b0)
    lane = lax.broadcasted_iota(jnp.int32, (SUB, HEAD), 1)
    row = lax.broadcasted_iota(jnp.int32, (SUB, HEAD), 0)
    lane_f = lane.astype(jnp.float32)
    row_f = row.astype(jnp.float32)
    left = lane < HEAD // 2
    parts = WINDOW // SUB
    q_gain = gains_ref[0:1, :]
    k_gain = gains_ref[1:2, :]
    frequency = f_ref[...]

    id_rows = []
    for block in blocks:
        both = block[2 * TOK : MSG, :].astype(jnp.float32)
        id_rows += [both[0:1], both[1:2]]
    below = jnp.zeros((SUB, HEAD), jnp.float32)
    for j in range(parts):
        column = jnp.broadcast_to(id_rows[j], (SUB, HEAD)).T
        kext[j * SUB : (j + 1) * SUB, HEAD:] = jnp.where(column == lane_f, 1.0, 0.0).astype(jnp.bfloat16)
        below = below + jnp.where(column < lane_f, 1.0, 0.0)
    first = jnp.sum(below, axis=0, keepdims=True)

    k_norm = [jnp.zeros((SUB, 1), jnp.float32)]

    def key_part(j):
        rows = slice(j * SUB, (j + 1) * SUB)
        here = slice((j % 2) * SUB, (j % 2 + 1) * SUB)
        block = blocks[j // 2]
        member = kext[rows, HEAD:].astype(jnp.float32)
        start = jnp.sum(member * first, axis=1, keepdims=True)
        position = (row + j * SUB).astype(jnp.float32) - start
        both = cos_sin(position, frequency)
        turned = half_turned(both)
        c = jnp.where(left, both, turned)
        s = jnp.where(left, -turned, both)
        cosine[rows, :] = c
        sine[rows, :] = s
        x = block[here, :].astype(jnp.float32)
        normed = x * lax.rsqrt(jnp.mean(x * x, axis=1, keepdims=True) + EPSILON) * k_gain
        hat = normed * c + half_turned(normed) * s
        k_norm[0] = jnp.maximum(k_norm[0], jnp.sum(hat * hat, axis=1, keepdims=True))
        kext[rows, 0:HEAD] = hat.astype(jnp.bfloat16)
        khat_t[:, rows] = hat.T.astype(jnp.bfloat16)
        values = block[TOK + (j % 2) * SUB : TOK + (j % 2 + 1) * SUB, :]
        vwin[rows, :] = values
        v_t[:, rows] = values.astype(jnp.float32).T.astype(jnp.bfloat16)

    def query_part(pair):
        for sub in range(2):
            window_rows = slice(REACH * TOK + sub * SUB, REACH * TOK + (sub + 1) * SUB)
            other = jnp.where(row_f == id_rows[2 * REACH + sub], 0.0, -1e30).astype(jnp.bfloat16)
            for g in range(2):
                at = pair * 512 + sub * 256 + g * SUB
                lanes = slice(at % 512, at % 512 + SUB)
                normed = xh_ref[at : at + SUB, :] * q_gain
                hat = normed * cosine[window_rows, :] + half_turned(normed) * sine[window_rows, :]
                qhat[at : at + SUB, :] = hat.astype(jnp.bfloat16)
                hat_t = hat.T
                bounds[pair, 0:1, lanes] = jnp.sum(hat_t * hat_t, axis=0, keepdims=True)
                qext_t[pair, 0:HEAD, lanes] = hat_t.astype(jnp.bfloat16)
                qext_t[pair, HEAD:, lanes] = other
                yield

    dk[...] = jnp.zeros_like(dk)
    dv[...] = jnp.zeros_like(dv)
    qg_acc[...] = jnp.zeros_like(qg_acc)
    later = jnp.where(row <= lane, 0.0, -1e30)
    later = jnp.concatenate([later, later], axis=1)
    spans = (slice(0, SPAN), slice(SUB, WINDOW))
    columns_of = (slice(0, 256), slice(256, 512))

    def copies(pair):
        columns = slice(pair * 256, (pair + 1) * 256)
        return (
            pltpu.make_async_copy(att_ref.at[:, columns], att_hbm.at[:, columns], att_sem.at[pair]),
            pltpu.make_async_copy(gq_ref.at[:, columns], gq_hbm.at[:, columns], gq_sem.at[pair]),
        )

    shifts, inverses, centers, queries_t = {}, {}, {}, {}

    def scores(pair, sub):
        q = qext_t[pair, :, columns_of[sub]]
        top = jnp.full((8, 256), -1e30, jnp.float32)
        for start in range(0, SPAN, SUB):
            s = dot(kext[sub * SUB + start : sub * SUB + start + SUB, :], q)
            if start + SUB == SPAN:
                s = s + later
            s_ref[pair % 2, sub, start : start + SUB, :] = s
            top = jnp.maximum(top, jnp.max(s.reshape(SUB // 8, 8, 256), axis=0))
            yield
        shifts[pair, sub] = jnp.max(top, axis=0, keepdims=True) * EXP2

    def exponents(pair, sub):
        slot = pair % 2
        shift = shifts[pair, sub]
        total = jnp.zeros((8, 256), jnp.float32)
        for at in range(0, SPAN, FINE):
            rows = slice(at, at + FINE)
            e = jnp.exp2(s_ref[slot, sub, rows, :] * EXP2 - shift)
            s_ref[slot, sub, rows, :] = e
            total = total + jnp.sum(e.reshape(FINE // 8, 8, 256), axis=0)
            yield
        inverses[pair, sub] = 1.0 / jnp.sum(total, axis=0, keepdims=True)

    def bounded_exponents(pair, sub):
        q = qext_t[pair, :, columns_of[sub]]
        shift = bounds[pair, 0:1, columns_of[sub]]
        total = jnp.zeros((8, 256), jnp.float32)
        for start in range(0, SPAN, SUB):
            s = dot(kext[sub * SUB + start : sub * SUB + start + SUB, :], q)
            if start + SUB == SPAN:
                s = s + later
            e = jnp.exp2(s * EXP2 - shift)
            s_ref[pair % 2, sub, start : start + SUB, :] = e
            total = total + jnp.sum(e.reshape(SUB // 8, 8, 256), axis=0)
            yield
        inverses[pair, sub] = 1.0 / jnp.sum(total, axis=0, keepdims=True)

    def weights(pair, sub):
        inverse = inverses[pair, sub]
        for at in range(0, SPAN, FINE):
            w = s_ref[pair % 2, sub, at : at + FINE, :] * inverse
            keys = slice(sub * SUB + at, sub * SUB + at + FINE)
            w_ref[pair % 2, keys, columns_of[sub]] = w.astype(jnp.bfloat16)
            yield

    def attend(pair, sub):
        att_t = dot(v_t[:, spans[sub]], w_ref[pair % 2, spans[sub], columns_of[sub]])
        d_t = dcat_t[pair, :, columns_of[sub]]
        centers[pair, sub] = jnp.sum(att_t * d_t.astype(jnp.float32), axis=0, keepdims=True)
        yield
        tokens = slice(sub * SUB, (sub + 1) * SUB)
        for g in range(2):
            columns = slice(pair * 256 + g * HEAD, pair * 256 + (g + 1) * HEAD)
            att_ref[tokens, columns] = att_t[:, g * SUB : (g + 1) * SUB].T.astype(jnp.bfloat16)
            yield

    def score_terms(pair, sub):
        slot = pair % 2
        d_t = dcat_t[pair, :, columns_of[sub]]
        center = centers[pair, sub]
        for c in range(CHUNKS):
            keys = slice((sub + c) * SUB, (sub + c + 1) * SUB)
            dw = dot(vwin[keys, :], d_t)
            w = w_ref[slot, keys, columns_of[sub]].astype(jnp.float32)
            ds_ref[slot, keys, columns_of[sub]] = (w * (dw - center)).astype(jnp.bfloat16)
            yield

    def query_sums(pair, sub):
        dq_t = dot(khat_t[:, spans[sub]], ds_ref[pair % 2, spans[sub], columns_of[sub]])
        queries_t[pair, sub] = dq_t * SCALING
        yield

    def query_terms(pair, sub):
        dq_t = queries_t[pair, sub]
        tokens = slice(sub * SUB, (sub + 1) * SUB)
        window_rows = slice(REACH * TOK + sub * SUB, REACH * TOK + (sub + 1) * SUB)
        c_q = cosine[window_rows, :]
        s_q = sine[window_rows, :]
        for g in range(2):
            columns = slice(pair * 256 + g * HEAD, pair * 256 + (g + 1) * HEAD)
            at = pair * 512 + sub * 256 + g * SUB
            rows = slice(at, at + SUB)
            dq = dq_t[:, g * SUB : (g + 1) * SUB].T
            xh = xh_ref[rows, :]
            dn = dq * c_q - half_turned(dq) * s_q
            qg_acc[...] += jnp.sum((dn * xh).reshape(SUB // 8, 8, HEAD), axis=0)
            dxh = dn * q_gain
            gq = scale_ref[rows, :] * (dxh - xh * jnp.mean(dxh * xh, axis=1, keepdims=True))
            gq_ref[tokens, columns] = gq.astype(jnp.bfloat16)
            yield

    def key_terms(pair):
        for start, stop, low, high in KEY_BLOCKS:
            keys, lanes = slice(start, stop), slice(low, high)
            rows = slice(pair * 512 + low, pair * 512 + high)
            dk[keys, :] += dot(ds_ref[pair % 2, keys, lanes], qhat[rows, :])
            yield
            dv[keys, :] += dot(w_ref[pair % 2, keys, lanes], dcat[rows, :])
            yield

    def first_of(stream, count):
        for _ in range(count):
            if next(stream, stop) is stop:
                return
            yield

    def weave(*streams):
        streams = [iter(stream) for stream in streams]
        while streams:
            streams = [stream for stream in streams if next(stream, stop) is not stop]

    stop = object()
    chains = [(pair, sub) for pair in range(HEADS // 2) for sub in range(2)]
    for j in range(parts):
        key_part(j)
    for pair in range(HEADS // 2):
        weave(query_part(pair))

    longest = jnp.sqrt(jnp.max(k_norm[0], axis=0, keepdims=True)) * (1.02 * EXP2)
    for pair in range(HEADS // 2):
        bounds[pair, 0:1, :] = jnp.sqrt(bounds[pair, 0:1, :]) * longest
    top = jnp.maximum(
        jnp.maximum(bounds[0, 0:1, :], bounds[1, 0:1, :]), jnp.maximum(bounds[2, 0:1, :], bounds[3, 0:1, :])
    )
    small = jnp.max(top) <= 60.0

    def finish():
        last = HEADS // 2 - 1
        weave(query_sums(last, 1))

        outs = ((four_ref, 0), (swap_ref, 2 * TOK), (two_ref, 0), (swap_ref, 0), (own_ref, 0))
        k_sums = [jnp.zeros((8, HEAD), jnp.float32)]

        def key_ends(j):
            rows = slice(j * SUB, (j + 1) * SUB)
            here = slice((j % 2) * SUB, (j % 2 + 1) * SUB)
            x = blocks[j // 2][here, :].astype(jnp.float32)
            r = lax.rsqrt(jnp.mean(x * x, axis=1, keepdims=True) + EPSILON)
            xh = x * r
            d = dk[rows, :] * SCALING
            dn = d * cosine[rows, :] - half_turned(d) * sine[rows, :]
            k_sums[0] = k_sums[0] + jnp.sum((dn * xh).reshape(SUB // 8, 8, HEAD), axis=0)
            dxh = dn * k_gain
            gk = r * (dxh - xh * jnp.mean(dxh * xh, axis=1, keepdims=True))
            out, at = outs[j // 2]
            at = at + (j % 2) * SUB
            out[at : at + SUB, :] = gk.astype(out.dtype)
            out[at + TOK : at + TOK + SUB, :] = dv[rows, :].astype(out.dtype)

        def all_key_ends():
            yield
            yield
            yield
            key_ends(0)
            yield
            for j in range(1, parts - 1):
                key_ends(j)
                yield

        weave(key_terms(last), all_key_ends(), query_terms(last, 1))
        key_ends(parts - 1)
        for copy in copies(last):
            copy.start()
        kg = k_sums[0]
        gains = jnp.concatenate(
            [jnp.sum(qg_acc[...], axis=0, keepdims=True), jnp.sum(kg, axis=0, keepdims=True)]
        )
        gain_ref[...] = gains
        high = gains.astype(jnp.bfloat16).astype(jnp.float32)
        middle = (gains - high).astype(jnp.bfloat16).astype(jnp.float32)
        low = gains - high - middle
        swap_ref[4 * TOK :, :] = jnp.concatenate(
            [high, middle, low, jnp.zeros((ID_ROWS - 6, HEAD), jnp.float32)]
        ).astype(jnp.bfloat16)

    def run(bounded):
        keys_before = iter(())
        first_step = bounded_exponents if bounded else scores
        weave(first_step(*chains[0]))
        for i, (pair, sub) in enumerate(chains):
            if sub == 0 and pair > 0:
                keys_before = key_terms(pair - 1)
            ahead = [first_step(*chains[i + 1])] if i + 1 < len(chains) else []
            behind = [query_sums(*chains[i - 1])] if i > 0 else []
            if bounded:
                weave(weights(pair, sub), *ahead, *behind, first_of(keys_before, 3))
            else:
                weave(exponents(pair, sub), *ahead)
                weave(weights(pair, sub), *behind, first_of(keys_before, 3))
            behind = [query_terms(*chains[i - 1])] if i > 0 else []
            weave(attend(pair, sub), *behind)
            weave(score_terms(pair, sub), first_of(keys_before, 3))
            if sub == 0 and pair > 0:
                for copy in copies(pair - 1):
                    copy.start()
        finish()

    pl.when(small)(lambda: run(True))
    pl.when(jnp.logical_not(small))(lambda: run(False))
    for pair in range(HEADS // 2):
        for copy in copies(pair):
            copy.wait()


def attention(blocks, prepared, frequency):
    vmem = pl.BlockSpec(memory_space=pltpu.VMEM)
    hbm = pl.BlockSpec(memory_space=pl.ANY)
    f32, bf16 = jnp.float32, jnp.bfloat16
    shape = jax.ShapeDtypeStruct
    return pl.pallas_call(
        kernel,
        out_shape=[
            shape((TOK, HEADS * HEAD), bf16),
            shape((TOK, HEADS * HEAD), bf16),
            shape((2 * TOK, HEAD), f32),
            shape((2 * TOK, HEAD), f32),
            shape((2 * TOK, HEAD), f32),
            shape((4 * TOK + ID_ROWS, HEAD), bf16),
            shape((2, HEAD), f32),
        ],
        in_specs=[vmem] * 12,
        out_specs=[hbm] * 2 + [vmem] * 5,
        scratch_shapes=[
            pltpu.VMEM((TOK, HEADS * HEAD), bf16),
            pltpu.VMEM((TOK, HEADS * HEAD), bf16),
            pltpu.VMEM((WINDOW, HEAD), f32),
            pltpu.VMEM((WINDOW, HEAD), f32),
            pltpu.VMEM((WINDOW, 2 * HEAD), bf16),
            pltpu.VMEM((WINDOW, HEAD), bf16),
            pltpu.VMEM((HEAD, WINDOW), bf16),
            pltpu.VMEM((HEAD, WINDOW), bf16),
            pltpu.VMEM((HEADS * TOK, HEAD), bf16),
            pltpu.VMEM((HEADS // 2, 2 * HEAD, 512), bf16),
            pltpu.VMEM((2, 2, SPAN, 256), f32),
            pltpu.VMEM((2, WINDOW, 512), bf16),
            pltpu.VMEM((2, WINDOW, 512), bf16),
            pltpu.VMEM((WINDOW, HEAD), f32),
            pltpu.VMEM((WINDOW, HEAD), f32),
            pltpu.VMEM((8, HEAD), f32),
            pltpu.VMEM((MSG, HEAD), bf16),
            pltpu.VMEM((MSG, HEAD), bf16),
            pltpu.VMEM((HEADS // 2, 8, 512), f32),
            pltpu.SemaphoreType.DMA((HEADS // 2,)),
            pltpu.SemaphoreType.DMA((HEADS // 2,)),
        ],
        compiler_params=pltpu.CompilerParams(vmem_limit_bytes=40 * 1024 * 1024),
    )(*blocks, *prepared, frequency)


def pack_kernel(keys, values, ids, out):
    out[0:TOK, :] = keys[...]
    out[TOK : 2 * TOK, :] = values[...]
    marked = (ids[...] + 1).astype(jnp.float32)
    out[2 * TOK :, :] = jnp.concatenate(
        [marked, jnp.zeros((ID_ROWS - 2, HEAD), jnp.float32)]
    ).astype(jnp.bfloat16)


def pack(keys, values, ids):
    vmem = pl.BlockSpec(memory_space=pltpu.VMEM)
    return pl.pallas_call(
        pack_kernel,
        out_shape=jax.ShapeDtypeStruct((MSG, HEAD), jnp.bfloat16),
        in_specs=[vmem] * 3,
        out_specs=vmem,
    )(keys, values, ids)


def swapped(block, ways=(0, 1)):
    route = [(i, i ^ 1) for i in range(lax.axis_size("context")) if i % 2 in ways]
    return lax.ppermute(block, "context", route)


def chip_kernel(swap, four, two, own, gains, four_out, two_out, own_out, gains_out):
    even = lax.rem(lax.axis_index("context"), 2) == 0
    one, three = slice(0, 2 * TOK), slice(2 * TOK, 4 * TOK)

    @pl.when(even)
    def _():
        four_out[...] = four[...].astype(jnp.bfloat16)
        two_out[...] = two[...] + swap[three, :].astype(jnp.float32)
        own_out[...] = own[...] + swap[one, :].astype(jnp.float32)

    @pl.when(jnp.logical_not(even))
    def _():
        four_out[...] = (four[...] + swap[three, :].astype(jnp.float32)).astype(jnp.bfloat16)
        two_out[...] = two[...] + swap[one, :].astype(jnp.float32)
        own_out[...] = own[...]

    split = swap[4 * TOK :, :].astype(jnp.float32)
    total = gains[...] + ((split[0:2] + split[2:4]) + split[4:6])
    gains_out[...] = jnp.concatenate([total] * (gains_out.shape[0] // 2))


def hop_kernel(two, hop, two_out):
    two_out[...] = (two[...] + hop[...].astype(jnp.float32)).astype(jnp.bfloat16)


def last_kernel(own, hop, terms, keys, values, q_gain, k_gain):
    total = (own[...] + hop[...].astype(jnp.float32)).astype(jnp.bfloat16)
    keys[...] = total[:TOK]
    values[...] = total[TOK:]
    gains = jnp.sum(terms[...].reshape(-1, 8, HEAD), axis=0)
    q_gain[...] = (gains[0:1] + gains[2:3]) + (gains[4:5] + gains[6:7])
    k_gain[...] = (gains[1:2] + gains[3:4]) + (gains[5:6] + gains[7:8])


def small_call(kernel, out_shape, *operands):
    vmem = pl.BlockSpec(memory_space=pltpu.VMEM)
    return pl.pallas_call(
        kernel,
        out_shape=[jax.ShapeDtypeStruct(shape, dtype) for shape, dtype in out_shape],
        in_specs=[vmem] * len(operands),
        out_specs=[vmem] * len(out_shape),
        compiler_params=pltpu.CompilerParams(vmem_limit_bytes=16 * 1024 * 1024),
    )(*operands)


def body(queries, keys, values, output_gradient, q_gain, k_gain, doc_ids):
    f32, bf16 = jnp.float32, jnp.bfloat16
    message = pack(keys, values, doc_ids.reshape(2, HEAD))
    two = passed_along(message, "context", 2)
    first_swap = swapped(message, (0,))
    four = passed_along(message, "context", 4)
    prepared = prepare(queries, output_gradient, q_gain.reshape(1, HEAD), k_gain.reshape(1, HEAD))
    two, *prepared = lax.optimization_barrier((two, *prepared))
    middle_swap = swapped(two)
    last_swap = swapped(four, (1,))
    blocks = [four, two, message, first_swap, middle_swap, last_swap]
    half = jnp.arange(HEAD // 2, dtype=jnp.float32)
    frequency = THETA ** (-(half * 2.0 / HEAD))
    frequency = jnp.concatenate([frequency, frequency]).reshape(1, HEAD)
    attended, query_gradient, four, two, own, swap, gains = attention(blocks, prepared, frequency)

    axes = ("context", "tensor")
    chips = lax.axis_size(axes) // 2
    block = (2 * TOK, HEAD)
    four, two, own, gains = small_call(
        chip_kernel,
        [(block, bf16), (block, f32), (block, f32), ((2 * chips, HEAD), f32)],
        *(swapped(swap), four, two, own, gains),
    )
    hop = passed_along(four, "context", -2)
    width = lax.axis_size("tensor")
    cores = [
        [(2 * n + core) * width + z for n in range(chips // width) for z in range(width)]
        for core in range(2)
    ]
    gains = lax.all_to_all(gains.reshape(chips, 2, HEAD), axes, 0, 0, axis_index_groups=cores)
    gains = gains.reshape(2 * chips, HEAD)
    (two,) = small_call(hop_kernel, [(block, bf16)], two, hop)
    hop = passed_along(two, "context", -2)
    half_block = (TOK, HEAD)
    key_gradient, value_gradient, q_total, k_total = small_call(
        last_kernel,
        [(half_block, bf16), (half_block, bf16), ((1, HEAD), f32), ((1, HEAD), f32)],
        *(own, hop, gains),
    )
    return (
        attended,
        query_gradient,
        key_gradient,
        value_gradient,
        q_total.reshape(HEAD),
        k_total.reshape(HEAD),
    )


def solution(mesh):
    placed = (
        P("context", "tensor"),
        P("context", "tensor"),
        P("context", "tensor"),
        P("context", "tensor"),
        P(),
        P(),
        P("context"),
    )
    return jax.shard_map(
        body,
        mesh=mesh,
        in_specs=placed,
        out_specs=(
            P("context", "tensor"),
            P("context", "tensor"),
            P("context", "tensor"),
            P("context", "tensor"),
            P(),
            P(),
        ),
        check_vma=False,
    )
```

```python
import jax
import jax.numpy as jnp
import numpy as np
from jax import lax
from jax.experimental import pallas as pl
from jax.experimental.pallas import tpu as pltpu
from jax.sharding import PartitionSpec as P

REACH = 4
THETA = 500000.0
EPSILON = 1e-06
TOK = 256
HEAD = 128
HEADS = 8
WINDOW = (REACH + 1) * TOK
SUB = 128
SPAN = 1152
CHUNKS = SPAN // SUB
FINE = 64
KEY_BLOCKS = (
    [(0, SUB, 0, 256)]
    + [(start, start + 256, 0, 512) for start in range(SUB, SPAN, 256)]
    + [(SPAN, WINDOW, 256, 512)]
)
ID_ROWS = 16
MSG = 2 * TOK + ID_ROWS
SCALING = HEAD ** (-0.5)
EXP2 = float(SCALING * np.log2(np.e))

PI_A = 3.140625
PI_B = float(np.round((np.pi - PI_A) * 2.0**23) / 2.0**23)
PI_C = float(np.pi - PI_A - PI_B)


def passed_along(block, axis, distance):
    devices = range(lax.axis_size(axis))
    route = [(i - distance, i) for i in devices if i - distance in devices]
    return lax.ppermute(block, axis, route)


def dot(a, b):
    return jnp.dot(a, b, preferred_element_type=jnp.float32)


def half_turned(x):
    return pltpu.roll(x, HEAD // 2, 1)


def cos_sin(position, frequency):
    angle = position * frequency
    lane = lax.broadcasted_iota(jnp.int32, (1, HEAD), 1)
    quarter = jnp.where(lane < HEAD // 2, 0.5, 0.0)
    turns = jnp.floor(angle * np.float32(1.0 / np.pi) + (quarter + 0.5))
    count = turns - quarter
    rest = ((angle - count * PI_A) - count * PI_B) - count * PI_C
    square = rest * rest
    series = np.float32(-1.9806614727713168e-4) + square * np.float32(2.6000534489867277e-6)
    series = np.float32(8.333017118275166e-3) + square * series
    series = np.float32(-1.6666656732559204e-1) + square * series
    value = rest + rest * (square * series)
    return jnp.where((turns.astype(jnp.int32) & 1) == 1, -value, value)


def prepare_kernel(q_ref, d_ref, qg_ref, kg_ref, xh_ref, scale_ref, dcat, dcat_t, gains):
    gains[0:1, :] = qg_ref[...]
    gains[1:2, :] = kg_ref[...]
    for sub in range(2):
        tokens = slice(sub * SUB, (sub + 1) * SUB)
        for h in range(HEADS):
            at = (h // 2) * 512 + sub * 256 + (h % 2) * SUB
            rows = slice(at, at + SUB)
            x = q_ref[tokens, h * HEAD : (h + 1) * HEAD].astype(jnp.float32)
            r = lax.rsqrt(jnp.mean(x * x, axis=1, keepdims=True) + EPSILON)
            xh_ref[rows, :] = x * r
            scale_ref[rows, :] = jnp.broadcast_to(r, (SUB, HEAD))
            d = d_ref[tokens, h * HEAD : (h + 1) * HEAD]
            dcat[rows, :] = d
            dcat_t[h // 2, :, at % 512 : at % 512 + SUB] = d.astype(jnp.float32).T.astype(jnp.bfloat16)


def prepare(queries, output_gradient, q_gain, k_gain):
    vmem = pl.BlockSpec(memory_space=pltpu.VMEM)
    f32, bf16 = jnp.float32, jnp.bfloat16
    shape = jax.ShapeDtypeStruct
    return pl.pallas_call(
        prepare_kernel,
        out_shape=[
            shape((HEADS * TOK, HEAD), f32),
            shape((HEADS * TOK, HEAD), f32),
            shape((HEADS * TOK, HEAD), bf16),
            shape((HEADS // 2, HEAD, 512), bf16),
            shape((2, HEAD), f32),
        ],
        in_specs=[vmem] * 4,
        out_specs=[vmem] * 5,
        compiler_params=pltpu.CompilerParams(vmem_limit_bytes=16 * 1024 * 1024),
        cost_estimate=pl.CostEstimate(flops=10**9, bytes_accessed=4 * 2**20, transcendentals=0),
    )(queries, output_gradient, q_gain, k_gain)


def kernel(
    b4, b2, b0, first_swap, middle_swap, last_swap, xh_ref, scale_ref, dcat, dcat_t, gains_ref, f_ref,
    att_hbm, gq_hbm, four_ref, two_ref, own_ref, swap_ref, gain_ref,
    att_ref, gq_ref, cosine, sine, kext, vwin, khat_t, v_t, qhat, qext_t,
    s_ref, w_ref, ds_ref, dk, dv, qg_acc, b3, b1, bias, att_sem, gq_sem,
):
    even = lax.rem(lax.axis_index("context"), 2) == 0

    @pl.when(even)
    def _():
        b3[...] = last_swap[...]
        b1[...] = middle_swap[...]

    @pl.when(jnp.logical_not(even))
    def _():
        b3[...] = middle_swap[...]
        b1[...] = first_swap[...]

    blocks = (b4, b3, b2, b1, b0)
    lane = lax.broadcasted_iota(jnp.int32, (SUB, HEAD), 1)
    row = lax.broadcasted_iota(jnp.int32, (SUB, HEAD), 0)
    lane_f = lane.astype(jnp.float32)
    left = lane < HEAD // 2
    parts = WINDOW // SUB
    q_gain = gains_ref[0:1, :]
    k_gain = gains_ref[1:2, :]
    frequency = f_ref[...]

    id_rows = []
    for block in blocks:
        both = block[2 * TOK : MSG, :].astype(jnp.float32)
        id_rows += [both[0:1], both[1:2]]
    below = jnp.zeros((SUB, HEAD), jnp.float32)
    for j in range(parts):
        column = jnp.broadcast_to(id_rows[j], (SUB, HEAD)).T
        kext[j * SUB : (j + 1) * SUB, HEAD:] = jnp.where(column == lane_f, 1.0, 0.0).astype(jnp.bfloat16)
        below = below + jnp.where(column < lane_f, 1.0, 0.0)
        for sub in range(2):
            if sub <= j < sub + SPAN // SUB:
                kept = column == id_rows[2 * REACH + sub]
                if j == sub + SPAN // SUB - 1:
                    kept = kept & (row <= lane)
                bias[sub, (j - sub) * SUB : (j - sub + 1) * SUB, :] = jnp.where(kept, 0.0, -1e30)
    first = jnp.sum(below, axis=0, keepdims=True)

    def key_part(j):
        rows = slice(j * SUB, (j + 1) * SUB)
        here = slice((j % 2) * SUB, (j % 2 + 1) * SUB)
        block = blocks[j // 2]
        member = kext[rows, HEAD:].astype(jnp.float32)
        start = jnp.sum(member * first, axis=1, keepdims=True)
        position = (row + j * SUB).astype(jnp.float32) - start
        both = cos_sin(position, frequency)
        turned = half_turned(both)
        c = jnp.where(left, both, turned)
        s = jnp.where(left, -turned, both)
        cosine[rows, :] = c
        sine[rows, :] = s
        x = block[here, :].astype(jnp.float32)
        normed = x * lax.rsqrt(jnp.mean(x * x, axis=1, keepdims=True) + EPSILON) * k_gain
        hat = normed * c + half_turned(normed) * s
        kext[rows, 0:HEAD] = hat.astype(jnp.bfloat16)
        khat_t[:, rows] = hat.T.astype(jnp.bfloat16)
        values = block[TOK + (j % 2) * SUB : TOK + (j % 2 + 1) * SUB, :]
        vwin[rows, :] = values
        v_t[:, rows] = values.astype(jnp.float32).T.astype(jnp.bfloat16)

    def query_part(pair):
        for sub in range(2):
            window_rows = slice(REACH * TOK + sub * SUB, REACH * TOK + (sub + 1) * SUB)
            for g in range(2):
                at = pair * 512 + sub * 256 + g * SUB
                lanes = slice(at % 512, at % 512 + SUB)
                normed = xh_ref[at : at + SUB, :] * q_gain
                hat = normed * cosine[window_rows, :] + half_turned(normed) * sine[window_rows, :]
                qhat[at : at + SUB, :] = hat.astype(jnp.bfloat16)
                qext_t[pair, 0:HEAD, lanes] = hat.T.astype(jnp.bfloat16)
                yield

    dk[...] = jnp.zeros_like(dk)
    dv[...] = jnp.zeros_like(dv)
    qg_acc[...] = jnp.zeros_like(qg_acc)
    spans = (slice(0, SPAN), slice(SUB, WINDOW))
    columns_of = (slice(0, 256), slice(256, 512))

    def copies(pair):
        columns = slice(pair * 256, (pair + 1) * 256)
        return (
            pltpu.make_async_copy(att_ref.at[:, columns], att_hbm.at[:, columns], att_sem.at[pair]),
            pltpu.make_async_copy(gq_ref.at[:, columns], gq_hbm.at[:, columns], gq_sem.at[pair]),
        )

    shifts, inverses, centers, queries_t = {}, {}, {}, {}

    def scores(pair, sub):
        q = qext_t[pair, 0:HEAD, columns_of[sub]]
        top = jnp.full((8, 256), -1e30, jnp.float32)
        for start in range(0, SPAN, SUB):
            s = dot(kext[sub * SUB + start : sub * SUB + start + SUB, 0:HEAD], q)
            kept = bias[sub, start : start + SUB, :]
            s = s + jnp.concatenate([kept, kept], axis=1)
            s_ref[pair % 2, sub, start : start + SUB, :] = s
            top = jnp.maximum(top, jnp.max(s.reshape(SUB // 8, 8, 256), axis=0))
            yield
        shifts[pair, sub] = jnp.max(top, axis=0, keepdims=True) * EXP2

    def exponents(pair, sub):
        slot = pair % 2
        shift = shifts[pair, sub]
        total = jnp.zeros((8, 256), jnp.float32)
        for at in range(0, SPAN, FINE):
            rows = slice(at, at + FINE)
            e = jnp.exp2(s_ref[slot, sub, rows, :] * EXP2 - shift)
            s_ref[slot, sub, rows, :] = e
            total = total + jnp.sum(e.reshape(FINE // 8, 8, 256), axis=0)
            yield
        inverses[pair, sub] = 1.0 / jnp.sum(total, axis=0, keepdims=True)

    def weights(pair, sub):
        inverse = inverses[pair, sub]
        for at in range(0, SPAN, FINE):
            w = s_ref[pair % 2, sub, at : at + FINE, :] * inverse
            keys = slice(sub * SUB + at, sub * SUB + at + FINE)
            w_ref[pair % 2, keys, columns_of[sub]] = w.astype(jnp.bfloat16)
            yield

    def attend(pair, sub):
        att_t = dot(v_t[:, spans[sub]], w_ref[pair % 2, spans[sub], columns_of[sub]])
        d_t = dcat_t[pair, :, columns_of[sub]]
        centers[pair, sub] = jnp.sum(att_t * d_t.astype(jnp.float32), axis=0, keepdims=True)
        yield
        tokens = slice(sub * SUB, (sub + 1) * SUB)
        for g in range(2):
            columns = slice(pair * 256 + g * HEAD, pair * 256 + (g + 1) * HEAD)
            att_ref[tokens, columns] = att_t[:, g * SUB : (g + 1) * SUB].T.astype(jnp.bfloat16)
            yield

    def score_terms(pair, sub):
        slot = pair % 2
        d_t = dcat_t[pair, :, columns_of[sub]]
        center = centers[pair, sub]
        for c in range(CHUNKS):
            keys = slice((sub + c) * SUB, (sub + c + 1) * SUB)
            dw = dot(vwin[keys, :], d_t)
            w = w_ref[slot, keys, columns_of[sub]].astype(jnp.float32)
            ds_ref[slot, keys, columns_of[sub]] = (w * (dw - center)).astype(jnp.bfloat16)
            yield

    def query_sums(pair, sub):
        dq_t = dot(khat_t[:, spans[sub]], ds_ref[pair % 2, spans[sub], columns_of[sub]])
        queries_t[pair, sub] = dq_t * SCALING
        yield

    def query_terms(pair, sub):
        dq_t = queries_t[pair, sub]
        tokens = slice(sub * SUB, (sub + 1) * SUB)
        window_rows = slice(REACH * TOK + sub * SUB, REACH * TOK + (sub + 1) * SUB)
        c_q = cosine[window_rows, :]
        s_q = sine[window_rows, :]
        for g in range(2):
            columns = slice(pair * 256 + g * HEAD, pair * 256 + (g + 1) * HEAD)
            at = pair * 512 + sub * 256 + g * SUB
            rows = slice(at, at + SUB)
            dq = dq_t[:, g * SUB : (g + 1) * SUB].T
            xh = xh_ref[rows, :]
            dn = dq * c_q - half_turned(dq) * s_q
            qg_acc[...] += jnp.sum((dn * xh).reshape(SUB // 8, 8, HEAD), axis=0)
            dxh = dn * q_gain
            gq = scale_ref[rows, :] * (dxh - xh * jnp.mean(dxh * xh, axis=1, keepdims=True))
            gq_ref[tokens, columns] = gq.astype(jnp.bfloat16)
            yield

    def key_terms(pair):
        for start, stop, low, high in KEY_BLOCKS:
            keys, lanes = slice(start, stop), slice(low, high)
            rows = slice(pair * 512 + low, pair * 512 + high)
            dk[keys, :] += dot(ds_ref[pair % 2, keys, lanes], qhat[rows, :])
            yield
            dv[keys, :] += dot(w_ref[pair % 2, keys, lanes], dcat[rows, :])
            yield

    def first_of(stream, count):
        for _ in range(count):
            if next(stream, stop) is stop:
                return
            yield

    def weave(*streams):
        streams = [iter(stream) for stream in streams]
        while streams:
            streams = [stream for stream in streams if next(stream, stop) is not stop]

    stop = object()
    chains = [(pair, sub) for pair in range(HEADS // 2) for sub in range(2)]
    keys_before = iter(())

    def first_keys():
        for j in range(parts - 2):
            key_part(j)
            yield

    key_part(parts - 2)
    key_part(parts - 1)
    weave(query_part(0))
    weave(first_keys(), scores(*chains[0]))
    for i, (pair, sub) in enumerate(chains):
        if sub == 0 and pair > 0:
            keys_before = key_terms(pair - 1)
        ahead = [scores(*chains[i + 1])] if i + 1 < len(chains) else []
        weave(exponents(pair, sub), *ahead)
        behind = [query_sums(*chains[i - 1])] if i > 0 else []
        weave(weights(pair, sub), *behind, first_of(keys_before, 3))
        behind = [query_terms(*chains[i - 1])] if i > 0 else []
        if sub == 0 and pair + 1 < HEADS // 2:
            behind.append(query_part(pair + 1))
        weave(attend(pair, sub), *behind)
        weave(score_terms(pair, sub), first_of(keys_before, 3))
        if sub == 0 and pair > 0:
            for copy in copies(pair - 1):
                copy.start()
    last = HEADS // 2 - 1
    weave(query_sums(last, 1))

    outs = ((four_ref, 0), (swap_ref, 2 * TOK), (two_ref, 0), (swap_ref, 0), (own_ref, 0))
    k_sums = [jnp.zeros((8, HEAD), jnp.float32)]

    def key_ends(j):
        rows = slice(j * SUB, (j + 1) * SUB)
        here = slice((j % 2) * SUB, (j % 2 + 1) * SUB)
        x = blocks[j // 2][here, :].astype(jnp.float32)
        r = lax.rsqrt(jnp.mean(x * x, axis=1, keepdims=True) + EPSILON)
        xh = x * r
        d = dk[rows, :] * SCALING
        dn = d * cosine[rows, :] - half_turned(d) * sine[rows, :]
        k_sums[0] = k_sums[0] + jnp.sum((dn * xh).reshape(SUB // 8, 8, HEAD), axis=0)
        dxh = dn * k_gain
        gk = r * (dxh - xh * jnp.mean(dxh * xh, axis=1, keepdims=True))
        out, at = outs[j // 2]
        at = at + (j % 2) * SUB
        out[at : at + SUB, :] = gk.astype(out.dtype)
        out[at + TOK : at + TOK + SUB, :] = dv[rows, :].astype(out.dtype)

    def all_key_ends():
        yield
        yield
        yield
        key_ends(0)
        yield
        for j in range(1, parts - 1):
            key_ends(j)
            yield

    weave(key_terms(last), all_key_ends(), query_terms(last, 1))
    key_ends(parts - 1)
    for copy in copies(last):
        copy.start()
    kg = k_sums[0]
    gains = jnp.concatenate(
        [jnp.sum(qg_acc[...], axis=0, keepdims=True), jnp.sum(kg, axis=0, keepdims=True)]
    )
    gain_ref[...] = gains
    high = gains.astype(jnp.bfloat16).astype(jnp.float32)
    middle = (gains - high).astype(jnp.bfloat16).astype(jnp.float32)
    low = gains - high - middle
    swap_ref[4 * TOK :, :] = jnp.concatenate(
        [high, middle, low, jnp.zeros((ID_ROWS - 6, HEAD), jnp.float32)]
    ).astype(jnp.bfloat16)
    for pair in range(HEADS // 2):
        for copy in copies(pair):
            copy.wait()


def attention(blocks, prepared, frequency):
    vmem = pl.BlockSpec(memory_space=pltpu.VMEM)
    hbm = pl.BlockSpec(memory_space=pl.ANY)
    f32, bf16 = jnp.float32, jnp.bfloat16
    shape = jax.ShapeDtypeStruct
    return pl.pallas_call(
        kernel,
        out_shape=[
            shape((TOK, HEADS * HEAD), bf16),
            shape((TOK, HEADS * HEAD), bf16),
            shape((2 * TOK, HEAD), f32),
            shape((2 * TOK, HEAD), f32),
            shape((2 * TOK, HEAD), f32),
            shape((4 * TOK + ID_ROWS, HEAD), bf16),
            shape((2, HEAD), f32),
        ],
        in_specs=[vmem] * 12,
        out_specs=[hbm] * 2 + [vmem] * 5,
        scratch_shapes=[
            pltpu.VMEM((TOK, HEADS * HEAD), bf16),
            pltpu.VMEM((TOK, HEADS * HEAD), bf16),
            pltpu.VMEM((WINDOW, HEAD), f32),
            pltpu.VMEM((WINDOW, HEAD), f32),
            pltpu.VMEM((WINDOW, 2 * HEAD), bf16),
            pltpu.VMEM((WINDOW, HEAD), bf16),
            pltpu.VMEM((HEAD, WINDOW), bf16),
            pltpu.VMEM((HEAD, WINDOW), bf16),
            pltpu.VMEM((HEADS * TOK, HEAD), bf16),
            pltpu.VMEM((HEADS // 2, HEAD, 512), bf16),
            pltpu.VMEM((2, 2, SPAN, 256), f32),
            pltpu.VMEM((2, WINDOW, 512), bf16),
            pltpu.VMEM((2, WINDOW, 512), bf16),
            pltpu.VMEM((WINDOW, HEAD), f32),
            pltpu.VMEM((WINDOW, HEAD), f32),
            pltpu.VMEM((8, HEAD), f32),
            pltpu.VMEM((MSG, HEAD), bf16),
            pltpu.VMEM((MSG, HEAD), bf16),
            pltpu.VMEM((2, SPAN, SUB), f32),
            pltpu.SemaphoreType.DMA((HEADS // 2,)),
            pltpu.SemaphoreType.DMA((HEADS // 2,)),
        ],
        compiler_params=pltpu.CompilerParams(vmem_limit_bytes=40 * 1024 * 1024),
    )(*blocks, *prepared, frequency)


def pack_kernel(keys, values, ids, out):
    out[0:TOK, :] = keys[...]
    out[TOK : 2 * TOK, :] = values[...]
    marked = (ids[...] + 1).astype(jnp.float32)
    out[2 * TOK :, :] = jnp.concatenate(
        [marked, jnp.zeros((ID_ROWS - 2, HEAD), jnp.float32)]
    ).astype(jnp.bfloat16)


def pack(keys, values, ids):
    vmem = pl.BlockSpec(memory_space=pltpu.VMEM)
    return pl.pallas_call(
        pack_kernel,
        out_shape=jax.ShapeDtypeStruct((MSG, HEAD), jnp.bfloat16),
        in_specs=[vmem] * 3,
        out_specs=vmem,
    )(keys, values, ids)


def swapped(block, ways=(0, 1)):
    route = [(i, i ^ 1) for i in range(lax.axis_size("context")) if i % 2 in ways]
    return lax.ppermute(block, "context", route)


def chip_kernel(swap, four, two, own, gains, four_out, two_out, own_out, gains_out):
    even = lax.rem(lax.axis_index("context"), 2) == 0
    one, three = slice(0, 2 * TOK), slice(2 * TOK, 4 * TOK)

    @pl.when(even)
    def _():
        four_out[...] = four[...].astype(jnp.bfloat16)
        two_out[...] = two[...] + swap[three, :].astype(jnp.float32)
        own_out[...] = own[...] + swap[one, :].astype(jnp.float32)

    @pl.when(jnp.logical_not(even))
    def _():
        four_out[...] = (four[...] + swap[three, :].astype(jnp.float32)).astype(jnp.bfloat16)
        two_out[...] = two[...] + swap[one, :].astype(jnp.float32)
        own_out[...] = own[...]

    split = swap[4 * TOK :, :].astype(jnp.float32)
    total = gains[...] + ((split[0:2] + split[2:4]) + split[4:6])
    gains_out[...] = jnp.concatenate([total] * (gains_out.shape[0] // 2))


def hop_kernel(two, hop, two_out):
    two_out[...] = (two[...] + hop[...].astype(jnp.float32)).astype(jnp.bfloat16)


def last_kernel(own, hop, terms, keys, values, q_gain, k_gain):
    total = (own[...] + hop[...].astype(jnp.float32)).astype(jnp.bfloat16)
    keys[...] = total[:TOK]
    values[...] = total[TOK:]
    gains = jnp.sum(terms[...].reshape(-1, 8, HEAD), axis=0)
    q_gain[...] = (gains[0:1] + gains[2:3]) + (gains[4:5] + gains[6:7])
    k_gain[...] = (gains[1:2] + gains[3:4]) + (gains[5:6] + gains[7:8])


def small_call(kernel, out_shape, *operands):
    vmem = pl.BlockSpec(memory_space=pltpu.VMEM)
    return pl.pallas_call(
        kernel,
        out_shape=[jax.ShapeDtypeStruct(shape, dtype) for shape, dtype in out_shape],
        in_specs=[vmem] * len(operands),
        out_specs=[vmem] * len(out_shape),
        compiler_params=pltpu.CompilerParams(vmem_limit_bytes=16 * 1024 * 1024),
    )(*operands)


def body(queries, keys, values, output_gradient, q_gain, k_gain, doc_ids):
    f32, bf16 = jnp.float32, jnp.bfloat16
    message = pack(keys, values, doc_ids.reshape(2, HEAD))
    two = passed_along(message, "context", 2)
    first_swap = swapped(message, (0,))
    four = passed_along(message, "context", 4)
    prepared = prepare(queries, output_gradient, q_gain.reshape(1, HEAD), k_gain.reshape(1, HEAD))
    two, *prepared = lax.optimization_barrier((two, *prepared))
    middle_swap = swapped(two)
    last_swap = swapped(four, (1,))
    blocks = [four, two, message, first_swap, middle_swap, last_swap]
    half = jnp.arange(HEAD // 2, dtype=jnp.float32)
    frequency = THETA ** (-(half * 2.0 / HEAD))
    frequency = jnp.concatenate([frequency, frequency]).reshape(1, HEAD)
    attended, query_gradient, four, two, own, swap, gains = attention(blocks, prepared, frequency)

    axes = ("context", "tensor")
    chips = lax.axis_size(axes) // 2
    block = (2 * TOK, HEAD)
    four, two, own, gains = small_call(
        chip_kernel,
        [(block, bf16), (block, f32), (block, f32), ((2 * chips, HEAD), f32)],
        *(swapped(swap), four, two, own, gains),
    )
    hop = passed_along(four, "context", -2)
    width = lax.axis_size("tensor")
    cores = [
        [(2 * n + core) * width + z for n in range(chips // width) for z in range(width)]
        for core in range(2)
    ]
    gains = lax.all_to_all(gains.reshape(chips, 2, HEAD), axes, 0, 0, axis_index_groups=cores)
    gains = gains.reshape(2 * chips, HEAD)
    (two,) = small_call(hop_kernel, [(block, bf16)], two, hop)
    hop = passed_along(two, "context", -2)
    half_block = (TOK, HEAD)
    key_gradient, value_gradient, q_total, k_total = small_call(
        last_kernel,
        [(half_block, bf16), (half_block, bf16), ((1, HEAD), f32), ((1, HEAD), f32)],
        *(own, hop, gains),
    )
    return (
        attended,
        query_gradient,
        key_gradient,
        value_gradient,
        q_total.reshape(HEAD),
        k_total.reshape(HEAD),
    )


def solution(mesh):
    placed = (
        P("context", "tensor"),
        P("context", "tensor"),
        P("context", "tensor"),
        P("context", "tensor"),
        P(),
        P(),
        P("context"),
    )
    return jax.shard_map(
        body,
        mesh=mesh,
        in_specs=placed,
        out_specs=(
            P("context", "tensor"),
            P("context", "tensor"),
            P("context", "tensor"),
            P("context", "tensor"),
            P(),
            P(),
        ),
        check_vma=False,
    )
```

```python
import jax
import jax.numpy as jnp
import numpy as np
from jax import lax
from jax.experimental import pallas as pl
from jax.experimental.pallas import tpu as pltpu
from jax.sharding import PartitionSpec as P

REACH = 4
THETA = 500000.0
EPSILON = 1e-06
TOK = 256
HEAD = 128
HEADS = 8
WINDOW = (REACH + 1) * TOK
SUB = 128
SPAN = 1152
CHUNKS = SPAN // SUB
FINE = 64
KEY_BLOCKS = (
    [(0, SUB, 0, 256)]
    + [(start, start + 256, 0, 512) for start in range(SUB, SPAN, 256)]
    + [(SPAN, WINDOW, 256, 512)]
)
ID_ROWS = 16
MSG = 2 * TOK + ID_ROWS
SCALING = HEAD ** (-0.5)
EXP2 = float(SCALING * np.log2(np.e))

PI_A = 3.140625
PI_B = float(np.round((np.pi - PI_A) * 2.0**23) / 2.0**23)
PI_C = float(np.pi - PI_A - PI_B)


def passed_along(block, axis, distance):
    devices = range(lax.axis_size(axis))
    route = [(i - distance, i) for i in devices if i - distance in devices]
    return lax.ppermute(block, axis, route)


def dot(a, b):
    return jnp.dot(a, b, preferred_element_type=jnp.float32)


def half_turned(x):
    return pltpu.roll(x, HEAD // 2, 1)


def cos_sin(position, frequency):
    angle = position * frequency
    lane = lax.broadcasted_iota(jnp.int32, (1, HEAD), 1)
    quarter = jnp.where(lane < HEAD // 2, 0.5, 0.0)
    turns = jnp.floor(angle * np.float32(1.0 / np.pi) + (quarter + 0.5))
    count = turns - quarter
    rest = ((angle - count * PI_A) - count * PI_B) - count * PI_C
    square = rest * rest
    series = np.float32(-1.9806614727713168e-4) + square * np.float32(2.6000534489867277e-6)
    series = np.float32(8.333017118275166e-3) + square * series
    series = np.float32(-1.6666656732559204e-1) + square * series
    value = rest + rest * (square * series)
    return jnp.where((turns.astype(jnp.int32) & 1) == 1, -value, value)


def prepare_kernel(q_ref, d_ref, qg_ref, kg_ref, xh_ref, scale_ref, dcat, dcat_t, gains):
    gains[0:1, :] = qg_ref[...]
    gains[1:2, :] = kg_ref[...]
    for sub in range(2):
        tokens = slice(sub * SUB, (sub + 1) * SUB)
        for h in range(HEADS):
            at = (h // 2) * 512 + sub * 256 + (h % 2) * SUB
            rows = slice(at, at + SUB)
            x = q_ref[tokens, h * HEAD : (h + 1) * HEAD].astype(jnp.float32)
            r = lax.rsqrt(jnp.mean(x * x, axis=1, keepdims=True) + EPSILON)
            xh_ref[rows, :] = x * r
            scale_ref[rows, :] = jnp.broadcast_to(r, (SUB, HEAD))
            d = d_ref[tokens, h * HEAD : (h + 1) * HEAD]
            dcat[rows, :] = d
            dcat_t[h // 2, :, at % 512 : at % 512 + SUB] = d.astype(jnp.float32).T.astype(jnp.bfloat16)


def prepare(queries, output_gradient, q_gain, k_gain):
    vmem = pl.BlockSpec(memory_space=pltpu.VMEM)
    f32, bf16 = jnp.float32, jnp.bfloat16
    shape = jax.ShapeDtypeStruct
    return pl.pallas_call(
        prepare_kernel,
        out_shape=[
            shape((HEADS * TOK, HEAD), f32),
            shape((HEADS * TOK, HEAD), f32),
            shape((HEADS * TOK, HEAD), bf16),
            shape((HEADS // 2, HEAD, 512), bf16),
            shape((2, HEAD), f32),
        ],
        in_specs=[vmem] * 4,
        out_specs=[vmem] * 5,
        compiler_params=pltpu.CompilerParams(vmem_limit_bytes=16 * 1024 * 1024),
        cost_estimate=pl.CostEstimate(flops=10**9, bytes_accessed=4 * 2**20, transcendentals=0),
    )(queries, output_gradient, q_gain, k_gain)


def kernel(
    b4, b2, b0, first_swap, middle_swap, last_swap, xh_ref, scale_ref, dcat, dcat_t, gains_ref, f_ref,
    att_hbm, gq_hbm, four_ref, two_ref, own_ref, swap_ref, near_ref, gain_ref,
    att_ref, gq_ref, cosine, sine, kext, vwin, khat_t, v_t, qhat, qext_t,
    s_ref, w_ref, ds_ref, dk, dv, qg_acc, b3, b1, att_sem, gq_sem,
):
    even = lax.rem(lax.axis_index("context"), 2) == 0

    @pl.when(even)
    def _():
        b3[...] = last_swap[...]
        b1[...] = middle_swap[...]

    @pl.when(jnp.logical_not(even))
    def _():
        b3[...] = middle_swap[...]
        b1[...] = first_swap[...]

    blocks = (b4, b3, b2, b1, b0)
    lane = lax.broadcasted_iota(jnp.int32, (SUB, HEAD), 1)
    row = lax.broadcasted_iota(jnp.int32, (SUB, HEAD), 0)
    lane_f = lane.astype(jnp.float32)
    row_f = row.astype(jnp.float32)
    left = lane < HEAD // 2
    parts = WINDOW // SUB
    q_gain = gains_ref[0:1, :]
    k_gain = gains_ref[1:2, :]
    frequency = f_ref[...]

    id_rows = []
    for block in blocks:
        both = block[2 * TOK : MSG, :].astype(jnp.float32)
        id_rows += [both[0:1], both[1:2]]
    below = jnp.zeros((SUB, HEAD), jnp.float32)
    for j in range(parts):
        column = jnp.broadcast_to(id_rows[j], (SUB, HEAD)).T
        kext[j * SUB : (j + 1) * SUB, HEAD:] = jnp.where(column == lane_f, 1.0, 0.0).astype(jnp.bfloat16)
        below = below + jnp.where(column < lane_f, 1.0, 0.0)
    first = jnp.sum(below, axis=0, keepdims=True)

    def key_part(j):
        rows = slice(j * SUB, (j + 1) * SUB)
        here = slice((j % 2) * SUB, (j % 2 + 1) * SUB)
        block = blocks[j // 2]
        member = kext[rows, HEAD:].astype(jnp.float32)
        start = jnp.sum(member * first, axis=1, keepdims=True)
        position = (row + j * SUB).astype(jnp.float32) - start
        both = cos_sin(position, frequency)
        turned = half_turned(both)
        c = jnp.where(left, both, turned)
        s = jnp.where(left, -turned, both)
        cosine[rows, :] = c
        sine[rows, :] = s
        x = block[here, :].astype(jnp.float32)
        normed = x * lax.rsqrt(jnp.mean(x * x, axis=1, keepdims=True) + EPSILON) * k_gain
        hat = normed * c + half_turned(normed) * s
        kext[rows, 0:HEAD] = hat.astype(jnp.bfloat16)
        khat_t[:, rows] = hat.T.astype(jnp.bfloat16)
        values = block[TOK + (j % 2) * SUB : TOK + (j % 2 + 1) * SUB, :]
        vwin[rows, :] = values
        v_t[:, rows] = values.astype(jnp.float32).T.astype(jnp.bfloat16)

    def query_part(pair):
        for sub in range(2):
            window_rows = slice(REACH * TOK + sub * SUB, REACH * TOK + (sub + 1) * SUB)
            other = jnp.where(row_f == id_rows[2 * REACH + sub], 0.0, -1e30).astype(jnp.bfloat16)
            for g in range(2):
                at = pair * 512 + sub * 256 + g * SUB
                lanes = slice(at % 512, at % 512 + SUB)
                normed = xh_ref[at : at + SUB, :] * q_gain
                hat = normed * cosine[window_rows, :] + half_turned(normed) * sine[window_rows, :]
                qhat[at : at + SUB, :] = hat.astype(jnp.bfloat16)
                qext_t[pair, 0:HEAD, lanes] = hat.T.astype(jnp.bfloat16)
                qext_t[pair, HEAD:, lanes] = other
                yield

    dk[...] = jnp.zeros_like(dk)
    dv[...] = jnp.zeros_like(dv)
    qg_acc[...] = jnp.zeros_like(qg_acc)
    later = jnp.where(row <= lane, 0.0, -1e30)
    later = jnp.concatenate([later, later], axis=1)
    spans = (slice(0, SPAN), slice(SUB, WINDOW))
    columns_of = (slice(0, 256), slice(256, 512))

    def copies(pair):
        columns = slice(pair * 256, (pair + 1) * 256)
        return (
            pltpu.make_async_copy(att_ref.at[:, columns], att_hbm.at[:, columns], att_sem.at[pair]),
            pltpu.make_async_copy(gq_ref.at[:, columns], gq_hbm.at[:, columns], gq_sem.at[pair]),
        )

    shifts, inverses, centers, queries_t = {}, {}, {}, {}

    def scores(pair, sub):
        q = qext_t[pair, :, columns_of[sub]]
        top = jnp.full((8, 256), -1e30, jnp.float32)
        for start in range(0, SPAN, SUB):
            s = dot(kext[sub * SUB + start : sub * SUB + start + SUB, :], q)
            if start + SUB == SPAN:
                s = s + later
            s_ref[pair % 2, sub, start : start + SUB, :] = s
            top = jnp.maximum(top, jnp.max(s.reshape(SUB // 8, 8, 256), axis=0))
            yield
        shifts[pair, sub] = jnp.max(top, axis=0, keepdims=True) * EXP2

    def exponents(pair, sub):
        slot = pair % 2
        shift = shifts[pair, sub]
        total = jnp.zeros((8, 256), jnp.float32)
        for at in range(0, SPAN, FINE):
            rows = slice(at, at + FINE)
            e = jnp.exp2(s_ref[slot, sub, rows, :] * EXP2 - shift)
            s_ref[slot, sub, rows, :] = e
            total = total + jnp.sum(e.reshape(FINE // 8, 8, 256), axis=0)
            yield
        inverses[pair, sub] = 1.0 / jnp.sum(total, axis=0, keepdims=True)

    def weights(pair, sub):
        inverse = inverses[pair, sub]
        for at in range(0, SPAN, FINE):
            w = s_ref[pair % 2, sub, at : at + FINE, :] * inverse
            keys = slice(sub * SUB + at, sub * SUB + at + FINE)
            w_ref[pair % 2, keys, columns_of[sub]] = w.astype(jnp.bfloat16)
            yield

    def attend(pair, sub):
        att_t = dot(v_t[:, spans[sub]], w_ref[pair % 2, spans[sub], columns_of[sub]])
        d_t = dcat_t[pair, :, columns_of[sub]]
        centers[pair, sub] = jnp.sum(att_t * d_t.astype(jnp.float32), axis=0, keepdims=True)
        yield
        tokens = slice(sub * SUB, (sub + 1) * SUB)
        for g in range(2):
            columns = slice(pair * 256 + g * HEAD, pair * 256 + (g + 1) * HEAD)
            att_ref[tokens, columns] = att_t[:, g * SUB : (g + 1) * SUB].T.astype(jnp.bfloat16)
            yield

    def score_terms(pair, sub):
        slot = pair % 2
        d_t = dcat_t[pair, :, columns_of[sub]]
        center = centers[pair, sub]
        for c in range(CHUNKS):
            keys = slice((sub + c) * SUB, (sub + c + 1) * SUB)
            dw = dot(vwin[keys, :], d_t)
            w = w_ref[slot, keys, columns_of[sub]].astype(jnp.float32)
            ds_ref[slot, keys, columns_of[sub]] = (w * (dw - center)).astype(jnp.bfloat16)
            yield

    def query_sums(pair, sub):
        dq_t = dot(khat_t[:, spans[sub]], ds_ref[pair % 2, spans[sub], columns_of[sub]])
        queries_t[pair, sub] = dq_t * SCALING
        yield

    def query_terms(pair, sub):
        dq_t = queries_t[pair, sub]
        tokens = slice(sub * SUB, (sub + 1) * SUB)
        window_rows = slice(REACH * TOK + sub * SUB, REACH * TOK + (sub + 1) * SUB)
        c_q = cosine[window_rows, :]
        s_q = sine[window_rows, :]
        for g in range(2):
            columns = slice(pair * 256 + g * HEAD, pair * 256 + (g + 1) * HEAD)
            at = pair * 512 + sub * 256 + g * SUB
            rows = slice(at, at + SUB)
            dq = dq_t[:, g * SUB : (g + 1) * SUB].T
            xh = xh_ref[rows, :]
            dn = dq * c_q - half_turned(dq) * s_q
            qg_acc[...] += jnp.sum((dn * xh).reshape(SUB // 8, 8, HEAD), axis=0)
            dxh = dn * q_gain
            gq = scale_ref[rows, :] * (dxh - xh * jnp.mean(dxh * xh, axis=1, keepdims=True))
            gq_ref[tokens, columns] = gq.astype(jnp.bfloat16)
            yield

    def key_terms(pair):
        for start, stop, low, high in KEY_BLOCKS:
            keys, lanes = slice(start, stop), slice(low, high)
            rows = slice(pair * 512 + low, pair * 512 + high)
            dk[keys, :] += dot(ds_ref[pair % 2, keys, lanes], qhat[rows, :])
            yield
            dv[keys, :] += dot(w_ref[pair % 2, keys, lanes], dcat[rows, :])
            yield

    def first_of(stream, count):
        for _ in range(count):
            if next(stream, stop) is stop:
                return
            yield

    def weave(*streams):
        streams = [iter(stream) for stream in streams]
        while streams:
            streams = [stream for stream in streams if next(stream, stop) is not stop]

    stop = object()
    chains = [(pair, sub) for pair in range(HEADS // 2) for sub in range(2)]
    keys_before = iter(())

    def first_keys():
        for j in range(parts - 2):
            key_part(j)
            yield

    key_part(parts - 2)
    key_part(parts - 1)
    weave(query_part(0))
    weave(first_keys(), scores(*chains[0]))
    for i, (pair, sub) in enumerate(chains):
        if sub == 0 and pair > 0:
            keys_before = key_terms(pair - 1)
        ahead = [scores(*chains[i + 1])] if i + 1 < len(chains) else []
        weave(exponents(pair, sub), *ahead)
        behind = [query_sums(*chains[i - 1])] if i > 0 else []
        weave(weights(pair, sub), *behind, first_of(keys_before, 3))
        behind = [query_terms(*chains[i - 1])] if i > 0 else []
        if sub == 0 and pair + 1 < HEADS // 2:
            behind.append(query_part(pair + 1))
        weave(attend(pair, sub), *behind)
        weave(score_terms(pair, sub), first_of(keys_before, 3))
        if sub == 0 and pair > 0:
            for copy in copies(pair - 1):
                copy.start()
    last = HEADS // 2 - 1
    weave(query_sums(last, 1))

    outs = ((four_ref, 0), (swap_ref, 0), (two_ref, 0), (near_ref, 0), (own_ref, 0))
    k_sums = [jnp.zeros((8, HEAD), jnp.float32)]

    def key_ends(j):
        rows = slice(j * SUB, (j + 1) * SUB)
        here = slice((j % 2) * SUB, (j % 2 + 1) * SUB)
        x = blocks[j // 2][here, :].astype(jnp.float32)
        r = lax.rsqrt(jnp.mean(x * x, axis=1, keepdims=True) + EPSILON)
        xh = x * r
        d = dk[rows, :] * SCALING
        dn = d * cosine[rows, :] - half_turned(d) * sine[rows, :]
        k_sums[0] = k_sums[0] + jnp.sum((dn * xh).reshape(SUB // 8, 8, HEAD), axis=0)
        dxh = dn * k_gain
        gk = r * (dxh - xh * jnp.mean(dxh * xh, axis=1, keepdims=True))
        out, at = outs[j // 2]
        at = at + (j % 2) * SUB
        out[at : at + SUB, :] = gk.astype(out.dtype)
        out[at + TOK : at + TOK + SUB, :] = dv[rows, :].astype(out.dtype)

    def all_key_ends():
        yield
        yield
        yield
        key_ends(0)
        yield
        for j in range(1, parts - 1):
            key_ends(j)
            yield

    weave(key_terms(last), all_key_ends(), query_terms(last, 1))
    key_ends(parts - 1)
    for copy in copies(last):
        copy.start()
    kg = k_sums[0]
    gains = jnp.concatenate(
        [jnp.sum(qg_acc[...], axis=0, keepdims=True), jnp.sum(kg, axis=0, keepdims=True)]
    )
    gain_ref[...] = gains
    high = gains.astype(jnp.bfloat16).astype(jnp.float32)
    middle = (gains - high).astype(jnp.bfloat16).astype(jnp.float32)
    low = gains - high - middle
    swap_ref[2 * TOK :, :] = jnp.concatenate(
        [high, middle, low, jnp.zeros((ID_ROWS - 6, HEAD), jnp.float32)]
    ).astype(jnp.bfloat16)
    for pair in range(HEADS // 2):
        for copy in copies(pair):
            copy.wait()


def attention(blocks, prepared, frequency):
    vmem = pl.BlockSpec(memory_space=pltpu.VMEM)
    hbm = pl.BlockSpec(memory_space=pl.ANY)
    f32, bf16 = jnp.float32, jnp.bfloat16
    shape = jax.ShapeDtypeStruct
    return pl.pallas_call(
        kernel,
        out_shape=[
            shape((TOK, HEADS * HEAD), bf16),
            shape((TOK, HEADS * HEAD), bf16),
            shape((2 * TOK, HEAD), f32),
            shape((2 * TOK, HEAD), f32),
            shape((2 * TOK, HEAD), f32),
            shape((2 * TOK + ID_ROWS, HEAD), bf16),
            shape((2 * TOK, HEAD), bf16),
            shape((2, HEAD), f32),
        ],
        in_specs=[vmem] * 12,
        out_specs=[hbm] * 2 + [vmem] * 6,
        scratch_shapes=[
            pltpu.VMEM((TOK, HEADS * HEAD), bf16),
            pltpu.VMEM((TOK, HEADS * HEAD), bf16),
            pltpu.VMEM((WINDOW, HEAD), f32),
            pltpu.VMEM((WINDOW, HEAD), f32),
            pltpu.VMEM((WINDOW, 2 * HEAD), bf16),
            pltpu.VMEM((WINDOW, HEAD), bf16),
            pltpu.VMEM((HEAD, WINDOW), bf16),
            pltpu.VMEM((HEAD, WINDOW), bf16),
            pltpu.VMEM((HEADS * TOK, HEAD), bf16),
            pltpu.VMEM((HEADS // 2, 2 * HEAD, 512), bf16),
            pltpu.VMEM((2, 2, SPAN, 256), f32),
            pltpu.VMEM((2, WINDOW, 512), bf16),
            pltpu.VMEM((2, WINDOW, 512), bf16),
            pltpu.VMEM((WINDOW, HEAD), f32),
            pltpu.VMEM((WINDOW, HEAD), f32),
            pltpu.VMEM((8, HEAD), f32),
            pltpu.VMEM((MSG, HEAD), bf16),
            pltpu.VMEM((MSG, HEAD), bf16),
            pltpu.SemaphoreType.DMA((HEADS // 2,)),
            pltpu.SemaphoreType.DMA((HEADS // 2,)),
        ],
        compiler_params=pltpu.CompilerParams(vmem_limit_bytes=40 * 1024 * 1024),
    )(*blocks, *prepared, frequency)


def pack_kernel(keys, values, ids, out):
    out[0:TOK, :] = keys[...]
    out[TOK : 2 * TOK, :] = values[...]
    marked = (ids[...] + 1).astype(jnp.float32)
    out[2 * TOK :, :] = jnp.concatenate(
        [marked, jnp.zeros((ID_ROWS - 2, HEAD), jnp.float32)]
    ).astype(jnp.bfloat16)


def pack(keys, values, ids):
    vmem = pl.BlockSpec(memory_space=pltpu.VMEM)
    return pl.pallas_call(
        pack_kernel,
        out_shape=jax.ShapeDtypeStruct((MSG, HEAD), jnp.bfloat16),
        in_specs=[vmem] * 3,
        out_specs=vmem,
    )(keys, values, ids)


def swapped(block, ways=(0, 1)):
    route = [(i, i ^ 1) for i in range(lax.axis_size("context")) if i % 2 in ways]
    return lax.ppermute(block, "context", route)


def on_even():
    return lax.rem(lax.axis_index("context"), 2) == 0


def chip_kernel(swap, four, gains, four_out, gains_out):
    far = jnp.where(on_even(), 0.0, swap[0 : 2 * TOK, :].astype(jnp.float32))
    four_out[...] = (four[...] + far).astype(jnp.bfloat16)
    split = swap[2 * TOK :, :].astype(jnp.float32)
    total = gains[...] + ((split[0:2] + split[2:4]) + split[4:6])
    gains_out[...] = jnp.concatenate([total] * (gains_out.shape[0] // 2))


def hop_kernel(two, hop, swap, near, two_out):
    other = jnp.where(on_even(), swap[0 : 2 * TOK, :].astype(jnp.float32), near[...].astype(jnp.float32))
    two_out[...] = ((two[...] + other) + hop[...].astype(jnp.float32)).astype(jnp.bfloat16)


def last_kernel(own, hop, near, terms, keys, values, q_gain, k_gain):
    other = jnp.where(on_even(), near[...].astype(jnp.float32), 0.0)
    total = ((own[...] + other) + hop[...].astype(jnp.float32)).astype(jnp.bfloat16)
    keys[...] = total[:TOK]
    values[...] = total[TOK:]
    gains = jnp.sum(terms[...].reshape(-1, 8, HEAD), axis=0)
    q_gain[...] = (gains[0:1] + gains[2:3]) + (gains[4:5] + gains[6:7])
    k_gain[...] = (gains[1:2] + gains[3:4]) + (gains[5:6] + gains[7:8])


def small_call(kernel, out_shape, *operands):
    vmem = pl.BlockSpec(memory_space=pltpu.VMEM)
    return pl.pallas_call(
        kernel,
        out_shape=[jax.ShapeDtypeStruct(shape, dtype) for shape, dtype in out_shape],
        in_specs=[vmem] * len(operands),
        out_specs=[vmem] * len(out_shape),
        compiler_params=pltpu.CompilerParams(vmem_limit_bytes=16 * 1024 * 1024),
    )(*operands)


def body(queries, keys, values, output_gradient, q_gain, k_gain, doc_ids):
    f32, bf16 = jnp.float32, jnp.bfloat16
    message = pack(keys, values, doc_ids.reshape(2, HEAD))
    two = passed_along(message, "context", 2)
    first_swap = swapped(message, (0,))
    four = passed_along(message, "context", 4)
    prepared = prepare(queries, output_gradient, q_gain.reshape(1, HEAD), k_gain.reshape(1, HEAD))
    two, *prepared = lax.optimization_barrier((two, *prepared))
    middle_swap = swapped(two)
    last_swap = swapped(four, (1,))
    blocks = [four, two, message, first_swap, middle_swap, last_swap]
    half = jnp.arange(HEAD // 2, dtype=jnp.float32)
    frequency = THETA ** (-(half * 2.0 / HEAD))
    frequency = jnp.concatenate([frequency, frequency]).reshape(1, HEAD)
    attended, query_gradient, four, two, own, swap, near, gains = attention(blocks, prepared, frequency)

    axes = ("context", "tensor")
    chips = lax.axis_size(axes) // 2
    block = (2 * TOK, HEAD)
    swap = swapped(swap)
    four, gains = small_call(
        chip_kernel, [(block, bf16), ((2 * chips, HEAD), f32)], swap, four, gains
    )
    near = swapped(near)
    hop = passed_along(four, "context", -2)
    width = lax.axis_size("tensor")
    cores = [
        [(2 * n + core) * width + z for n in range(chips // width) for z in range(width)]
        for core in range(2)
    ]
    gains = lax.all_to_all(gains.reshape(chips, 2, HEAD), axes, 0, 0, axis_index_groups=cores)
    gains = gains.reshape(2 * chips, HEAD)
    (two,) = small_call(hop_kernel, [(block, bf16)], two, hop, swap, near)
    hop = passed_along(two, "context", -2)
    half_block = (TOK, HEAD)
    key_gradient, value_gradient, q_total, k_total = small_call(
        last_kernel,
        [(half_block, bf16), (half_block, bf16), ((1, HEAD), f32), ((1, HEAD), f32)],
        *(own, hop, near, gains),
    )
    return (
        attended,
        query_gradient,
        key_gradient,
        value_gradient,
        q_total.reshape(HEAD),
        k_total.reshape(HEAD),
    )


def solution(mesh):
    placed = (
        P("context", "tensor"),
        P("context", "tensor"),
        P("context", "tensor"),
        P("context", "tensor"),
        P(),
        P(),
        P("context"),
    )
    return jax.shard_map(
        body,
        mesh=mesh,
        in_specs=placed,
        out_specs=(
            P("context", "tensor"),
            P("context", "tensor"),
            P("context", "tensor"),
            P("context", "tensor"),
            P(),
            P(),
        ),
        check_vma=False,
    )
```
